32 devices in a mesh: dp: 16 (over z, y, core), mp: 2 (over x).
Axes of the slice: x: 2, y: 2, z: 4, core: 2. Of those that a mesh axis runs over, the one named last changes fastest.
Arguments:
- tokens: bfloat16 [16384, 768], P('dp'), may hold values from -6 to 6
- lengths: int32 [32], P('dp'), may hold values from 64 to 512, as said below
- weights: float32 [768, 13, 768], P('dp', None, 'mp')
- weight_m1: float32 [768, 13, 768], P('dp', None, 'mp')
- weight_m2: float32 [768, 13, 768], P('dp', None, 'mp')
- head_vecs: float32 [6, 768], P(None, 'mp')
- head_m1: float32 [6, 768], P(None, 'mp')
- head_m2: float32 [6, 768], P(None, 'mp')
- norm_vecs: float32 [6, 768], replicated
- norm_m1: float32 [6, 768], replicated
- norm_m2: float32 [6, 768], replicated
- cotangent: bfloat16 [16384, 768], P(('dp', 'mp')), may hold values from -6 to 6
Outputs:
- out_tokens: bfloat16 [16384, 768], P(('dp', 'mp'))
- grad_tokens: float32 [16384, 768], P(('dp', 'mp'))
- new_weights: float32 [768, 13, 768], P('dp', None, 'mp')
- new_weight_m1: float32 [768, 13, 768], P('dp', None, 'mp')
- new_weight_m2: float32 [768, 13, 768], P('dp', None, 'mp')
- new_head_vecs: float32 [6, 768], P(None, 'mp')
- new_head_m1: float32 [6, 768], P(None, 'mp')
- new_head_m2: float32 [6, 768], P(None, 'mp')
- new_norm_vecs: float32 [6, 768], replicated
- new_norm_m1: float32 [6, 768], replicated
- new_norm_m2: float32 [6, 768], replicated
The draws below stay inside these ranges and needn't reach their ends.
Inputs may be any that keep to these rules, and one draw needn't show every extreme that they name: `lengths`: some sequence has 512 tokens in use in every draw.
All inputs are finite; a program needn't handle non-finite values.
Results may differ from the reference program's by a relative error of at most 0.015.
The reference program's roundings to bfloat16 on the way count: a program that leaves them out, or rounds other values in their place, can miss the bound.
Values may be sent and summed in bfloat16 or wider, within the bound.
No kernel may reach another device: no remote copies, remote signals or barrier semaphores. Data moves between devices by JAX's collectives and lax.ppermute only.
A program may use at most 192 MiB of HBM per device.

```python
import math
import jax
import jax.numpy as jnp
from jax import lax

D = 768
HEAD_TOTAL = 12
HEAD_FEATURES = 64
FF = 3072
L = 512
STEP = 5
HD = 768
SEQS = 32
TOKENS = 16384


def weight_scales():
    return jnp.array([1.3 * D ** (-0.5), 1.3 * D ** (-0.5), D ** (-0.5), 1.3 * D ** (-0.5), 4.0 * (HEAD_TOTAL * HEAD_FEATURES) ** (-0.5)] + [D ** (-0.5)] * 4 + [1.6 * FF ** (-0.5)] * 4, jnp.float32)


def weight_grad_sizes():
    return jnp.array([0.3, 0.3, 0.5, 0.5, 0.15] + [0.35] * 4 + [0.45] * 4, jnp.float32) * TOKENS ** 0.5


def head_grad_sizes():
    return jnp.array([0.3, 0.3, 0.35, 0.35, 0.35, 0.35], jnp.float32) * TOKENS ** 0.5


def norm_grad_sizes():
    return jnp.array([1.0, 1.0, 1.0, 1.0, 0.8, 0.7], jnp.float32) * TOKENS ** 0.5


def square_factor(key, shape):
    return jnp.exp(jax.random.uniform(key, shape, jnp.float32, math.log(0.5), math.log(8.0)))


def draw_lengths(key, part):
    key = jax.random.fold_in(key, 20)
    key_base, key_power, key_pick = jax.random.split(key, 3)
    base_len = jax.random.randint(key_base, (SEQS,), L // 8, L // 4 + 1)
    power = jax.random.randint(key_power, (SEQS,), 0, 4)
    stretched = jnp.minimum(jnp.left_shift(base_len, power), L)
    picked = jax.random.randint(key_pick, (), 0, SEQS)
    return jnp.where(jnp.arange(SEQS) == picked, L, stretched).astype(jnp.int32)


def draw_weights(key, part):
    key = jax.random.fold_in(key, 11)
    shape = (D, 13, HEAD_TOTAL * HEAD_FEATURES)
    base = jnp.clip(jax.random.normal(key, shape, jnp.float32), -4.0, 4.0)
    return base * weight_scales()[None, :, None]


def draw_weight_m1(key, part):
    key = jax.random.fold_in(key, 12)
    shape = (D, 13, HEAD_TOTAL * HEAD_FEATURES)
    base = jnp.clip(jax.random.normal(key, shape, jnp.float32), -4.0, 4.0)
    return base * weight_grad_sizes()[None, :, None]


def draw_weight_m2(key, part):
    key = jax.random.fold_in(key, 13)
    sizes = weight_grad_sizes()
    return square_factor(key, (D, 13, HEAD_TOTAL * HEAD_FEATURES)) * (sizes * sizes)[None, :, None]


def draw_head_vecs(key, part):
    key = jax.random.fold_in(key, 14)
    shape = (6, HEAD_TOTAL * HEAD_FEATURES)
    base = jnp.clip(jax.random.normal(key, shape, jnp.float32), -4.0, 4.0)
    return base * jnp.array([0.5, 0.5, 0.3, 0.3, 0.3, 0.3], jnp.float32)[:, None]


def draw_head_m1(key, part):
    key = jax.random.fold_in(key, 15)
    shape = (6, HEAD_TOTAL * HEAD_FEATURES)
    base = jnp.clip(jax.random.normal(key, shape, jnp.float32), -4.0, 4.0)
    return base * head_grad_sizes()[:, None]


def draw_head_m2(key, part):
    key = jax.random.fold_in(key, 16)
    sizes = head_grad_sizes()
    return square_factor(key, (6, HEAD_TOTAL * HEAD_FEATURES)) * (sizes * sizes)[:, None]


def draw_norm_vecs(key, part):
    key = jax.random.fold_in(key, 17)
    key_gain, key_bias = jax.random.split(key)
    gains = jax.random.uniform(key_gain, (6, D), jnp.float32, 0.6, 1.4)
    biases = 0.3 * jnp.clip(jax.random.normal(key_bias, (6, D), jnp.float32), -4.0, 4.0)
    gain_rows = jnp.array([1.0, 0.0, 1.0, 0.0, 0.0, 0.0], jnp.float32)[:, None]
    return gain_rows * gains + (1.0 - gain_rows) * biases


def draw_norm_m1(key, part):
    key = jax.random.fold_in(key, 18)
    shape = (6, D)
    base = jnp.clip(jax.random.normal(key, shape, jnp.float32), -4.0, 4.0)
    return base * norm_grad_sizes()[:, None]


def draw_norm_m2(key, part):
    key = jax.random.fold_in(key, 19)
    sizes = norm_grad_sizes()
    return square_factor(key, (6, D)) * (sizes * sizes)[:, None]


def block_levels(rng, shape, shards, smallest, largest):
    def one(position, parts):
        draws = jax.random.uniform(jax.random.fold_in(jax.random.fold_in(rng, 6), position), (parts,), jnp.float32, smallest / len(shards), largest / len(shards))
        return jnp.repeat(jnp.exp(draws), shape[position] // parts).reshape((-1,) + (1,) * (len(shape) - position - 1))

    level = one(*shards[0])
    for cut in shards[1:]:
        level = level * one(*cut)
    return level


def scatter_about(key, shape, width, limit, shards=(), dtype=jnp.bfloat16):
    entries = jax.random.normal(key, shape, jnp.float32) * width
    if len(shards) > 0:
        entries = block_levels(key, shape, shards, -0.22, 0.18) * entries
    return jnp.clip(entries, min=-limit, max=limit).astype(dtype)


def setup_inputs(seed: int = 0) -> dict:
    key_of = jax.random.split(jax.random.key(seed), 13)
    return {
        "tokens": scatter_about(key_of[0], (TOKENS, D), 1.0, 6.0, ((0, 16),)),
        "lengths": draw_lengths(jax.random.fold_in(key_of[12], 71), 0),
        "weights": draw_weights(jax.random.fold_in(key_of[12], 71), 0),
        "weight_m1": draw_weight_m1(jax.random.fold_in(key_of[12], 71), 0),
        "weight_m2": draw_weight_m2(jax.random.fold_in(key_of[12], 71), 0),
        "head_vecs": draw_head_vecs(jax.random.fold_in(key_of[12], 71), 0),
        "head_m1": draw_head_m1(jax.random.fold_in(key_of[12], 71), 0),
        "head_m2": draw_head_m2(jax.random.fold_in(key_of[12], 71), 0),
        "norm_vecs": draw_norm_vecs(jax.random.fold_in(key_of[12], 71), 0),
        "norm_m1": draw_norm_m1(jax.random.fold_in(key_of[12], 71), 0),
        "norm_m2": draw_norm_m2(jax.random.fold_in(key_of[12], 71), 0),
        "cotangent": scatter_about(key_of[11], (TOKENS, D), 1.0, 6.0, ((0, 32),)),
    }


EPS_NORM = 1e-05
EPS_ADAM = 1e-08
BETA_ONE = 0.5
BETA_TWO = 0.5
RATE_BIG = 0.03
RATE_SMALL = 0.2
DECAY = 0.01
MASKED = -1e+30
FULL_PRECISION = lax.Precision.HIGHEST

@jax.custom_vjp
def low(v):
    return lax.optimization_barrier(v.astype(jnp.bfloat16)).astype(jnp.float32)

@jax.custom_vjp
def low_back(v):
    return v

def low_keep(v):
    return (low(v), None)

def low_pass(kept, grad):
    return (grad,)

def back_keep(v):
    return (v, None)

def back_low(kept, grad):
    return (low(grad),)
low.defvjp(low_keep, low_pass)
low_back.defvjp(back_keep, back_low)

def relative_embedding(length, model_width):
    distance = (length - 1 - jnp.arange(2 * length - 1)).astype(jnp.float32)
    freq_index = jnp.arange(model_width // 2).astype(jnp.float32)
    inverse = 1.0 / 10000.0 ** (2.0 * freq_index / model_width)
    angles = distance[:, None] * inverse[None, :]
    return jnp.concatenate([jnp.sin(angles), jnp.cos(angles)], axis=1)

def shifted_scores(matrix):
    leading = matrix.shape[:-2]
    row_count = matrix.shape[-2]
    col_count = matrix.shape[-1]
    flattened = matrix.reshape(leading + (row_count * col_count,))
    flattened = lax.slice_in_dim(flattened, row_count - 1, row_count - 1 + row_count * (col_count - 1), axis=flattened.ndim - 1)
    return flattened.reshape(leading + (row_count, col_count - 1))[..., :row_count]

def layer_norm(features, scale_row, shift_row):
    row_mean = lax.optimization_barrier(jnp.mean(features, axis=-1, keepdims=True))
    centred = features - row_mean
    spread = lax.optimization_barrier(jnp.mean(centred * centred, axis=-1, keepdims=True))
    return centred * lax.rsqrt(spread + EPS_NORM) * scale_row + shift_row

def gelu(features):
    return 0.5 * features * (1.0 + jax.scipy.special.erf(features * 0.7071067811865476))

def adam_update(param, grad_sum, moment_one, moment_two, rate):
    new_one = BETA_ONE * moment_one + (1.0 - BETA_ONE) * grad_sum
    new_two = BETA_TWO * moment_two + (1.0 - BETA_TWO) * grad_sum * grad_sum
    corrected_one = new_one / (1.0 - BETA_ONE ** STEP)
    corrected_two = new_two / (1.0 - BETA_TWO ** STEP)
    new_param = param - rate * (corrected_one / (jnp.sqrt(corrected_two) + EPS_ADAM) + DECAY * param)
    return (new_param, new_one, new_two)

def sequence_layer(inputs, length, blocks, head_vecs, norm_vecs, relative_table):
    seq_len = inputs.shape[0]
    q_proj = low_back(jnp.dot(inputs, blocks[:, 0], precision=FULL_PRECISION, preferred_element_type=jnp.float32))
    key_rows = low(low_back(jnp.dot(inputs, blocks[:, 1], precision=FULL_PRECISION, preferred_element_type=jnp.float32)))
    value_rows = low(low_back(jnp.dot(inputs, blocks[:, 2], precision=FULL_PRECISION, preferred_element_type=jnp.float32)))
    query_c = low(q_proj + head_vecs[0]).reshape(seq_len, HEAD_TOTAL, HEAD_FEATURES)
    query_position = low(q_proj + head_vecs[1]).reshape(seq_len, HEAD_TOTAL, HEAD_FEATURES)
    key_heads = key_rows.reshape(seq_len, HEAD_TOTAL, HEAD_FEATURES)
    value_heads = value_rows.reshape(seq_len, HEAD_TOTAL, HEAD_FEATURES)
    content = jnp.einsum('qhd,khd->hqk', query_c, key_heads, precision=FULL_PRECISION)
    position_offset = shifted_scores(jnp.einsum('slf,ylf->lsy', query_position, relative_table.reshape(-1, HEAD_TOTAL, HEAD_FEATURES), precision=FULL_PRECISION))
    scores = low_back(content + position_offset) * HEAD_FEATURES ** (-0.5)
    key_valid = jnp.arange(seq_len) < length
    scores = jnp.where(key_valid[None, None, :], scores, MASKED)
    row_max = lax.optimization_barrier(jnp.max(scores, axis=-1, keepdims=True))
    exp_scores = jnp.exp(scores - row_max)
    attend_probs = low(exp_scores / lax.optimization_barrier(jnp.sum(exp_scores, axis=-1, keepdims=True)))
    mixed_rows = jnp.einsum('hqk,khd->qhd', attend_probs, value_heads, precision=FULL_PRECISION).reshape(seq_len, HD)
    mixed_rows = low(low_back(mixed_rows))
    attn_out = low_back(jnp.dot(mixed_rows, blocks[:, 4].T, precision=FULL_PRECISION, preferred_element_type=jnp.float32)) + norm_vecs[4]
    first = layer_norm(inputs + attn_out, norm_vecs[0], norm_vecs[1])
    first_low = low(first)
    w_in = blocks[:, 5:9].reshape(D, FF)
    w_back = blocks[:, 9:13].reshape(D, FF)
    hidden = low_back(jnp.dot(first_low, w_in, precision=FULL_PRECISION, preferred_element_type=jnp.float32) + head_vecs[2:6].reshape(FF))
    active = low(gelu(hidden))
    ffn_out = low_back(jnp.dot(active, w_back.T, precision=FULL_PRECISION, preferred_element_type=jnp.float32)) + norm_vecs[5]
    return layer_norm(first + ffn_out, norm_vecs[2], norm_vecs[3])

def reference(tokens, lengths, weights, weight_m1, weight_m2, head_vecs, head_m1, head_m2, norm_vecs, norm_m1, norm_m2, cotangent):
    seq_inputs = tokens.astype(jnp.float32).reshape(SEQS, L, D)
    seq_grads = cotangent.astype(jnp.float32).reshape(SEQS, L, D)
    sine_low = relative_embedding(L, D).astype(jnp.bfloat16).astype(jnp.float32)

    def whole_layer(inputs, weights_f, head_f, norm_f):
        blocks = low(weights_f)
        relative_table = low(jnp.dot(sine_low, blocks[:, 3], precision=FULL_PRECISION, preferred_element_type=jnp.float32))

        def one_sequence(running, sequence_item):
            result = jax.checkpoint(sequence_layer)(sequence_item[0], sequence_item[1], blocks, head_f, norm_f, relative_table)
            return (running, result)
        _, outputs = lax.scan(one_sequence, jnp.zeros((), jnp.float32), (inputs, lengths))
        return outputs
    outputs, pullback = jax.vjp(whole_layer, seq_inputs, weights, head_vecs, norm_vecs)
    grad_in, grad_weights, grad_head, grad_norm = pullback(seq_grads)
    new_weights, new_weight_m1, new_weight_m2 = adam_update(weights, grad_weights, weight_m1, weight_m2, RATE_BIG)
    new_head, new_head_m1, new_head_m2 = adam_update(head_vecs, grad_head, head_m1, head_m2, RATE_SMALL)
    new_norm, new_norm_m1, new_norm_m2 = adam_update(norm_vecs, grad_norm, norm_m1, norm_m2, RATE_SMALL)
    out_tokens = outputs.reshape(TOKENS, D).astype(jnp.bfloat16)
    grad_tokens = grad_in.reshape(TOKENS, D)
    return (out_tokens, grad_tokens, new_weights, new_weight_m1, new_weight_m2, new_head, new_head_m1, new_head_m2, new_norm, new_norm_m1, new_norm_m2)
```

```python
import functools

import jax
import jax.numpy as jnp
from jax import lax
from jax.experimental import pallas as pl
from jax.experimental.pallas import tpu as pltpu
from jax.sharding import PartitionSpec as P

HEAD_FEATURES = 64
STEP = 5
EPS_NORM = 1e-05
EPS_ADAM = 1e-08
BETA_ONE = 0.5
BETA_TWO = 0.5
RATE_BIG = 0.03
RATE_SMALL = 0.2
DECAY = 0.01
MASKED = -1e30
SCALE = HEAD_FEATURES ** (-0.5)
ROW_BLOCK = 256
BF = jnp.bfloat16
F32 = jnp.float32
VMEM_LIMIT = 56 * 1024 * 1024

NN = (((1,), (0,)), ((), ()))
NT = (((1,), (1,)), ((), ()))
TN = (((0,), (0,)), ((), ()))


def mm(a, b, dims=NN):
    return lax.dot_general(a, b, dims, preferred_element_type=F32)


def whole(shape):
    return pl.BlockSpec(shape, lambda *_: (0,) * len(shape))


def params():
    return pltpu.CompilerParams(vmem_limit_bytes=VMEM_LIMIT)


def relative_embedding(length, model_width):
    distance = (length - 1 - jnp.arange(2 * length)).astype(F32)
    freq_index = jnp.arange(model_width // 2).astype(F32)
    inverse = 1.0 / 10000.0 ** (2.0 * freq_index / model_width)
    angles = distance[:, None] * inverse[None, :]
    return jnp.concatenate([jnp.sin(angles), jnp.cos(angles)], axis=1)


def adam_update(param, grad_sum, moment_one, moment_two, rate):
    new_one = BETA_ONE * moment_one + (1.0 - BETA_ONE) * grad_sum
    new_two = BETA_TWO * moment_two + (1.0 - BETA_TWO) * grad_sum * grad_sum
    corrected_one = new_one / (1.0 - BETA_ONE**STEP)
    corrected_two = new_two / (1.0 - BETA_TWO**STEP)
    new_param = param - rate * (
        corrected_one / (jnp.sqrt(corrected_two) + EPS_ADAM) + DECAY * param
    )
    return (new_param, new_one, new_two)


def full_matrix(w_ref):
    return jnp.concatenate([w_ref[0], w_ref[1]], axis=1)


def store_matrix(out_ref, value):
    half = value.shape[1] // 2
    out_ref[0] = value[:, :half].astype(BF)
    out_ref[1] = value[:, half:].astype(BF)


def project_kernel(x_ref, w_ref, vec_ref, sine_ref, qc_ref, qp_ref, k_ref, v_ref, rel_ref):
    step = pl.program_id(0)

    @pl.when(step == 0)
    def _():
        q = mm(x_ref[...], full_matrix(w_ref))
        qc_ref[...] = (q + vec_ref[0:1]).astype(BF) * BF(SCALE)
        qp_ref[...] = (q + vec_ref[1:2]).astype(BF) * BF(SCALE)

    @pl.when(step == 1)
    def _():
        k_ref[...] = mm(x_ref[...], full_matrix(w_ref)).astype(BF)

    @pl.when(step == 2)
    def _():
        v_ref[...] = mm(x_ref[...], full_matrix(w_ref)).astype(BF)

    @pl.when(step == 3)
    def _():
        rel_ref[...] = mm(sine_ref[...], full_matrix(w_ref)).astype(BF)


def project(x, w, vecs, sine):
    length, width = x.shape
    rows = sine.shape[0]
    shapes = [(length, width)] * 4 + [(rows, width)]
    return pl.pallas_call(
        project_kernel,
        grid=(4,),
        in_specs=[
            whole(x.shape),
            pl.BlockSpec((None,) + w.shape[1:], lambda b: (b, 0, 0, 0)),
            whole(vecs.shape),
            whole(sine.shape),
        ],
        out_specs=[whole(s) for s in shapes],
        out_shape=[jax.ShapeDtypeStruct(s, BF) for s in shapes],
        compiler_params=params(),
        name="project",
    )(x, w, vecs, sine)


def lane_mask(which, shape):
    lanes = lax.broadcasted_iota(jnp.int32, shape, 1)
    return (lanes >= HEAD_FEATURES) if which else (lanes < HEAD_FEATURES)


def attend_kernel(len_ref, qc_ref, qp_ref, k_ref, v_ref, rel_ref, probs_ref, mixed_ref):
    length = qc_ref.shape[0]
    block = ROW_BLOCK
    pair = qc_ref.shape[1]
    valid = lax.broadcasted_iota(jnp.int32, (1, length), 1) < len_ref[0]
    k = k_ref[...]
    v = v_ref[...]
    zero = jnp.zeros((), BF)
    for top in range(0, length, block):
        rows = pl.ds(top, block)
        first = length - block - top
        span = length + block
        rel = rel_ref[first : first + span, :]
        total = None
        for head in range(2):
            mask = lane_mask(head, (block, pair))
            content = mm(jnp.where(mask, qc_ref[rows, :], zero), k, NT)
            place = mm(jnp.where(mask, qp_ref[rows, :], zero), rel, NT)
            place = pltpu.roll(place, span - (block - 1), 1, stride=1, stride_axis=0)
            scores = jnp.where(valid, content + place[:, :length], MASKED)
            top_score = jnp.max(scores, axis=1, keepdims=True)
            grown = jnp.exp(scores - top_score)
            probs = grown * (1.0 / jnp.sum(grown, axis=1, keepdims=True))
            probs_low = probs.astype(BF)
            probs_ref[head, rows, :] = probs_low
            part = jnp.where(mask, mm(probs_low, v), 0.0)
            total = part if total is None else total + part
        mixed_ref[rows, :] = total.astype(BF)


def attend(length_used, qc, qp, k, v, rel):
    length, width = qc.shape
    pair = 2 * HEAD_FEATURES
    heads = width // HEAD_FEATURES
    column = pl.BlockSpec((length, pair), lambda p: (0, p))
    return pl.pallas_call(
        attend_kernel,
        grid=(heads // 2,),
        in_specs=[pl.BlockSpec(memory_space=pltpu.SMEM)]
        + [column] * 4
        + [pl.BlockSpec((rel.shape[0], pair), lambda p: (0, p))],
        out_specs=[pl.BlockSpec((2, length, length), lambda p: (p, 0, 0)), column],
        out_shape=[
            jax.ShapeDtypeStruct((heads, length, length), BF),
            jax.ShapeDtypeStruct((length, width), BF),
        ],
        compiler_params=params(),
        name="attend",
    )(length_used, qc, qp, k, v, rel)


def norm_parts(rows):
    mean = jnp.mean(rows, axis=1, keepdims=True)
    centred = rows - mean
    spread = jnp.mean(centred * centred, axis=1, keepdims=True)
    inverse = lax.rsqrt(spread + EPS_NORM)
    return centred * inverse, inverse


def norm_back(unit, inverse, scaled):
    return (
        scaled
        - jnp.mean(scaled, axis=1, keepdims=True)
        - unit * jnp.mean(scaled * unit, axis=1, keepdims=True)
    ) * inverse


def feed_kernel(
    mixed_ref, wo_ref, x_ref, nv_ref, hb_ref, win_ref, wback_ref, cot_ref,
    unit_ref, inv_ref, low_ref, act_ref, slope_ref, out_ref, gh2_ref, gffn_ref, sums_ref,
    first_ref, acc_ref,
):
    step = pl.program_id(0)
    last = pl.num_programs(0) - 1

    @pl.when(step == 0)
    def _():
        attn = mm(mixed_ref[...], full_matrix(wo_ref), NT)
        h1 = x_ref[...].astype(F32) + attn + nv_ref[4:5]
        unit, inverse = norm_parts(h1)
        unit_ref[...] = unit
        inv_ref[...] = jnp.broadcast_to(inverse, inv_ref.shape)
        first = unit * nv_ref[0:1] + nv_ref[1:2]
        first_ref[...] = first
        low_ref[...] = first.astype(BF)

    hidden = mm(low_ref[...], full_matrix(win_ref)) + hb_ref[0]
    bell = 0.5 * (1.0 + lax.erf(hidden * 0.7071067811865476))
    active = (hidden * bell).astype(BF)
    act_ref[...] = active
    slope_ref[...] = (
        bell + hidden * (jnp.exp(hidden * hidden * -0.5) * 0.3989422804014327)
    ).astype(BF)
    part = mm(active, full_matrix(wback_ref), NT)

    @pl.when(step == 0)
    def _():
        acc_ref[...] = part

    @pl.when(step > 0)
    def _():
        acc_ref[...] += part

    @pl.when(step == last)
    def _():
        h2 = first_ref[...] + acc_ref[...] + nv_ref[5:6]
        unit, inverse = norm_parts(h2)
        out_ref[...] = (unit * nv_ref[2:3] + nv_ref[3:4]).astype(BF)
        cot = cot_ref[...].astype(F32)
        gh2 = norm_back(unit, inverse, cot * nv_ref[2:3])
        gh2_ref[...] = gh2
        gffn_ref[...] = gh2.astype(BF)
        sums_ref[0:1] = jnp.sum(cot * unit, axis=0, keepdims=True)
        sums_ref[1:2] = jnp.sum(cot, axis=0, keepdims=True)
        sums_ref[2:3] = jnp.sum(gh2, axis=0, keepdims=True)
        sums_ref[3:8] = jnp.zeros((5, sums_ref.shape[1]), F32)


def feed(mixed, wo, x, nv, hb, win, wback, cot):
    length, width = x.shape
    blocks = win.shape[0]
    matrix = pl.BlockSpec((None,) + win.shape[1:], lambda b: (b, 0, 0, 0))
    one = whole((length, width))
    column = pl.BlockSpec((None, length, width), lambda b: (b, 0, 0))
    token = lambda d: jax.ShapeDtypeStruct((length, width), d)
    hidden = jax.ShapeDtypeStruct((blocks, length, width), BF)
    return pl.pallas_call(
        feed_kernel,
        grid=(blocks,),
        in_specs=[
            one,
            pl.BlockSpec((None,) + wo.shape[1:], lambda b: (0, 0, 0, 0)),
            one,
            whole(nv.shape),
            pl.BlockSpec((1, 1, width), lambda b: (b, 0, 0)),
            matrix,
            matrix,
            one,
        ],
        out_specs=[
            one, whole((length, 128)), one, column, column, one, one, one, whole((8, width)),
        ],
        out_shape=[
            token(F32), jax.ShapeDtypeStruct((length, 128), F32), token(BF), hidden, hidden,
            token(BF), token(F32), token(BF), jax.ShapeDtypeStruct((8, width), F32),
        ],
        scratch_shapes=[pltpu.VMEM((length, width), F32), pltpu.VMEM((length, width), F32)],
        compiler_params=params(),
        name="feed",
    )(mixed, wo, x, nv, hb, win, wback, cot)


def back_grad_kernel(gffn_ref, act_ref, out_ref, turned_ref):
    @pl.when(pl.program_id(0) == 0)
    def _():
        turned_ref[...] = gffn_ref[...].T

    store_matrix(out_ref, mm(turned_ref[...], act_ref[...]))


def back_grad(gffn, active):
    length, width = gffn.shape
    blocks = active.shape[0]
    shape = (blocks, 2, width, width // 2)
    return pl.pallas_call(
        back_grad_kernel,
        grid=(blocks,),
        in_specs=[
            whole(gffn.shape),
            pl.BlockSpec((None, length, width), lambda b: (b, 0, 0)),
        ],
        out_specs=pl.BlockSpec((None,) + shape[1:], lambda b: (b, 0, 0, 0)),
        out_shape=jax.ShapeDtypeStruct(shape, BF),
        scratch_shapes=[pltpu.VMEM((width, length), BF)],
        compiler_params=params(),
        name="back_grad",
    )(gffn, active)


def feed_back_kernel(
    gffn_ref, slope_ref, low_ref, wback_ref, win_ref, gh2_ref, unit_ref, inv_ref, nv_ref,
    wo_ref, mixed_ref,
    gwin_ref, hsum_ref, gh1_ref, gwo_ref, gmixed_ref, sums_ref,
    turned_ref, acc_ref,
):
    step = pl.program_id(0)
    last = pl.num_programs(0) - 1

    @pl.when(step == 0)
    def _():
        turned_ref[...] = low_ref[...].T
        acc_ref[...] = gh2_ref[...]

    gact = mm(gffn_ref[...], full_matrix(wback_ref))
    ghid = (gact * slope_ref[...].astype(F32)).astype(BF)
    hsum_ref[0] = jnp.sum(ghid.astype(F32), axis=0, keepdims=True)
    store_matrix(gwin_ref, mm(turned_ref[...], ghid))
    acc_ref[...] += mm(ghid, full_matrix(win_ref), NT)

    @pl.when(step == last)
    def _():
        gfirst = acc_ref[...]
        unit = unit_ref[...]
        gh1 = norm_back(unit, inv_ref[:, 0:1], gfirst * nv_ref[0:1])
        gh1_ref[...] = gh1
        gattn = gh1.astype(BF)
        store_matrix(gwo_ref, mm(gattn.T, mixed_ref[...]))
        gmixed_ref[...] = mm(gattn, full_matrix(wo_ref)).astype(BF)
        sums_ref[0:1] = jnp.sum(gfirst * unit, axis=0, keepdims=True)
        sums_ref[1:2] = jnp.sum(gfirst, axis=0, keepdims=True)
        sums_ref[2:3] = jnp.sum(gh1, axis=0, keepdims=True)
        sums_ref[3:8] = jnp.zeros((5, sums_ref.shape[1]), F32)


def feed_back(gffn, slope, low, wback, win, gh2, unit, inv, nv, wo, mixed):
    length, width = gffn.shape
    blocks = slope.shape[0]
    matrix = pl.BlockSpec((None,) + win.shape[1:], lambda b: (b, 0, 0, 0))
    single = pl.BlockSpec((None,) + wo.shape[1:], lambda b: (0, 0, 0, 0))
    one = whole((length, width))
    token = lambda d: jax.ShapeDtypeStruct((length, width), d)
    return pl.pallas_call(
        feed_back_kernel,
        grid=(blocks,),
        in_specs=[
            one,
            pl.BlockSpec((None, length, width), lambda b: (b, 0, 0)),
            one, matrix, matrix, one, one, whole(inv.shape), whole(nv.shape), single, one,
        ],
        out_specs=[
            matrix,
            pl.BlockSpec((1, 1, width), lambda b: (b, 0, 0)),
            one, single, one, whole((8, width)),
        ],
        out_shape=[
            jax.ShapeDtypeStruct(win.shape, BF),
            jax.ShapeDtypeStruct((blocks, 1, width), F32),
            token(F32),
            jax.ShapeDtypeStruct((1,) + win.shape[1:], BF),
            token(BF),
            jax.ShapeDtypeStruct((8, width), F32),
        ],
        scratch_shapes=[pltpu.VMEM((width, length), BF), pltpu.VMEM((length, width), F32)],
        compiler_params=params(),
        name="feed_back",
    )(gffn, slope, low, wback, win, gh2, unit, inv, nv, wo, mixed)


def attend_back_kernel(
    probs_ref, gm_ref, qc_ref, qp_ref, k_ref, v_ref, rel_ref,
    gq_ref, gk_ref, gv_ref, grel_ref, sums_ref,
    rel_acc,
):
    length, pair = gm_ref.shape
    block = ROW_BLOCK
    span = length + block
    zero = jnp.zeros((), BF)
    flip = (
        lax.broadcasted_iota(jnp.int32, (block, block), 0)
        + lax.broadcasted_iota(jnp.int32, (block, block), 1)
        == block - 1
    ).astype(F32).astype(BF)
    k = k_ref[...]
    v = v_ref[...]
    rel_acc[...] = jnp.zeros_like(rel_acc)
    gk = None
    gv = None
    sum_c = None
    sum_p = None
    for top in range(0, length, block):
        rows = pl.ds(top, block)
        first = length - block - top
        band = pl.ds(first, span)
        rel = rel_ref[band, :]
        qp_turned = mm(flip, qp_ref[rows, :]).astype(BF)
        gqc = None
        gqp = None
        for head in range(2):
            mask = lane_mask(head, (block, pair))
            tall = lane_mask(head, (length, pair))
            probs_low = probs_ref[head, rows, :]
            probs = probs_low.astype(F32)
            gm = jnp.where(mask, gm_ref[rows, :], zero)
            gprobs = mm(gm, v, NT)
            product = probs * gprobs
            inner = jnp.sum(product, axis=1, keepdims=True)
            gsum = (product - probs * inner).astype(BF)
            a = mm(gsum, jnp.where(tall, k, zero))
            gqc = a if gqc is None else gqc + a
            b = mm(gsum, jnp.where(mask, qc_ref[rows, :], zero), TN)
            gk = b if gk is None else gk + b
            c = mm(probs_low, gm, TN)
            gv = c if gv is None else gv + c
            turned = mm(flip, gsum)
            wide = jnp.concatenate([turned, jnp.zeros((block, block), F32)], axis=1)
            wide = pltpu.roll(wide, 0, 1, stride=1, stride_axis=0).astype(BF)
            rel_mask = lane_mask(head, (span, pair))
            d = mm(wide, jnp.where(rel_mask, rel, zero))
            gqp = d if gqp is None else gqp + d
            rel_acc[band, :] += mm(wide, jnp.where(mask, qp_turned, zero), TN)
        gqc = gqc * SCALE
        gqp = gqp * SCALE
        high = gqp.astype(BF)
        rest = (gqp - high.astype(F32)).astype(BF)
        straight = mm(flip, high) + mm(flip, rest)
        gq_ref[rows, :] = (gqc + straight).astype(BF)
        e = jnp.sum(gqc, axis=0, keepdims=True)
        f = jnp.sum(gqp, axis=0, keepdims=True)
        sum_c = e if sum_c is None else sum_c + e
        sum_p = f if sum_p is None else sum_p + f
    gk_ref[...] = gk.astype(BF)
    gv_ref[...] = gv.astype(BF)
    grel_ref[...] = rel_acc[...].astype(BF)
    sums_ref[0:1] = sum_c
    sums_ref[1:2] = sum_p
    sums_ref[2:8] = jnp.zeros((6, pair), F32)


def attend_back(probs, gm, qc, qp, k, v, rel):
    length, width = qc.shape
    pair = 2 * HEAD_FEATURES
    heads = width // HEAD_FEATURES
    column = pl.BlockSpec((length, pair), lambda p: (0, p))
    tall = pl.BlockSpec((rel.shape[0], pair), lambda p: (0, p))
    token = jax.ShapeDtypeStruct((length, width), BF)
    return pl.pallas_call(
        attend_back_kernel,
        grid=(heads // 2,),
        in_specs=[pl.BlockSpec((2, length, length), lambda p: (p, 0, 0))] + [column] * 5 + [tall],
        out_specs=[column, column, column, tall, pl.BlockSpec((8, pair), lambda p: (0, p))],
        out_shape=[
            token, token, token,
            jax.ShapeDtypeStruct(rel.shape, BF),
            jax.ShapeDtypeStruct((8, width), F32),
        ],
        scratch_shapes=[pltpu.VMEM((rel.shape[0], pair), F32)],
        compiler_params=params(),
        name="attend_back",
    )(probs, gm, qc, qp, k, v, rel)


def project_back_kernel(
    x_ref, gq_ref, gk_ref, gv_ref, grel_ref, sine_t_ref, w_ref, gh1_ref,
    gw_ref, gtok_ref,
    turned_ref,
):
    step = pl.program_id(0)

    @pl.when(step == 0)
    def _():
        turned_ref[...] = x_ref[...].T
        gtok_ref[...] = gh1_ref[...]

    for which, g_ref in enumerate((gq_ref, gk_ref, gv_ref)):

        @pl.when(step == which)
        def _():
            store_matrix(gw_ref, mm(turned_ref[...], g_ref[...]))
            gtok_ref[...] += mm(g_ref[...], full_matrix(w_ref), NT)

    @pl.when(step == 3)
    def _():
        store_matrix(gw_ref, mm(sine_t_ref[...], grel_ref[...]))


def project_back(x, gq, gk, gv, grel, sine_t, w, gh1):
    length, width = x.shape
    one = whole((length, width))
    return pl.pallas_call(
        project_back_kernel,
        grid=(4,),
        in_specs=[
            one, one, one, one, whole(grel.shape), whole(sine_t.shape),
            pl.BlockSpec((None,) + w.shape[1:], lambda b: (jnp.minimum(b, 2), 0, 0, 0)),
            one,
        ],
        out_specs=[pl.BlockSpec((None,) + w.shape[1:], lambda b: (b, 0, 0, 0)), one],
        out_shape=[
            jax.ShapeDtypeStruct((4,) + w.shape[1:], BF),
            jax.ShapeDtypeStruct((length, width), F32),
        ],
        scratch_shapes=[pltpu.VMEM((width, length), BF)],
        compiler_params=params(),
        name="project_back",
    )(x, gq, gk, gv, grel, sine_t, w, gh1)


def gather_matrices(shard):
    dp, mp = lax.axis_size("dp"), lax.axis_size("mp")
    blocks, rows, columns = shard.shape
    pieces = lax.all_gather(shard, ("mp", "dp"), axis=0, tiled=False)
    pieces = pieces.reshape(mp, dp, blocks, rows, columns)
    return pieces.transpose(2, 0, 1, 3, 4).reshape(blocks, mp, dp * rows, columns)


def scatter_matrices(grads):
    dp = lax.axis_size("dp")
    blocks, mp, all_rows, columns = grads.shape
    pieces = grads.reshape(blocks, mp, dp, all_rows // dp, columns).transpose(1, 2, 0, 3, 4)
    pieces = pieces.reshape(mp * dp, blocks, all_rows // dp, columns)
    return lax.psum_scatter(pieces, ("mp", "dp"), scatter_dimension=0, tiled=False)


def per_device(
    tokens,
    lengths,
    weights,
    weight_m1,
    weight_m2,
    head_vecs,
    head_m1,
    head_m2,
    norm_vecs,
    norm_m1,
    norm_m2,
    cotangent,
):
    mp_index = lax.axis_index("mp")
    seq_len = cotangent.shape[0]
    local_width = weights.shape[2]
    model_width = tokens.shape[1]
    x = lax.dynamic_slice_in_dim(tokens, mp_index * seq_len, seq_len, 0)
    used = lax.dynamic_slice_in_dim(lengths, mp_index, 1, 0)
    sine = relative_embedding(seq_len, model_width).astype(BF)
    shard = weights.transpose(1, 0, 2)
    blocks = gather_matrices(shard.astype(BF))
    heads_all = lax.all_gather(head_vecs, "mp", axis=1, tiled=True)

    qc, qp, k, v, rel = project(x, blocks[0:4], heads_all[0:2], sine)
    probs, mixed = attend(used, qc, qp, k, v, rel)
    hb = heads_all[2:6].reshape(4, 1, model_width)
    unit, inv, low, active, slope, out, gh2, gffn, sums2 = feed(
        mixed, blocks[4:5], x, norm_vecs, hb, blocks[5:9], blocks[9:13], cotangent
    )
    gwback = back_grad(gffn, active)
    gwin, hsum, gh1, gwo, gmixed, sums1 = feed_back(
        gffn, slope, low, blocks[9:13], blocks[5:9], gh2, unit, inv, norm_vecs, blocks[4:5], mixed
    )
    gq, gk, gv, grel, sums_q = attend_back(probs, gmixed, qc, qp, k, v, rel)
    gproj, grad_tokens = project_back(x, gq, gk, gv, grel, sine.T, blocks[0:4], gh1)

    weight_grad = scatter_matrices(
        jnp.concatenate([gproj, gwo, gwin, gwback], axis=0)
    ).astype(F32)
    norm_part = jnp.concatenate([sums1[0:2], sums2[0:2], sums1[2:3], sums2[2:3]], axis=0)
    head_part = jnp.concatenate([sums_q[0:2], hsum[:, 0]], axis=0)
    norm_grad, head_total = lax.psum((norm_part, head_part), ("dp", "mp"))
    head_grad = lax.dynamic_slice_in_dim(head_total, mp_index * local_width, local_width, 1)

    new_big = adam_update(
        shard, weight_grad, weight_m1.transpose(1, 0, 2), weight_m2.transpose(1, 0, 2), RATE_BIG
    )
    new_weights, new_weight_m1, new_weight_m2 = [a.transpose(1, 0, 2) for a in new_big]
    new_head, new_head_m1, new_head_m2 = adam_update(
        head_vecs, head_grad, head_m1, head_m2, RATE_SMALL
    )
    new_norm, new_norm_m1, new_norm_m2 = adam_update(
        norm_vecs, norm_grad, norm_m1, norm_m2, RATE_SMALL
    )
    return (
        out,
        grad_tokens,
        new_weights,
        new_weight_m1,
        new_weight_m2,
        new_head,
        new_head_m1,
        new_head_m2,
        new_norm,
        new_norm_m1,
        new_norm_m2,
    )


def solution(mesh):
    shard = P("dp", None, "mp")
    return jax.shard_map(
        per_device,
        mesh=mesh,
        in_specs=(P("dp", None), P("dp"), shard, shard, shard)
        + (P(None, "mp"),) * 3
        + (P(),) * 3
        + (P(("dp", "mp"), None),),
        out_specs=(P(("dp", "mp"), None),) * 2
        + (shard,) * 3
        + (P(None, "mp"),) * 3
        + (P(),) * 3,
        check_vma=False,
    )
```

```python
import functools

import jax
import jax.numpy as jnp
from jax import lax
from jax.experimental import pallas as pl
from jax.experimental.pallas import tpu as pltpu
from jax.sharding import PartitionSpec as P

HEAD_FEATURES = 64
STEP = 5
EPS_NORM = 1e-05
EPS_ADAM = 1e-08
BETA_ONE = 0.5
BETA_TWO = 0.5
RATE_BIG = 0.03
RATE_SMALL = 0.2
DECAY = 0.01
MASKED = -1e30
SCALE = HEAD_FEATURES ** (-0.5)
ROW_BLOCK = 256
BF = jnp.bfloat16
F32 = jnp.float32
VMEM_LIMIT = 56 * 1024 * 1024

NN = (((1,), (0,)), ((), ()))
NT = (((1,), (1,)), ((), ()))
TN = (((0,), (0,)), ((), ()))


def mm(a, b, dims=NN):
    return lax.dot_general(a, b, dims, preferred_element_type=F32)


def whole(shape):
    return pl.BlockSpec(shape, lambda *_: (0,) * len(shape))


def params():
    return pltpu.CompilerParams(vmem_limit_bytes=VMEM_LIMIT)


def cost(micros):
    return pl.CostEstimate(flops=int(micros * 1e9), bytes_accessed=0, transcendentals=0)


def relative_embedding(length, model_width):
    distance = (length - 1 - jnp.arange(2 * length)).astype(F32)
    freq_index = jnp.arange(model_width // 2).astype(F32)
    inverse = 1.0 / 10000.0 ** (2.0 * freq_index / model_width)
    angles = distance[:, None] * inverse[None, :]
    return jnp.concatenate([jnp.sin(angles), jnp.cos(angles)], axis=1)


def adam_update(param, grad_sum, moment_one, moment_two, rate):
    new_one = BETA_ONE * moment_one + (1.0 - BETA_ONE) * grad_sum
    new_two = BETA_TWO * moment_two + (1.0 - BETA_TWO) * grad_sum * grad_sum
    corrected_one = new_one / (1.0 - BETA_ONE**STEP)
    corrected_two = new_two / (1.0 - BETA_TWO**STEP)
    new_param = param - rate * (
        corrected_one / (jnp.sqrt(corrected_two) + EPS_ADAM) + DECAY * param
    )
    return (new_param, new_one, new_two)


def weight_spec(shape, which):
    if len(shape) == 5:
        return pl.BlockSpec(shape[:2] + (None,) + shape[3:], lambda b: (0, 0, which(b), 0, 0))
    return pl.BlockSpec((None,) + shape[1:], lambda b: (which(b), 0, 0, 0))


def full_matrix(w_ref):
    w = w_ref[...]
    if w.ndim == 4:
        w = w.reshape(w.shape[0], w.shape[1] * w.shape[2], w.shape[3])
    return jnp.concatenate([w[0], w[1]], axis=1)


RING = ((0, 0, 0), (0, 0, 1), (0, 1, 1), (0, 1, 0), (1, 1, 0), (1, 1, 1), (1, 0, 1), (1, 0, 0))


def layered(lines, rows):
    return rows % 16 == 0


def grad_shape(blocks, lines, rows, columns):
    if layered(lines, rows):
        return (len(RING), lines, blocks, rows, columns)
    return (blocks, 2, lines * 4 * rows, columns)


def grad_spec(shape):
    if len(shape) == 5:
        return pl.BlockSpec(shape[:2] + (None,) + shape[3:], lambda b: (0, 0, b, 0, 0))
    return pl.BlockSpec((None,) + shape[1:], lambda b: (b, 0, 0, 0))


def store_matrix(out_ref, value):
    half = value.shape[1] // 2
    low = value.astype(BF)
    if len(out_ref.shape) == 3:
        out_ref[0] = low[:, :half]
        out_ref[1] = low[:, half:]
        return
    places, lines, rows, _ = out_ref.shape
    for place, (mp, y, core) in enumerate(RING):
        for line in range(lines):
            top = (line * 4 + y * 2 + core) * rows
            out_ref[place, line] = low[top : top + rows, mp * half : (mp + 1) * half]


def project_kernel(x_ref, w_ref, vec_ref, sine_ref, qc_ref, qp_ref, k_ref, v_ref, rel_ref):
    step = pl.program_id(0)

    @pl.when(step == 0)
    def _():
        q = mm(x_ref[...], full_matrix(w_ref))
        qc_ref[...] = (q + vec_ref[0:1]).astype(BF) * BF(SCALE)
        qp_ref[...] = (q + vec_ref[1:2]).astype(BF) * BF(SCALE)

    @pl.when(step == 1)
    def _():
        k_ref[...] = mm(x_ref[...], full_matrix(w_ref)).astype(BF)

    @pl.when(step == 2)
    def _():
        v_ref[...] = mm(x_ref[...], full_matrix(w_ref)).astype(BF)

    @pl.when(step == 3)
    def _():
        rel_ref[...] = mm(sine_ref[...], full_matrix(w_ref)).astype(BF)


def project(x, w, vecs, sine):
    length, width = x.shape
    rows = sine.shape[0]
    shapes = [(length, width)] * 4 + [(rows, width)]
    return pl.pallas_call(
        project_kernel,
        grid=(4,),
        in_specs=[
            whole(x.shape),
            weight_spec(w.shape, lambda b: b),
            whole(vecs.shape),
            whole(sine.shape),
        ],
        out_specs=[whole(s) for s in shapes],
        out_shape=[jax.ShapeDtypeStruct(s, BF) for s in shapes],
        compiler_params=params(),
        cost_estimate=cost(9),
        name="project",
    )(x, w, vecs, sine)


def lane_mask(which, shape):
    lanes = lax.broadcasted_iota(jnp.int32, shape, 1)
    return (lanes >= HEAD_FEATURES) if which else (lanes < HEAD_FEATURES)


def attend_kernel(len_ref, qc_ref, qp_ref, k_ref, v_ref, rel_ref, probs_ref, mixed_ref):
    length = qc_ref.shape[0]
    block = ROW_BLOCK
    pair = qc_ref.shape[1]
    valid = lax.broadcasted_iota(jnp.int32, (1, length), 1) < len_ref[0]
    k = k_ref[...]
    v = v_ref[...]
    zero = jnp.zeros((), BF)
    for top in range(0, length, block):
        rows = pl.ds(top, block)
        first = length - block - top
        span = length + block
        rel = rel_ref[first : first + span, :]
        total = None
        for head in range(2):
            mask = lane_mask(head, (block, pair))
            content = mm(jnp.where(mask, qc_ref[rows, :], zero), k, NT)
            place = mm(jnp.where(mask, qp_ref[rows, :], zero), rel, NT)
            place = pltpu.roll(place, span - (block - 1), 1, stride=1, stride_axis=0)
            scores = jnp.where(valid, content + place[:, :length], MASKED)
            top_score = jnp.max(scores, axis=1, keepdims=True)
            grown = jnp.exp(scores - top_score)
            probs = grown * (1.0 / jnp.sum(grown, axis=1, keepdims=True))
            probs_low = probs.astype(BF)
            probs_ref[head, rows, :] = probs_low
            part = jnp.where(mask, mm(probs_low, v), 0.0)
            total = part if total is None else total + part
        mixed_ref[rows, :] = total.astype(BF)


def attend(length_used, qc, qp, k, v, rel):
    length, width = qc.shape
    pair = 2 * HEAD_FEATURES
    heads = width // HEAD_FEATURES
    column = pl.BlockSpec((length, pair), lambda p: (0, p))
    return pl.pallas_call(
        attend_kernel,
        grid=(heads // 2,),
        in_specs=[pl.BlockSpec(memory_space=pltpu.SMEM)]
        + [column] * 4
        + [pl.BlockSpec((rel.shape[0], pair), lambda p: (0, p))],
        out_specs=[pl.BlockSpec((2, length, length), lambda p: (p, 0, 0)), column],
        out_shape=[
            jax.ShapeDtypeStruct((heads, length, length), BF),
            jax.ShapeDtypeStruct((length, width), BF),
        ],
        compiler_params=params(),
        cost_estimate=cost(19),
        name="attend",
    )(length_used, qc, qp, k, v, rel)


def norm_parts(rows):
    mean = jnp.mean(rows, axis=1, keepdims=True)
    centred = rows - mean
    spread = jnp.mean(centred * centred, axis=1, keepdims=True)
    inverse = lax.rsqrt(spread + EPS_NORM)
    return centred * inverse, inverse


def norm_back(unit, inverse, scaled):
    return (
        scaled
        - jnp.mean(scaled, axis=1, keepdims=True)
        - unit * jnp.mean(scaled * unit, axis=1, keepdims=True)
    ) * inverse


def feed_kernel(
    mixed_ref, wo_ref, x_ref, nv_ref, hb_ref, win_ref, wback_ref, cot_ref,
    unit_ref, inv_ref, low_ref, act_ref, slope_ref, out_ref, gh2_ref, gffn_ref, sums_ref,
    first_ref, acc_ref,
):
    step = pl.program_id(0)
    last = pl.num_programs(0) - 1

    @pl.when(step == 0)
    def _():
        attn = mm(mixed_ref[...], full_matrix(wo_ref), NT)
        h1 = x_ref[...].astype(F32) + attn + nv_ref[4:5]
        unit, inverse = norm_parts(h1)
        unit_ref[...] = unit
        inv_ref[...] = jnp.broadcast_to(inverse, inv_ref.shape)
        first = unit * nv_ref[0:1] + nv_ref[1:2]
        first_ref[...] = first
        low_ref[...] = first.astype(BF)

    hidden = mm(low_ref[...], full_matrix(win_ref)) + hb_ref[0]
    bell = 0.5 * (1.0 + lax.erf(hidden * 0.7071067811865476))
    active = (hidden * bell).astype(BF)
    act_ref[...] = active
    slope_ref[...] = (
        bell + hidden * (jnp.exp(hidden * hidden * -0.5) * 0.3989422804014327)
    ).astype(BF)
    part = mm(active, full_matrix(wback_ref), NT)

    @pl.when(step == 0)
    def _():
        acc_ref[...] = part

    @pl.when(step > 0)
    def _():
        acc_ref[...] += part

    @pl.when(step == last)
    def _():
        h2 = first_ref[...] + acc_ref[...] + nv_ref[5:6]
        unit, inverse = norm_parts(h2)
        out_ref[...] = (unit * nv_ref[2:3] + nv_ref[3:4]).astype(BF)
        cot = cot_ref[...].astype(F32)
        gh2 = norm_back(unit, inverse, cot * nv_ref[2:3])
        gh2_ref[...] = gh2
        gffn_ref[...] = gh2.astype(BF)
        sums_ref[0:1] = jnp.sum(cot * unit, axis=0, keepdims=True)
        sums_ref[1:2] = jnp.sum(cot, axis=0, keepdims=True)
        sums_ref[2:3] = jnp.sum(gh2, axis=0, keepdims=True)
        sums_ref[3:8] = jnp.zeros((5, sums_ref.shape[1]), F32)


def feed(mixed, w, x, nv, hb, w_feed, cot):
    length, width = x.shape
    blocks = hb.shape[0]
    one = whole((length, width))
    column = pl.BlockSpec((None, length, width), lambda b: (b, 0, 0))
    token = lambda d: jax.ShapeDtypeStruct((length, width), d)
    hidden = jax.ShapeDtypeStruct((blocks, length, width), BF)
    return pl.pallas_call(
        feed_kernel,
        grid=(blocks,),
        in_specs=[
            one,
            weight_spec(w.shape, lambda b: 4),
            one,
            whole(nv.shape),
            pl.BlockSpec((1, 1, width), lambda b: (b, 0, 0)),
            weight_spec(w_feed.shape, lambda b: b),
            weight_spec(w_feed.shape, lambda b: b + blocks),
            one,
        ],
        out_specs=[
            one, whole((length, 128)), one, column, column, one, one, one, whole((8, width)),
        ],
        out_shape=[
            token(F32), jax.ShapeDtypeStruct((length, 128), F32), token(BF), hidden, hidden,
            token(BF), token(F32), token(BF), jax.ShapeDtypeStruct((8, width), F32),
        ],
        scratch_shapes=[pltpu.VMEM((length, width), F32), pltpu.VMEM((length, width), F32)],
        compiler_params=params(),
        cost_estimate=cost(17),
        name="feed",
    )(mixed, w, x, nv, hb, w_feed, w_feed, cot)


def back_grad_kernel(gffn_ref, act_ref, out_ref, turned_ref):
    @pl.when(pl.program_id(0) == 0)
    def _():
        turned_ref[...] = gffn_ref[...].T

    store_matrix(out_ref, mm(turned_ref[...], act_ref[...]))


def back_grad(gffn, active, lines, rows):
    length, width = gffn.shape
    blocks = active.shape[0]
    shape = grad_shape(blocks, lines, rows, width // 2)
    return pl.pallas_call(
        back_grad_kernel,
        grid=(blocks,),
        in_specs=[
            whole(gffn.shape),
            pl.BlockSpec((None, length, width), lambda b: (b, 0, 0)),
        ],
        out_specs=grad_spec(shape),
        out_shape=jax.ShapeDtypeStruct(shape, BF),
        scratch_shapes=[pltpu.VMEM((width, length), BF)],
        compiler_params=params(),
        cost_estimate=cost(7),
        name="back_grad",
    )(gffn, active)


def feed_back_kernel(
    gffn_ref, slope_ref, low_ref, wback_ref, win_ref, gh2_ref, unit_ref, inv_ref, nv_ref,
    wo_ref, mixed_ref,
    gw_ref, hsum_ref, gh1_ref, gmixed_ref, sums_ref,
    turned_ref, acc_ref,
):
    step = pl.program_id(0)
    last = pl.num_programs(0) - 1

    @pl.when(step == 0)
    def _():
        turned_ref[...] = low_ref[...].T
        acc_ref[...] = gh2_ref[...]

    @pl.when(step < last)
    def _():
        gact = mm(gffn_ref[...], full_matrix(wback_ref))
        ghid = (gact * slope_ref[...].astype(F32)).astype(BF)
        hsum_ref[0] = jnp.sum(ghid.astype(F32), axis=0, keepdims=True)
        store_matrix(gw_ref, mm(turned_ref[...], ghid))
        acc_ref[...] += mm(ghid, full_matrix(win_ref), NT)

    @pl.when(step == last)
    def _():
        gfirst = acc_ref[...]
        unit = unit_ref[...]
        gh1 = norm_back(unit, inv_ref[:, 0:1], gfirst * nv_ref[0:1])
        gh1_ref[...] = gh1
        gattn = gh1.astype(BF)
        store_matrix(gw_ref, mm(gattn.T, mixed_ref[...]))
        gmixed_ref[...] = mm(gattn, full_matrix(wo_ref)).astype(BF)
        sums_ref[0:1] = jnp.sum(gfirst * unit, axis=0, keepdims=True)
        sums_ref[1:2] = jnp.sum(gfirst, axis=0, keepdims=True)
        sums_ref[2:3] = jnp.sum(gh1, axis=0, keepdims=True)
        sums_ref[3:8] = jnp.zeros((5, sums_ref.shape[1]), F32)


def feed_back(gffn, slope, low, w_feed, gh2, unit, inv, nv, w, mixed, lines, rows):
    length, width = gffn.shape
    blocks = slope.shape[0]
    capped = lambda b: jnp.minimum(b, blocks - 1)
    one = whole((length, width))
    token = lambda d: jax.ShapeDtypeStruct((length, width), d)
    shape = grad_shape(blocks + 1, lines, rows, width // 2)
    return pl.pallas_call(
        feed_back_kernel,
        grid=(blocks + 1,),
        in_specs=[
            one,
            pl.BlockSpec((None, length, width), lambda b: (capped(b), 0, 0)),
            one,
            weight_spec(w_feed.shape, lambda b: capped(b) + blocks),
            weight_spec(w_feed.shape, capped),
            one, one, whole(inv.shape), whole(nv.shape), weight_spec(w.shape, lambda b: 4), one,
        ],
        out_specs=[
            grad_spec(shape),
            pl.BlockSpec((1, 1, width), lambda b: (capped(b), 0, 0)),
            one, one, whole((8, width)),
        ],
        out_shape=[
            jax.ShapeDtypeStruct(shape, BF),
            jax.ShapeDtypeStruct((blocks, 1, width), F32),
            token(F32),
            token(BF),
            jax.ShapeDtypeStruct((8, width), F32),
        ],
        scratch_shapes=[pltpu.VMEM((width, length), BF), pltpu.VMEM((length, width), F32)],
        compiler_params=params(),
        cost_estimate=cost(17),
        name="feed_back",
    )(gffn, slope, low, w_feed, w_feed, gh2, unit, inv, nv, w, mixed)


def attend_back_kernel(
    probs_ref, gm_ref, qc_ref, qp_ref, k_ref, v_ref, rel_ref,
    gq_ref, gk_ref, gv_ref, grel_ref, sums_ref,
    rel_acc,
):
    length, pair = gm_ref.shape
    block = ROW_BLOCK
    span = length + block
    zero = jnp.zeros((), BF)
    flip = (
        lax.broadcasted_iota(jnp.int32, (block, block), 0)
        + lax.broadcasted_iota(jnp.int32, (block, block), 1)
        == block - 1
    ).astype(F32).astype(BF)
    k = k_ref[...]
    v = v_ref[...]
    rel_acc[...] = jnp.zeros_like(rel_acc)
    gk = None
    gv = None
    sum_c = None
    sum_p = None
    for top in range(0, length, block):
        rows = pl.ds(top, block)
        first = length - block - top
        band = pl.ds(first, span)
        rel = rel_ref[band, :]
        qp_turned = mm(flip, qp_ref[rows, :]).astype(BF)
        gqc = None
        gqp = None
        for head in range(2):
            mask = lane_mask(head, (block, pair))
            tall = lane_mask(head, (length, pair))
            probs_low = probs_ref[head, rows, :]
            probs = probs_low.astype(F32)
            gm = jnp.where(mask, gm_ref[rows, :], zero)
            gprobs = mm(gm, v, NT)
            product = probs * gprobs
            inner = jnp.sum(product, axis=1, keepdims=True)
            gsum = (product - probs * inner).astype(BF)
            a = mm(gsum, jnp.where(tall, k, zero))
            gqc = a if gqc is None else gqc + a
            b = mm(gsum, jnp.where(mask, qc_ref[rows, :], zero), TN)
            gk = b if gk is None else gk + b
            c = mm(probs_low, gm, TN)
            gv = c if gv is None else gv + c
            turned = mm(flip, gsum)
            wide = jnp.concatenate([turned, jnp.zeros((block, block), F32)], axis=1)
            wide = pltpu.roll(wide, 0, 1, stride=1, stride_axis=0).astype(BF)
            rel_mask = lane_mask(head, (span, pair))
            d = mm(wide, jnp.where(rel_mask, rel, zero))
            gqp = d if gqp is None else gqp + d
            rel_acc[band, :] += mm(wide, jnp.where(mask, qp_turned, zero), TN)
        gqc = gqc * SCALE
        gqp = gqp * SCALE
        high = gqp.astype(BF)
        rest = (gqp - high.astype(F32)).astype(BF)
        straight = mm(flip, high) + mm(flip, rest)
        gq_ref[rows, :] = (gqc + straight).astype(BF)
        e = jnp.sum(gqc, axis=0, keepdims=True)
        f = jnp.sum(gqp, axis=0, keepdims=True)
        sum_c = e if sum_c is None else sum_c + e
        sum_p = f if sum_p is None else sum_p + f
    gk_ref[...] = gk.astype(BF)
    gv_ref[...] = gv.astype(BF)
    grel_ref[...] = rel_acc[...].astype(BF)
    sums_ref[0:1] = sum_c
    sums_ref[1:2] = sum_p
    sums_ref[2:8] = jnp.zeros((6, pair), F32)


def attend_back(probs, gm, qc, qp, k, v, rel):
    length, width = qc.shape
    pair = 2 * HEAD_FEATURES
    heads = width // HEAD_FEATURES
    column = pl.BlockSpec((length, pair), lambda p: (0, p))
    tall = pl.BlockSpec((rel.shape[0], pair), lambda p: (0, p))
    token = jax.ShapeDtypeStruct((length, width), BF)
    return pl.pallas_call(
        attend_back_kernel,
        grid=(heads // 2,),
        in_specs=[pl.BlockSpec((2, length, length), lambda p: (p, 0, 0))] + [column] * 5 + [tall],
        out_specs=[column, column, column, tall, pl.BlockSpec((8, pair), lambda p: (0, p))],
        out_shape=[
            token, token, token,
            jax.ShapeDtypeStruct(rel.shape, BF),
            jax.ShapeDtypeStruct((8, width), F32),
        ],
        scratch_shapes=[pltpu.VMEM((rel.shape[0], pair), F32)],
        compiler_params=params(),
        cost_estimate=cost(28),
        name="attend_back",
    )(probs, gm, qc, qp, k, v, rel)


def project_back_kernel(
    x_ref, gq_ref, gk_ref, gv_ref, grel_ref, sine_t_ref, w_ref, gh1_ref,
    gw_ref, gtok_ref,
    turned_ref,
):
    step = pl.program_id(0)

    @pl.when(step == 0)
    def _():
        turned_ref[...] = x_ref[...].T
        gtok_ref[...] = gh1_ref[...]

    for which, g_ref in enumerate((gq_ref, gk_ref, gv_ref)):

        @pl.when(step == which)
        def _():
            store_matrix(gw_ref, mm(turned_ref[...], g_ref[...]))
            gtok_ref[...] += mm(g_ref[...], full_matrix(w_ref), NT)

    @pl.when(step == 3)
    def _():
        store_matrix(gw_ref, mm(sine_t_ref[...], grel_ref[...]))


def project_back(x, gq, gk, gv, grel, sine_t, w, gh1, lines, rows):
    length, width = x.shape
    one = whole((length, width))
    shape = grad_shape(4, lines, rows, width // 2)
    return pl.pallas_call(
        project_back_kernel,
        grid=(4,),
        in_specs=[
            one, one, one, one, whole(grel.shape), whole(sine_t.shape),
            weight_spec(w.shape, lambda b: jnp.minimum(b, 2)),
            one,
        ],
        out_specs=[grad_spec(shape), one],
        out_shape=[jax.ShapeDtypeStruct(shape, BF), jax.ShapeDtypeStruct((length, width), F32)],
        scratch_shapes=[pltpu.VMEM((width, length), BF)],
        compiler_params=params(),
        cost_estimate=cost(11),
        name="project_back",
    )(x, gq, gk, gv, grel, sine_t, w, gh1)


def swap_x(value):
    return lax.ppermute(value, "mp", [(0, 1), (1, 0)])


def swap_dp(value, bit):
    return lax.ppermute(value, "dp", [(d, d ^ bit) for d in range(lax.axis_size("dp"))])


def shift_line(value, step):
    dp = lax.axis_size("dp")
    return lax.ppermute(value, "dp", [(d, (d + 4 * step) % dp) for d in range(dp)])


def gather_matrices(shard):
    pieces = lax.all_gather(shard, ("mp", "dp"), axis=0, tiled=False)
    pieces = pieces.reshape((2, lax.axis_size("dp")) + shard.shape)
    if shard.shape[1] % 16 == 0:
        return pieces
    return whole_matrices(pieces)


def whole_matrices(pieces):
    mp, dp, blocks, rows, columns = pieces.shape
    return pieces.transpose(2, 0, 1, 3, 4).reshape(blocks, mp, dp * rows, columns)


def place_kernel(lines, place_ref, *refs):
    parts, out_ref, sem = refs[:-2], refs[-2], refs[-1]
    mp, line, y, core = (place_ref[i] for i in range(4))
    rows = parts[0].shape[2]
    copies = []
    for index, part in enumerate(parts):
        top, dx, dy, dc = PARTS[index]
        first = 0 if top == 0 else out_ref.shape[0] - part.shape[1]
        for step in range(lines):
            at = lax.rem(line + lines - step, lines) * 4 + (y ^ dy) * 2 + (core ^ dc)
            start = pl.multiple_of(at * rows, rows)
            copies.append(
                pltpu.make_async_copy(
                    part.at[step],
                    out_ref.at[pl.ds(first, part.shape[1]), mp ^ dx, pl.ds(start, rows)],
                    sem.at[len(copies)],
                )
            )
    for copy in copies:
        copy.start()
    for copy in copies:
        copy.wait()


PARTS = [
    (half, dx, dy, dc)
    for dc in (0, 1)
    for half, dx, dy in (
        (0, 0, 0), (1, 0, 0), (0, 1, 0), (1, 0, 1), (0, 0, 1), (1, 1, 0), (0, 1, 1), (1, 1, 1),
    )
]


def gather_stepwise(shard):
    dp = lax.axis_size("dp")
    blocks, rows, columns = shard.shape
    lines = dp // 4
    if lines != 4 or rows % 16 != 0:
        return gather_matrices(shard)
    near = jnp.stack([shard] + [shift_line(shard, step) for step in range(1, lines)])
    cut = blocks // 2
    one, two = near[:, :cut], near[:, cut:]
    one_x = swap_x(one)
    two_y = swap_dp(two, 2)
    one_y = swap_dp(one, 2)
    two_x = swap_x(two)
    one_xy = swap_dp(one_x, 2)
    two_xy = swap_x(two_y)
    lane = [one, two, one_x, two_y, one_y, two_x, one_xy, two_xy]
    parts = lane + [swap_dp(part, 1) for part in lane]
    index = lax.axis_index("dp")
    place = jnp.stack([lax.axis_index("mp"), index // 4, (index // 2) % 2, index % 2])
    anywhere = pl.BlockSpec(memory_space=pl.ANY)
    return pl.pallas_call(
        functools.partial(place_kernel, lines),
        in_specs=[pl.BlockSpec(memory_space=pltpu.SMEM)] + [anywhere] * len(parts),
        out_specs=pl.BlockSpec(memory_space=pltpu.VMEM),
        out_shape=jax.ShapeDtypeStruct((blocks, 2, dp * rows, columns), BF),
        scratch_shapes=[pltpu.SemaphoreType.DMA((len(parts) * lines,))],
        compiler_params=params(),
        cost_estimate=cost(5),
        name="place",
    )(place.astype(jnp.int32), *parts)


def plane_groups(dp):
    return [
        [mp * dp + line * 4 + y * 2 + core for mp, y, core in RING] for line in range(dp // 4)
    ]


def line_groups(dp):
    return [
        [mp * dp + line * 4 + low for line in range(dp // 4)] for mp in range(2) for low in range(4)
    ]


def scatter_plane(grads):
    dp = lax.axis_size("dp")
    if grads.ndim == 4:
        blocks, _, all_rows, columns = grads.shape
        grads = grads.reshape(blocks, 2, dp // 4, 2, 2, all_rows // dp, columns)
        grads = jnp.stack([grads[:, mp, :, y, core] for mp, y, core in RING])
        grads = grads.transpose(0, 2, 1, 3, 4)
    return lax.psum_scatter(
        grads, ("mp", "dp"), scatter_dimension=0, axis_index_groups=plane_groups(dp), tiled=False
    )


def scatter_line(part):
    dp = lax.axis_size("dp")
    lines = dp // 4
    if lines != 4:
        return lax.psum_scatter(
            part, ("mp", "dp"), scatter_dimension=0, axis_index_groups=line_groups(dp), tiled=False
        ).astype(F32)
    line = lax.axis_index("dp") // 4
    pick = lambda step: lax.dynamic_index_in_dim(part, (line + step) % lines, 0, keepdims=False)
    received = [shift_line(pick(step), step) for step in range(1, lines)]
    total = pick(0).astype(F32)
    for piece in received:
        total = total + piece.astype(F32)
    return total


def sum_small(value):
    value = value + swap_dp(value, 1)
    value = value + swap_x(value)
    value = value + swap_dp(value, 2)
    lines = lax.axis_size("dp") // 4
    if lines != 4:
        return lax.psum(value, ("dp",), axis_index_groups=line_only(lines))
    total = value
    for piece in [shift_line(value, step) for step in range(1, lines)]:
        total = total + piece
    return total


def line_only(lines):
    return [[line * 4 + low for line in range(lines)] for low in range(4)]


def adam_kernel(g_ref, p_ref, one_ref, two_ref, *refs):
    outs = refs[-3:]
    results = adam_update(p_ref[...], g_ref[...], one_ref[...], two_ref[...], RATE_BIG)
    for out, result in zip(outs, results):
        out[...] = result


def adam_blocks(grad, first, param, one, two, held):
    blocks, rows, columns = grad.shape
    step = 4
    part = pl.BlockSpec((step, rows, columns), lambda b: (b + first // step, 0, 0))
    anywhere = pl.BlockSpec(memory_space=pl.ANY)
    shape = jax.ShapeDtypeStruct(param.shape, F32)
    return pl.pallas_call(
        adam_kernel,
        grid=(pl.cdiv(blocks, step),),
        in_specs=[pl.BlockSpec((step, rows, columns), lambda b: (b, 0, 0)), part, part, part]
        + [anywhere] * len(held),
        out_specs=[part] * 3,
        out_shape=[shape] * 3,
        input_output_aliases={4 + i: i for i in range(len(held))},
        compiler_params=params(),
        cost_estimate=cost(blocks // 2),
        name="adam",
    )(grad, param, one, two, *held)


def per_device(
    tokens,
    lengths,
    weights,
    weight_m1,
    weight_m2,
    head_vecs,
    head_m1,
    head_m2,
    norm_vecs,
    norm_m1,
    norm_m2,
    cotangent,
):
    mp_index = lax.axis_index("mp")
    seq_len = cotangent.shape[0]
    weight_rows = weights.shape[0]
    local_width = weights.shape[2]
    model_width = tokens.shape[1]
    lines = lax.axis_size("dp") // 4
    x = lax.dynamic_slice_in_dim(tokens, mp_index * seq_len, seq_len, 0)
    used = lax.dynamic_slice_in_dim(lengths, mp_index, 1, 0)
    sine = relative_embedding(seq_len, model_width).astype(BF)
    shard = weights.transpose(1, 0, 2)
    shard_low = shard.astype(BF)
    w_feed = gather_matrices(shard_low[5:13])
    w = gather_stepwise(shard_low[0:5])
    heads_all = lax.all_gather(head_vecs, "mp", axis=1, tiled=True)

    qc, qp, k, v, rel = project(x, w, heads_all[0:2], sine)
    probs, mixed = attend(used, qc, qp, k, v, rel)
    hb = heads_all[2:6].reshape(4, 1, model_width)
    unit, inv, low, active, slope, out, gh2, gffn, sums2 = feed(
        mixed, w, x, norm_vecs, hb, w_feed, cotangent
    )
    gw_back = back_grad(gffn, active, lines, weight_rows)
    part_back = scatter_plane(gw_back)
    gffn, _ = lax.optimization_barrier((gffn, gw_back))
    gw_in, hsum, gh1, gmixed, sums1 = feed_back(
        gffn, slope, low, w_feed, gh2, unit, inv, norm_vecs, w, mixed, lines, weight_rows
    )
    gw_in, part_back = lax.optimization_barrier((gw_in, part_back))
    part_in = scatter_plane(gw_in)
    gq, gk, gv, grel, sums_q = attend_back(probs, gmixed, qc, qp, k, v, rel)
    line_back = scatter_line(part_back)
    gq, line_back = lax.optimization_barrier((gq, line_back))
    gproj, grad_tokens = project_back(
        x, gq, gk, gv, grel, sine.T, w, gh1, lines, weight_rows
    )
    gproj, part_in = lax.optimization_barrier((gproj, part_in))
    part_proj = scatter_plane(gproj)

    norm_part = jnp.concatenate([sums1[0:2], sums2[0:2], sums1[2:3], sums2[2:3]], axis=0)
    head_part = jnp.concatenate([sums_q[0:2], hsum[:, 0]], axis=0)
    small = jnp.concatenate([norm_part, head_part], axis=0)
    small = sum_small(small)
    norm_grad = small[0:6]
    head_grad = lax.dynamic_slice_in_dim(small[6:12], mp_index * local_width, local_width, 1)
    state = (shard, weight_m1.transpose(1, 0, 2), weight_m2.transpose(1, 0, 2))
    line_in = scatter_line(part_in)
    early = jnp.concatenate([line_in[4:5], line_in[0:4], line_back], axis=0)
    held = adam_blocks(early, 4, *state, ())
    new_big = adam_blocks(scatter_line(part_proj), 0, *state, held)
    new_weights, new_weight_m1, new_weight_m2 = [a.transpose(1, 0, 2) for a in new_big]
    new_head, new_head_m1, new_head_m2 = adam_update(
        head_vecs, head_grad, head_m1, head_m2, RATE_SMALL
    )
    new_norm, new_norm_m1, new_norm_m2 = adam_update(
        norm_vecs, norm_grad, norm_m1, norm_m2, RATE_SMALL
    )
    return (
        out,
        grad_tokens,
        new_weights,
        new_weight_m1,
        new_weight_m2,
        new_head,
        new_head_m1,
        new_head_m2,
        new_norm,
        new_norm_m1,
        new_norm_m2,
    )


def solution(mesh):
    shard = P("dp", None, "mp")
    return jax.shard_map(
        per_device,
        mesh=mesh,
        in_specs=(P("dp", None), P("dp"), shard, shard, shard)
        + (P(None, "mp"),) * 3
        + (P(),) * 3
        + (P(("dp", "mp"), None),),
        out_specs=(P(("dp", "mp"), None),) * 2
        + (shard,) * 3
        + (P(None, "mp"),) * 3
        + (P(),) * 3,
        check_vma=False,
    )
```

```python
import functools

import jax
import jax.numpy as jnp
from jax import lax
from jax.experimental import pallas as pl
from jax.experimental.pallas import tpu as pltpu
from jax.sharding import PartitionSpec as P

HEAD_FEATURES = 64
STEP = 5
EPS_NORM = 1e-05
EPS_ADAM = 1e-08
BETA_ONE = 0.5
BETA_TWO = 0.5
RATE_BIG = 0.03
RATE_SMALL = 0.2
DECAY = 0.01
MASKED = -1e30
SCALE = HEAD_FEATURES ** (-0.5)
ROW_BLOCK = 256
VMEM_MB = 56
BF = jnp.bfloat16
F32 = jnp.float32

NN = (((1,), (0,)), ((), ()))
NT = (((1,), (1,)), ((), ()))
TN = (((0,), (0,)), ((), ()))


def mm(a, b, dims=NN):
    return lax.dot_general(a, b, dims, preferred_element_type=F32)


def whole(shape):
    return pl.BlockSpec(shape, lambda *_: (0,) * len(shape))


def held(shape):
    return pl.BlockSpec(shape, lambda *_: (0,) * len(shape), pipeline_mode=pl.Buffered(1))


def params(mebibytes):
    return pltpu.CompilerParams(vmem_limit_bytes=mebibytes * 1024 * 1024)


def cost(micros):
    return pl.CostEstimate(flops=int(micros * 1e9), bytes_accessed=0, transcendentals=0)


def relative_embedding(length, model_width):
    distance = (length - 1 - jnp.arange(2 * length)).astype(F32)
    freq_index = jnp.arange(model_width // 2).astype(F32)
    inverse = 1.0 / 10000.0 ** (2.0 * freq_index / model_width)
    angles = distance[:, None] * inverse[None, :]
    return jnp.concatenate([jnp.sin(angles), jnp.cos(angles)], axis=1)


def adam_update(param, grad_sum, moment_one, moment_two, rate):
    new_one = BETA_ONE * moment_one + (1.0 - BETA_ONE) * grad_sum
    new_two = BETA_TWO * moment_two + (1.0 - BETA_TWO) * grad_sum * grad_sum
    corrected_one = new_one / (1.0 - BETA_ONE**STEP)
    corrected_two = new_two / (1.0 - BETA_TWO**STEP)
    new_param = param - rate * (
        corrected_one / (jnp.sqrt(corrected_two) + EPS_ADAM) + DECAY * param
    )
    return (new_param, new_one, new_two)


def weight_spec(shape, which):
    if shape[1] != 2:
        return pl.BlockSpec((shape[0], None) + shape[2:], lambda b: (0, which(b), 0, 0))
    return pl.BlockSpec((None,) + shape[1:], lambda b: (which(b), 0, 0, 0))


def ring_order(lines):
    order = []
    for turn, (mp, y) in enumerate(((0, 0), (0, 1), (1, 1), (1, 0))):
        for line in range(lines) if turn % 2 == 0 else reversed(range(lines)):
            order += [(mp, line * 4 + y * 2), (mp, line * 4 + y * 2 + 1)]
    return order


def full_matrix(w_ref):
    if len(w_ref.shape) == 3 and w_ref.shape[0] > 2:
        places = w_ref.shape[0]
        order = ring_order(places // 8)
        sides = [
            jnp.concatenate([w_ref[order.index((mp, dp))] for dp in range(places // 2)], axis=0)
            for mp in range(2)
        ]
        return jnp.concatenate(sides, axis=1)
    return jnp.concatenate([w_ref[0], w_ref[1]], axis=1)


RING = ((0, 0, 0), (0, 0, 1), (0, 1, 1), (0, 1, 0), (1, 1, 0), (1, 1, 1), (1, 0, 1), (1, 0, 0))


def layered(lines, rows):
    return rows % 16 == 0


def grad_shape(blocks, lines, rows, columns):
    if layered(lines, rows):
        return (len(RING), lines, blocks, rows, columns)
    return (blocks, 2, lines * 4 * rows, columns)


def grad_spec(shape):
    if len(shape) == 5:
        return pl.BlockSpec(shape[:2] + (None,) + shape[3:], lambda b: (0, 0, b, 0, 0))
    return pl.BlockSpec((None,) + shape[1:], lambda b: (b, 0, 0, 0))


def store_matrix(out_ref, value):
    half = value.shape[1] // 2
    low = value.astype(BF)
    if len(out_ref.shape) == 3:
        out_ref[0] = low[:, :half]
        out_ref[1] = low[:, half:]
        return
    places, lines, rows, _ = out_ref.shape
    for place, (mp, y, core) in enumerate(RING):
        for line in range(lines):
            top = (line * 4 + y * 2 + core) * rows
            out_ref[place, line] = low[top : top + rows, mp * half : (mp + 1) * half]


def project_kernel(x_ref, w_ref, vec_ref, sine_ref, qc_ref, qp_ref, k_ref, v_ref, rel_ref):
    step = pl.program_id(0)

    @pl.when(step == 0)
    def _():
        q = mm(x_ref[...], full_matrix(w_ref))
        qc_ref[...] = (q + vec_ref[0:1]).astype(BF) * BF(SCALE)
        qp_ref[...] = (q + vec_ref[1:2]).astype(BF) * BF(SCALE)

    @pl.when(step == 1)
    def _():
        k_ref[...] = mm(x_ref[...], full_matrix(w_ref)).astype(BF)

    @pl.when(step == 2)
    def _():
        v_ref[...] = mm(x_ref[...], full_matrix(w_ref)).astype(BF)

    @pl.when(step == 3)
    def _():
        rel_ref[...] = mm(sine_ref[...], full_matrix(w_ref)).astype(BF)


def project(x, w, vecs, sine):
    length, width = x.shape
    rows = sine.shape[0]
    shapes = [(length, width)] * 4 + [(rows, width)]
    return pl.pallas_call(
        project_kernel,
        grid=(4,),
        in_specs=[
            whole(x.shape),
            weight_spec(w.shape, lambda b: b),
            whole(vecs.shape),
            whole(sine.shape),
        ],
        out_specs=[whole(s) for s in shapes],
        out_shape=[jax.ShapeDtypeStruct(s, BF) for s in shapes],
        compiler_params=params(VMEM_MB),
        cost_estimate=cost(9),
        name="project",
    )(x, w, vecs, sine)


def lane_mask(which, shape):
    lanes = lax.broadcasted_iota(jnp.int32, shape, 1)
    return (lanes >= HEAD_FEATURES) if which else (lanes < HEAD_FEATURES)


def attend_kernel(len_ref, qc_ref, qp_ref, k_ref, v_ref, rel_ref, probs_ref, mixed_ref):
    length = qc_ref.shape[0]
    block = ROW_BLOCK
    pair = qc_ref.shape[1]
    valid = lax.broadcasted_iota(jnp.int32, (1, length), 1) < len_ref[0]
    k = k_ref[...]
    v = v_ref[...]
    zero = jnp.zeros((), BF)
    for top in range(0, length, block):
        rows = pl.ds(top, block)
        first = length - block - top
        span = length + block
        rel = rel_ref[first : first + span, :]
        total = None
        for head in range(2):
            mask = lane_mask(head, (block, pair))
            content = mm(jnp.where(mask, qc_ref[rows, :], zero), k, NT)
            place = mm(jnp.where(mask, qp_ref[rows, :], zero), rel, NT)
            place = pltpu.roll(place, span - (block - 1), 1, stride=1, stride_axis=0)
            scores = jnp.where(valid, content + place[:, :length], MASKED)
            top_score = jnp.max(scores, axis=1, keepdims=True)
            grown = jnp.exp(scores - top_score)
            probs = grown * (1.0 / jnp.sum(grown, axis=1, keepdims=True))
            probs_low = probs.astype(BF)
            probs_ref[head, rows, :] = probs_low
            part = jnp.where(mask, mm(probs_low, v), 0.0)
            total = part if total is None else total + part
        mixed_ref[rows, :] = total.astype(BF)


def attend(length_used, qc, qp, k, v, rel):
    length, width = qc.shape
    pair = 2 * HEAD_FEATURES
    heads = width // HEAD_FEATURES
    column = pl.BlockSpec((length, pair), lambda p: (0, p))
    return pl.pallas_call(
        attend_kernel,
        grid=(heads // 2,),
        in_specs=[pl.BlockSpec(memory_space=pltpu.SMEM)]
        + [column] * 4
        + [pl.BlockSpec((rel.shape[0], pair), lambda p: (0, p))],
        out_specs=[pl.BlockSpec((2, length, length), lambda p: (p, 0, 0)), column],
        out_shape=[
            jax.ShapeDtypeStruct((heads, length, length), BF),
            jax.ShapeDtypeStruct((length, width), BF),
        ],
        compiler_params=params(VMEM_MB),
        cost_estimate=cost(19),
        name="attend",
    )(length_used, qc, qp, k, v, rel)


def norm_parts(rows):
    mean = jnp.mean(rows, axis=1, keepdims=True)
    centred = rows - mean
    spread = jnp.mean(centred * centred, axis=1, keepdims=True)
    inverse = lax.rsqrt(spread + EPS_NORM)
    return centred * inverse, inverse


def norm_back(unit, inverse, scaled):
    return (
        scaled
        - jnp.mean(scaled, axis=1, keepdims=True)
        - unit * jnp.mean(scaled * unit, axis=1, keepdims=True)
    ) * inverse


def mlp_kernel(
    mixed_ref, wo_ref, x_ref, nv_ref, hb_ref, win_ref, wback_ref, cot_ref,
    out_ref, unit_ref, inv_ref, gfirst_ref, gw_ref, hsum_ref, sums_ref,
    wide_ref, first_ref, low_ref, turned_ref, act_ref, slope_ref, gffn_ref, gturned_ref, ghid_ref,
):
    step = pl.program_id(0)
    blocks = pl.num_programs(0) // 2
    length = x_ref.shape[0]

    @pl.when(step == 0)
    def _():
        wide_ref[...] = mm(mixed_ref[...], full_matrix(wo_ref), NT)

        def rows_in(rows):
            h1 = x_ref[rows, :].astype(F32) + wide_ref[rows, :] + nv_ref[4:5]
            unit, inverse = norm_parts(h1)
            unit_ref[rows, :] = unit
            inv_ref[rows, :] = jnp.broadcast_to(inverse, (unit.shape[0], inv_ref.shape[1]))
            first = unit * nv_ref[0:1] + nv_ref[1:2]
            first_ref[rows, :] = first + nv_ref[5:6]
            low_ref[rows, :] = first.astype(BF)

        rows_in(slice(None))
        turned_ref[...] = low_ref[...].T

    @pl.when(step < blocks)
    def _():
        wide_ref[...] = mm(low_ref[...], full_matrix(win_ref))

        def rows_gelu(rows):
            hidden = wide_ref[rows, :] + hb_ref[0]
            bell = 0.5 * (1.0 + lax.erf(hidden * 0.7071067811865476))
            act_ref[step, rows, :] = (hidden * bell).astype(BF)
            slope_ref[step, rows, :] = (
                bell + hidden * (jnp.exp(hidden * hidden * -0.5) * 0.3989422804014327)
            ).astype(BF)

        rows_gelu(slice(None))
        first_ref[...] += mm(act_ref[step], full_matrix(wback_ref), NT)

    @pl.when(step == blocks - 1)
    def _():
        def rows_out(rows):
            unit, inverse = norm_parts(first_ref[rows, :])
            out_ref[rows, :] = (unit * nv_ref[2:3] + nv_ref[3:4]).astype(BF)
            cot = cot_ref[rows, :].astype(F32)
            gh2 = norm_back(unit, inverse, cot * nv_ref[2:3])
            gfirst_ref[rows, :] = gh2
            gffn_ref[rows, :] = gh2.astype(BF)
            wide_ref[rows, :] = cot * unit

        rows_out(slice(None))
        gturned_ref[...] = gffn_ref[...].T
        sums_ref[0:1] = jnp.sum(wide_ref[...], axis=0, keepdims=True)
        sums_ref[1:2] = jnp.sum(cot_ref[...].astype(F32), axis=0, keepdims=True)
        sums_ref[2:3] = jnp.sum(gfirst_ref[...], axis=0, keepdims=True)
        sums_ref[3:8] = jnp.zeros((5, sums_ref.shape[1]), F32)

    @pl.when(step >= blocks)
    def _():
        block = step - blocks
        pick = lambda i: gw_ref.at[:, :, i] if len(gw_ref.shape) == 5 else gw_ref.at[i]
        store_matrix(pick(1), mm(gturned_ref[...], act_ref[block]))
        wide_ref[...] = mm(gffn_ref[...], full_matrix(wback_ref))

        def rows_slope(rows):
            ghid_ref[rows, :] = (wide_ref[rows, :] * slope_ref[block, rows, :].astype(F32)).astype(BF)

        rows_slope(slice(None))
        hsum_ref[0] = jnp.sum(ghid_ref[...].astype(F32), axis=0, keepdims=True)
        store_matrix(pick(0), mm(turned_ref[...], ghid_ref[...]))
        gfirst_ref[...] += mm(ghid_ref[...], full_matrix(win_ref), NT)


def mlp(mixed, w_feed, x, nv, hb, cot, lines, rows):
    length, width = x.shape
    blocks = hb.shape[0]
    one = whole((length, width))
    token = lambda d: jax.ShapeDtypeStruct((length, width), d)
    full = grad_shape(2 * blocks, lines, rows, width // 2)
    if len(full) == 5:
        spec = pl.BlockSpec(
            full[:2] + (2,) + full[3:], lambda b: (0, 0, jnp.maximum(b - blocks, 0), 0, 0)
        )
    else:
        spec = pl.BlockSpec((2,) + full[1:], lambda b: (jnp.maximum(b - blocks, 0), 0, 0, 0))
    buffer = lambda d: pltpu.VMEM((length, width), d)
    return pl.pallas_call(
        mlp_kernel,
        grid=(2 * blocks,),
        in_specs=[
            held((length, width)),
            weight_spec(w_feed.shape, lambda b: 0),
            held((length, width)),
            whole(nv.shape),
            pl.BlockSpec((1, 1, width), lambda b: (jnp.minimum(b, blocks - 1), 0, 0)),
            weight_spec(w_feed.shape, lambda b: 1 + lax.rem(b, blocks)),
            weight_spec(w_feed.shape, lambda b: 1 + blocks + lax.rem(b, blocks)),
            held((length, width)),
        ],
        out_specs=[
            one, one, whole((length, 128)), one, spec,
            pl.BlockSpec((1, 1, width), lambda b: (jnp.maximum(b - blocks, 0), 0, 0)),
            whole((8, width)),
        ],
        out_shape=[
            token(BF), token(F32), jax.ShapeDtypeStruct((length, 128), F32), token(F32),
            jax.ShapeDtypeStruct(full, BF),
            jax.ShapeDtypeStruct((blocks, 1, width), F32),
            jax.ShapeDtypeStruct((8, width), F32),
        ],
        scratch_shapes=[
            buffer(F32), buffer(F32), buffer(BF), pltpu.VMEM((width, length), BF),
            pltpu.VMEM((blocks, length, width), BF), pltpu.VMEM((blocks, length, width), BF),
            buffer(BF), pltpu.VMEM((width, length), BF), buffer(BF),
        ],
        compiler_params=params(VMEM_MB),
        cost_estimate=cost(30),
        name="mlp",
    )(mixed, w_feed, x, nv, hb, w_feed, w_feed, cot)


def norm_down_kernel(
    gfirst_ref, unit_ref, inv_ref, nv_ref, wo_ref, gh1_ref, gattn_ref, gmixed_ref, sums_ref, prod_ref
):
    def rows_back(rows):
        gfirst = gfirst_ref[rows, :]
        unit = unit_ref[rows, :]
        gh1 = norm_back(unit, inv_ref[rows, 0:1], gfirst * nv_ref[0:1])
        gh1_ref[rows, :] = gh1
        gattn_ref[rows, :] = gh1.astype(BF)
        prod_ref[rows, :] = gfirst * unit

    rows_back(slice(None))
    gmixed_ref[...] = mm(gattn_ref[...], full_matrix(wo_ref)).astype(BF)
    sums_ref[0:1] = jnp.sum(prod_ref[...], axis=0, keepdims=True)
    sums_ref[1:2] = jnp.sum(gfirst_ref[...], axis=0, keepdims=True)
    sums_ref[2:3] = jnp.sum(gh1_ref[...], axis=0, keepdims=True)
    sums_ref[3:8] = jnp.zeros((5, sums_ref.shape[1]), F32)


def norm_down(gfirst, unit, inv, nv, w_feed):
    length, width = gfirst.shape
    one = whole((length, width))
    token = lambda d: jax.ShapeDtypeStruct((length, width), d)
    return pl.pallas_call(
        norm_down_kernel,
        grid=(1,),
        in_specs=[one, one, whole(inv.shape), whole(nv.shape), weight_spec(w_feed.shape, lambda b: 0)],
        out_specs=[one, one, one, whole((8, width))],
        out_shape=[token(F32), token(BF), token(BF), jax.ShapeDtypeStruct((8, width), F32)],
        scratch_shapes=[pltpu.VMEM((length, width), F32)],
        compiler_params=params(VMEM_MB),
        cost_estimate=cost(5),
        name="norm_down",
    )(gfirst, unit, inv, nv, w_feed)


def attend_back_kernel(
    probs_ref, gm_ref, qc_ref, qp_ref, k_ref, v_ref, rel_ref,
    gq_ref, gk_ref, gv_ref, grel_ref, sums_ref,
    rel_acc,
):
    length, pair = gm_ref.shape
    block = ROW_BLOCK
    span = length + block
    zero = jnp.zeros((), BF)
    flip = (
        lax.broadcasted_iota(jnp.int32, (block, block), 0)
        + lax.broadcasted_iota(jnp.int32, (block, block), 1)
        == block - 1
    ).astype(F32).astype(BF)
    k = k_ref[...]
    v = v_ref[...]
    rel_acc[...] = jnp.zeros_like(rel_acc)
    gk = None
    gv = None
    sum_c = None
    sum_p = None
    for top in range(0, length, block):
        rows = pl.ds(top, block)
        first = length - block - top
        band = pl.ds(first, span)
        rel = rel_ref[band, :]
        qp_turned = mm(flip, qp_ref[rows, :]).astype(BF)
        gqc = None
        gqp = None
        for head in range(2):
            mask = lane_mask(head, (block, pair))
            tall = lane_mask(head, (length, pair))
            probs_low = probs_ref[head, rows, :]
            probs = probs_low.astype(F32)
            gm = jnp.where(mask, gm_ref[rows, :], zero)
            gprobs = mm(gm, v, NT)
            product = probs * gprobs
            inner = jnp.sum(product, axis=1, keepdims=True)
            gsum = (product - probs * inner).astype(BF)
            a = mm(gsum, jnp.where(tall, k, zero))
            gqc = a if gqc is None else gqc + a
            b = mm(gsum, jnp.where(mask, qc_ref[rows, :], zero), TN)
            gk = b if gk is None else gk + b
            c = mm(probs_low, gm, TN)
            gv = c if gv is None else gv + c
            turned = mm(flip, gsum)
            wide = jnp.concatenate([turned, jnp.zeros((block, block), F32)], axis=1)
            wide = pltpu.roll(wide, 0, 1, stride=1, stride_axis=0).astype(BF)
            rel_mask = lane_mask(head, (span, pair))
            d = mm(wide, jnp.where(rel_mask, rel, zero))
            gqp = d if gqp is None else gqp + d
            rel_acc[band, :] += mm(wide, jnp.where(mask, qp_turned, zero), TN)
        gqc = gqc * SCALE
        gqp = gqp * SCALE
        high = gqp.astype(BF)
        rest = (gqp - high.astype(F32)).astype(BF)
        straight = mm(flip, high) + mm(flip, rest)
        gq_ref[rows, :] = (gqc + straight).astype(BF)
        e = jnp.sum(gqc, axis=0, keepdims=True)
        f = jnp.sum(gqp, axis=0, keepdims=True)
        sum_c = e if sum_c is None else sum_c + e
        sum_p = f if sum_p is None else sum_p + f
    gk_ref[...] = gk.astype(BF)
    gv_ref[...] = gv.astype(BF)
    grel_ref[...] = rel_acc[...].astype(BF)
    sums_ref[0:1] = sum_c
    sums_ref[1:2] = sum_p
    sums_ref[2:8] = jnp.zeros((6, pair), F32)


def attend_back(probs, gm, qc, qp, k, v, rel):
    length, width = qc.shape
    pair = 2 * HEAD_FEATURES
    heads = width // HEAD_FEATURES
    column = pl.BlockSpec((length, pair), lambda p: (0, p))
    tall = pl.BlockSpec((rel.shape[0], pair), lambda p: (0, p))
    token = jax.ShapeDtypeStruct((length, width), BF)
    return pl.pallas_call(
        attend_back_kernel,
        grid=(heads // 2,),
        in_specs=[pl.BlockSpec((2, length, length), lambda p: (p, 0, 0))] + [column] * 5 + [tall],
        out_specs=[column, column, column, tall, pl.BlockSpec((8, pair), lambda p: (0, p))],
        out_shape=[
            token, token, token,
            jax.ShapeDtypeStruct(rel.shape, BF),
            jax.ShapeDtypeStruct((8, width), F32),
        ],
        scratch_shapes=[pltpu.VMEM((rel.shape[0], pair), F32)],
        compiler_params=params(VMEM_MB),
        cost_estimate=cost(28),
        name="attend_back",
    )(probs, gm, qc, qp, k, v, rel)


def project_back_kernel(
    x_ref, gq_ref, gk_ref, gv_ref, grel_ref, sine_t_ref, gattn_ref, mixed_ref, w_ref, gh1_ref,
    gw_ref, gtok_ref,
    turned_ref,
):
    step = pl.program_id(0)

    @pl.when(step == 0)
    def _():
        turned_ref[...] = x_ref[...].T
        gtok_ref[...] = gh1_ref[...]

    for which, g_ref in enumerate((gq_ref, gk_ref, gv_ref)):

        @pl.when(step == which)
        def _():
            store_matrix(gw_ref, mm(turned_ref[...], g_ref[...]))
            gtok_ref[...] += mm(g_ref[...], full_matrix(w_ref), NT)

    @pl.when(step == 3)
    def _():
        store_matrix(gw_ref, mm(sine_t_ref[...], grel_ref[...]))

    @pl.when(step == 4)
    def _():
        store_matrix(gw_ref, mm(gattn_ref[...], mixed_ref[...], TN))


def project_back(x, gq, gk, gv, grel, sine_t, gattn, mixed, w, gh1, lines, rows):
    length, width = x.shape
    one = held((length, width))
    shape = grad_shape(5, lines, rows, width // 2)
    return pl.pallas_call(
        project_back_kernel,
        grid=(5,),
        in_specs=[
            one, one, one, one, held(grel.shape), held(sine_t.shape), one, one,
            weight_spec(w.shape, lambda b: jnp.minimum(b, 2)),
            one,
        ],
        out_specs=[grad_spec(shape), whole((length, width))],
        out_shape=[
            jax.ShapeDtypeStruct(shape, BF),
            jax.ShapeDtypeStruct((length, width), F32),
        ],
        scratch_shapes=[pltpu.VMEM((width, length), BF)],
        compiler_params=params(VMEM_MB),
        cost_estimate=cost(12),
        name="project_back",
    )(x, gq, gk, gv, grel, sine_t, gattn, mixed, w, gh1)


def swap_x(value):
    return lax.ppermute(value, "mp", [(0, 1), (1, 0)])


def swap_dp(value, bit):
    return lax.ppermute(value, "dp", [(d, d ^ bit) for d in range(lax.axis_size("dp"))])


def shift_line(value, step):
    dp = lax.axis_size("dp")
    return lax.ppermute(value, "dp", [(d, (d + 4 * step) % dp) for d in range(dp)])


def gather_matrices(shard):
    dp = lax.axis_size("dp")
    if shard.shape[1] % 16 == 0:
        order = [mp * dp + index for mp, index in ring_order(dp // 4)]
        return lax.all_gather(
            shard, ("mp", "dp"), axis=0, axis_index_groups=[order], tiled=False
        )
    pieces = lax.all_gather(shard, ("mp", "dp"), axis=0, tiled=False)
    return whole_matrices(pieces.reshape((2, dp) + shard.shape))


def whole_matrices(pieces):
    mp, dp, blocks, rows, columns = pieces.shape
    return pieces.transpose(2, 0, 1, 3, 4).reshape(blocks, mp, dp * rows, columns)


def place_kernel(lines, place_ref, *refs):
    parts, out_ref, sem = refs[:-2], refs[-2], refs[-1]
    mp, line, y, core = (place_ref[i] for i in range(4))
    rows = parts[0].shape[2]
    copies = []
    for index, part in enumerate(parts):
        top, dx, dy, dc = PARTS[index]
        first = 0 if top == 0 else out_ref.shape[0] - part.shape[1]
        for step in range(lines):
            at = lax.rem(line + lines - step, lines) * 4 + (y ^ dy) * 2 + (core ^ dc)
            start = pl.multiple_of(at * rows, rows)
            copies.append(
                pltpu.make_async_copy(
                    part.at[step],
                    out_ref.at[pl.ds(first, part.shape[1]), mp ^ dx, pl.ds(start, rows)],
                    sem.at[len(copies)],
                )
            )
    for copy in copies:
        copy.start()
    for copy in copies:
        copy.wait()


PARTS = [
    (half, dx, dy, dc)
    for dc in (0, 1)
    for half, dx, dy in (
        (0, 0, 0), (1, 0, 0), (0, 1, 0), (1, 0, 1), (0, 0, 1), (1, 1, 0), (0, 1, 1), (1, 1, 1),
    )
]


def gather_lines(shard, others):
    lines = lax.axis_size("dp") // 4
    if lines != 4 or shard.shape[1] % 16 != 0:
        return shard, others
    near = [shard] + [shift_line(shard, step) for step in range(1, lines)]
    near, others = lax.optimization_barrier((near, others))
    return jnp.stack(near), others


def gather_stepwise(near, shard):
    dp = lax.axis_size("dp")
    blocks, rows, columns = shard.shape
    lines = dp // 4
    if lines != 4 or rows % 16 != 0:
        pieces = lax.all_gather(shard, ("mp", "dp"), axis=0, tiled=False)
        return whole_matrices(pieces.reshape((2, dp) + shard.shape))
    cut = blocks // 2
    one, two = near[:, :cut], near[:, cut:]
    one_x = swap_x(one)
    two_y = swap_dp(two, 2)
    one_y = swap_dp(one, 2)
    two_x = swap_x(two)
    one_xy = swap_dp(one_x, 2)
    two_xy = swap_x(two_y)
    lane = [one, two, one_x, two_y, one_y, two_x, one_xy, two_xy]
    parts = lane + [swap_dp(part, 1) for part in lane]
    index = lax.axis_index("dp")
    place = jnp.stack([lax.axis_index("mp"), index // 4, (index // 2) % 2, index % 2])
    anywhere = pl.BlockSpec(memory_space=pl.ANY)
    return pl.pallas_call(
        functools.partial(place_kernel, lines),
        in_specs=[pl.BlockSpec(memory_space=pltpu.SMEM)] + [anywhere] * len(parts),
        out_specs=pl.BlockSpec(memory_space=pltpu.VMEM),
        out_shape=jax.ShapeDtypeStruct((blocks, 2, dp * rows, columns), BF),
        scratch_shapes=[pltpu.SemaphoreType.DMA((len(parts) * lines,))],
        compiler_params=params(VMEM_MB),
        cost_estimate=cost(5),
        name="place",
    )(place.astype(jnp.int32), *parts)


def plane_groups(dp):
    return [
        [mp * dp + line * 4 + y * 2 + core for mp, y, core in RING] for line in range(dp // 4)
    ]


def line_groups(dp):
    return [
        [mp * dp + line * 4 + low for line in range(dp // 4)] for mp in range(2) for low in range(4)
    ]


def scatter_plane(grads):
    dp = lax.axis_size("dp")
    if grads.ndim == 4:
        blocks, _, all_rows, columns = grads.shape
        grads = grads.reshape(blocks, 2, dp // 4, 2, 2, all_rows // dp, columns)
        grads = jnp.stack([grads[:, mp, :, y, core] for mp, y, core in RING])
        grads = grads.transpose(0, 2, 1, 3, 4)
    return lax.psum_scatter(
        grads, ("mp", "dp"), scatter_dimension=0, axis_index_groups=plane_groups(dp), tiled=False
    )


def scatter_line(part):
    dp = lax.axis_size("dp")
    lines = dp // 4
    if lines != 4:
        return lax.psum_scatter(
            part, ("mp", "dp"), scatter_dimension=0, axis_index_groups=line_groups(dp), tiled=False
        ).astype(F32)
    line = lax.axis_index("dp") // 4
    pick = lambda step: lax.dynamic_index_in_dim(part, (line + step) % lines, 0, keepdims=False)
    received = [shift_line(pick(step), step) for step in range(1, lines)]
    total = pick(0).astype(F32)
    for piece in received:
        total = total + piece.astype(F32)
    return total


def sum_small(value, meanwhile):
    value = value + swap_dp(value, 1)
    value = value + swap_x(value)
    value = value + swap_dp(value, 2)
    value, meanwhile = lax.optimization_barrier((value, meanwhile))
    return sum_line(value), meanwhile


def sum_line(value):
    lines = lax.axis_size("dp") // 4
    if lines != 4:
        return lax.psum(value, ("dp",), axis_index_groups=line_only(lines))
    total = value
    for piece in [shift_line(value, step) for step in range(1, lines)]:
        total = total + piece
    return total


def line_only(lines):
    return [[line * 4 + low for line in range(lines)] for low in range(4)]


def adam_kernel(order, g_ref, p_ref, one_ref, two_ref, *refs):
    outs = refs[-3:]
    for block, at in enumerate(order):
        results = adam_update(p_ref[at], g_ref[block], one_ref[at], two_ref[at], RATE_BIG)
        for out, result in zip(outs, results):
            out[at] = result


def adam_blocks(grad, order, param, one, two, done):
    blocks, rows, columns = grad.shape
    part = whole((blocks, rows, columns) if done else param.shape)
    shape = jax.ShapeDtypeStruct(param.shape, F32)
    return pl.pallas_call(
        functools.partial(adam_kernel, order),
        grid=(1,),
        in_specs=[whole(grad.shape), part, part, part]
        + [pl.BlockSpec(memory_space=pl.ANY)] * len(done),
        out_specs=[part] * 3,
        out_shape=[shape] * 3,
        input_output_aliases={4 + i: i for i in range(len(done))},
        compiler_params=params(VMEM_MB),
        cost_estimate=cost(blocks // 2),
        name="adam",
    )(grad, param, one, two, *done)


def per_device(
    tokens,
    lengths,
    weights,
    weight_m1,
    weight_m2,
    head_vecs,
    head_m1,
    head_m2,
    norm_vecs,
    norm_m1,
    norm_m2,
    cotangent,
):
    mp_index = lax.axis_index("mp")
    seq_len = cotangent.shape[0]
    weight_rows = weights.shape[0]
    local_width = weights.shape[2]
    model_width = tokens.shape[1]
    lines = lax.axis_size("dp") // 4
    x = lax.dynamic_slice_in_dim(tokens, mp_index * seq_len, seq_len, 0)
    used = lax.dynamic_slice_in_dim(lengths, mp_index, 1, 0)
    sine = relative_embedding(seq_len, model_width).astype(BF)
    shard = weights.transpose(1, 0, 2)
    shard_low = shard.astype(BF)
    heads_all = lax.all_gather(head_vecs, "mp", axis=1, tiled=True)
    near, (x, sine, sine_t, heads_all, shard_feed) = gather_lines(
        shard_low[0:4], (x, sine, sine.T, heads_all, shard_low[4:13])
    )
    w_feed = gather_matrices(shard_feed)
    w = gather_stepwise(near, shard_low[0:4])

    qc, qp, k, v, rel = project(x, w, heads_all[0:2], sine)
    probs, mixed = attend(used, qc, qp, k, v, rel)
    hb = heads_all[2:6].reshape(4, 1, model_width)
    out, unit, inv, gfirst, gw_feed, hsum, sums2 = mlp(
        mixed, w_feed, x, norm_vecs, hb, cotangent, lines, weight_rows
    )
    part_feed = scatter_plane(gw_feed)
    gh1, gattn, gmixed, sums1 = norm_down(gfirst, unit, inv, norm_vecs, w_feed)
    gq, gk, gv, grel, sums_q = attend_back(probs, gmixed, qc, qp, k, v, rel)
    gproj, grad_tokens = project_back(
        x, gq, gk, gv, grel, sine_t, gattn, mixed, w, gh1, lines, weight_rows
    )
    gproj, part_feed = lax.optimization_barrier((gproj, part_feed))
    part_proj = scatter_plane(gproj)

    norm_part = jnp.concatenate([sums1[0:2], sums2[0:2], sums1[2:3], sums2[2:3]], axis=0)
    head_part = jnp.concatenate([sums_q[0:2], hsum[:, 0]], axis=0)
    line_feed = scatter_line(part_feed)
    small = jnp.concatenate([norm_part, head_part], axis=0)
    small, line_feed = sum_small(small, line_feed)
    norm_grad = small[0:6]
    head_grad = lax.dynamic_slice_in_dim(small[6:12], mp_index * local_width, local_width, 1)
    state = (shard, weight_m1.transpose(1, 0, 2), weight_m2.transpose(1, 0, 2))
    held_big = adam_blocks(line_feed, (5, 9, 6, 10, 7, 11, 8, 12), *state, ())
    new_big = adam_blocks(scatter_line(part_proj), tuple(range(5)), *state, held_big)
    new_weights, new_weight_m1, new_weight_m2 = [a.transpose(1, 0, 2) for a in new_big]
    new_head, new_head_m1, new_head_m2 = adam_update(
        head_vecs, head_grad, head_m1, head_m2, RATE_SMALL
    )
    new_norm, new_norm_m1, new_norm_m2 = adam_update(
        norm_vecs, norm_grad, norm_m1, norm_m2, RATE_SMALL
    )
    return (
        out,
        grad_tokens,
        new_weights,
        new_weight_m1,
        new_weight_m2,
        new_head,
        new_head_m1,
        new_head_m2,
        new_norm,
        new_norm_m1,
        new_norm_m2,
    )


def solution(mesh):
    shard = P("dp", None, "mp")
    return jax.shard_map(
        per_device,
        mesh=mesh,
        in_specs=(P("dp", None), P("dp"), shard, shard, shard)
        + (P(None, "mp"),) * 3
        + (P(),) * 3
        + (P(("dp", "mp"), None),),
        out_specs=(P(("dp", "mp"), None),) * 2
        + (shard,) * 3
        + (P(None, "mp"),) * 3
        + (P(),) * 3,
        check_vma=False,
    )
```

```python
import functools

import jax
import jax.numpy as jnp
from jax import lax
from jax.experimental import pallas as pl
from jax.experimental.pallas import tpu as pltpu
from jax.sharding import PartitionSpec as P

HEAD_FEATURES = 64
STEP = 5
EPS_NORM = 1e-05
EPS_ADAM = 1e-08
BETA_ONE = 0.5
BETA_TWO = 0.5
RATE_BIG = 0.03
RATE_SMALL = 0.2
DECAY = 0.01
MASKED = -1e30
SCALE = HEAD_FEATURES ** (-0.5)
ROW_BLOCK = 256
VMEM_MB = 56
BF = jnp.bfloat16
F32 = jnp.float32

NN = (((1,), (0,)), ((), ()))
NT = (((1,), (1,)), ((), ()))
TN = (((0,), (0,)), ((), ()))


def mm(a, b, dims=NN):
    return lax.dot_general(a, b, dims, preferred_element_type=F32)


def whole(shape):
    return pl.BlockSpec(shape, lambda *_: (0,) * len(shape))


def held(shape):
    return pl.BlockSpec(shape, lambda *_: (0,) * len(shape), pipeline_mode=pl.Buffered(1))


def params(mebibytes):
    return pltpu.CompilerParams(vmem_limit_bytes=mebibytes * 1024 * 1024)


def cost(micros):
    return pl.CostEstimate(flops=int(micros * 1e9), bytes_accessed=0, transcendentals=0)


def relative_embedding(length, model_width):
    distance = (length - 1 - jnp.arange(2 * length)).astype(F32)
    freq_index = jnp.arange(model_width // 2).astype(F32)
    inverse = 1.0 / 10000.0 ** (2.0 * freq_index / model_width)
    angles = distance[:, None] * inverse[None, :]
    return jnp.concatenate([jnp.sin(angles), jnp.cos(angles)], axis=1)


def adam_update(param, grad_sum, moment_one, moment_two, rate):
    new_one = BETA_ONE * moment_one + (1.0 - BETA_ONE) * grad_sum
    new_two = BETA_TWO * moment_two + (1.0 - BETA_TWO) * grad_sum * grad_sum
    corrected_one = new_one / (1.0 - BETA_ONE**STEP)
    corrected_two = new_two / (1.0 - BETA_TWO**STEP)
    new_param = param - rate * (
        corrected_one / (jnp.sqrt(corrected_two) + EPS_ADAM) + DECAY * param
    )
    return (new_param, new_one, new_two)


def weight_spec(shape, which, each=None):
    if shape[1] != 2:
        return pl.BlockSpec((shape[0], each) + shape[2:], lambda b: (0, which(b), 0, 0))
    return pl.BlockSpec((each,) + shape[1:], lambda b: (which(b), 0, 0, 0))


def one_block(ref, index):
    if len(ref.shape) == 5:
        return ref.at[:, :, index]
    return ref.at[:, index] if ref.shape[0] > 8 else ref.at[index]


def ring_order(lines):
    order = []
    for turn, (mp, y) in enumerate(((0, 0), (0, 1), (1, 1), (1, 0))):
        for line in range(lines) if turn % 2 == 0 else reversed(range(lines)):
            order += [(mp, line * 4 + y * 2), (mp, line * 4 + y * 2 + 1)]
    return order


def full_matrix(w_ref):
    if len(w_ref.shape) == 3 and w_ref.shape[0] > 2:
        places = w_ref.shape[0]
        order = ring_order(places // 8)
        sides = [
            jnp.concatenate([w_ref[order.index((mp, dp))] for dp in range(places // 2)], axis=0)
            for mp in range(2)
        ]
        return jnp.concatenate(sides, axis=1)
    return jnp.concatenate([w_ref[0], w_ref[1]], axis=1)


RING = ((0, 0, 0), (0, 0, 1), (0, 1, 1), (0, 1, 0), (1, 1, 0), (1, 1, 1), (1, 0, 1), (1, 0, 0))


def layered(lines, rows):
    return rows % 16 == 0


def grad_shape(blocks, lines, rows, columns):
    if layered(lines, rows):
        return (len(RING), lines, blocks, rows, columns)
    return (blocks, 2, lines * 4 * rows, columns)


def grad_spec(shape):
    if len(shape) == 5:
        return pl.BlockSpec(shape[:2] + (None,) + shape[3:], lambda b: (0, 0, b, 0, 0))
    return pl.BlockSpec((None,) + shape[1:], lambda b: (b, 0, 0, 0))


def store_matrix(out_ref, value):
    half = value.shape[1] // 2
    low = value.astype(BF)
    if len(out_ref.shape) == 3:
        out_ref[0] = low[:, :half]
        out_ref[1] = low[:, half:]
        return
    places, lines, rows, _ = out_ref.shape
    for place, (mp, y, core) in enumerate(RING):
        for line in range(lines):
            top = (line * 4 + y * 2 + core) * rows
            out_ref[place, line] = low[top : top + rows, mp * half : (mp + 1) * half]


def project_kernel(x_ref, w_ref, vec_ref, sine_ref, qc_ref, qp_ref, k_ref, v_ref, rel_ref):
    step = pl.program_id(0)

    @pl.when(step == 0)
    def _():
        q = mm(x_ref[...], full_matrix(w_ref))
        qc_ref[...] = (q + vec_ref[0:1]).astype(BF) * BF(SCALE)
        qp_ref[...] = (q + vec_ref[1:2]).astype(BF) * BF(SCALE)

    @pl.when(step == 1)
    def _():
        k_ref[...] = mm(x_ref[...], full_matrix(w_ref)).astype(BF)

    @pl.when(step == 2)
    def _():
        v_ref[...] = mm(x_ref[...], full_matrix(w_ref)).astype(BF)

    @pl.when(step == 3)
    def _():
        rel_ref[...] = mm(sine_ref[...], full_matrix(w_ref)).astype(BF)


def project(x, w, vecs, sine):
    length, width = x.shape
    rows = sine.shape[0]
    shapes = [(length, width)] * 4 + [(rows, width)]
    return pl.pallas_call(
        project_kernel,
        grid=(4,),
        in_specs=[
            whole(x.shape),
            weight_spec(w.shape, lambda b: b),
            whole(vecs.shape),
            whole(sine.shape),
        ],
        out_specs=[whole(s) for s in shapes],
        out_shape=[jax.ShapeDtypeStruct(s, BF) for s in shapes],
        compiler_params=params(VMEM_MB),
        cost_estimate=cost(9),
        name="project",
    )(x, w, vecs, sine)


PARTS = [
    (half, dx, dy, dc)
    for dc in (0, 1)
    for half, dx, dy in (
        (0, 0, 0), (1, 0, 0), (0, 1, 0), (1, 0, 1), (0, 0, 1), (1, 1, 0), (0, 1, 1), (1, 1, 1),
    )
]


def project_parts_kernel(
    cut, place_ref, x_ref, vec_ref, sine_ref, *refs,
):
    parts = refs[: len(PARTS)]
    outs = refs[len(PARTS) : len(PARTS) + 6]
    buffers = refs[len(PARTS) + 6 : len(PARTS) + 12]
    in_sem, out_sem = refs[-2:]
    w_ref = buffers[5]
    mp, line, y, core = (place_ref[i] for i in range(4))
    lines, _, rows, _ = parts[0].shape
    arriving = ([], [])
    for index, (half, dx, dy, dc) in enumerate(PARTS):
        for step in range(lines):
            at = lax.rem(line + lines - step, lines) * 4 + (y ^ dy) * 2 + (core ^ dc)
            start = pl.multiple_of(at * rows, rows)
            arriving[half].append(
                pltpu.make_async_copy(
                    parts[index].at[step],
                    w_ref.at[pl.ds(half * cut, cut), mp ^ dx, pl.ds(start, rows)],
                    in_sem.at[index * lines + step],
                )
            )
    for copy in arriving[0] + arriving[1]:
        copy.start()
    leaving = []

    def leave(source, target):
        copy = pltpu.make_async_copy(source, target, out_sem.at[len(leaving)])
        copy.start()
        leaving.append(copy)

    for copy in arriving[0]:
        copy.wait()
    leave(w_ref.at[0:2], outs[5].at[0:2])
    q = mm(x_ref[...], full_matrix(w_ref.at[0]))
    buffers[0][...] = (q + vec_ref[0:1]).astype(BF) * BF(SCALE)
    leave(buffers[0], outs[0])
    buffers[1][...] = (q + vec_ref[1:2]).astype(BF) * BF(SCALE)
    leave(buffers[1], outs[1])
    buffers[2][...] = mm(x_ref[...], full_matrix(w_ref.at[1])).astype(BF)
    leave(buffers[2], outs[2])
    for copy in arriving[1]:
        copy.wait()
    leave(w_ref.at[2:3], outs[5].at[2:3])
    buffers[4][...] = mm(sine_ref[...], full_matrix(w_ref.at[3])).astype(BF)
    leave(buffers[4], outs[4])
    buffers[3][...] = mm(x_ref[...], full_matrix(w_ref.at[2])).astype(BF)
    leave(buffers[3], outs[3])
    for copy in leaving:
        copy.wait()


def project_parts(x, parts, vecs, sine, place):
    if len(parts) == 1:
        return [*project(x, parts[0], vecs, sine), parts[0]]
    length, width = x.shape
    lines, cut, rows, columns = parts[0].shape
    shapes = [(length, width)] * 4 + [sine.shape]
    matrix = (2, lines * 4 * rows, columns)
    anywhere = pl.BlockSpec(memory_space=pl.ANY)
    return pl.pallas_call(
        functools.partial(project_parts_kernel, cut),
        grid=(1,),
        in_specs=[
            pl.BlockSpec(memory_space=pltpu.SMEM), held(x.shape), held(vecs.shape), held(sine.shape),
        ]
        + [anywhere] * len(parts),
        out_specs=[anywhere] * 6,
        out_shape=[jax.ShapeDtypeStruct(shape, BF) for shape in shapes + [(3,) + matrix]],
        scratch_shapes=[pltpu.VMEM(shape, BF) for shape in shapes + [(4,) + matrix]]
        + [pltpu.SemaphoreType.DMA((len(parts) * lines,)), pltpu.SemaphoreType.DMA((7,))],
        compiler_params=params(VMEM_MB),
        cost_estimate=cost(9),
        name="project",
    )(place, x, vecs, sine, *parts)


def lane_mask(which, shape):
    lanes = lax.broadcasted_iota(jnp.int32, shape, 1)
    return (lanes >= HEAD_FEATURES) if which else (lanes < HEAD_FEATURES)


def attend_kernel(len_ref, qc_ref, qp_ref, k_ref, v_ref, rel_ref, probs_ref, mixed_ref):
    length = qc_ref.shape[0]
    block = ROW_BLOCK
    pair = qc_ref.shape[1]
    valid = lax.broadcasted_iota(jnp.int32, (1, length), 1) < len_ref[0]
    k = k_ref[...]
    v = v_ref[...]
    zero = jnp.zeros((), BF)
    span = length + block
    jobs = [(top, head) for top in range(0, length, block) for head in range(2)]
    raw = []
    for top, head in jobs:
        rows = pl.ds(top, block)
        first = length - block - top
        mask = lane_mask(head, (block, pair))
        content = mm(jnp.where(mask, qc_ref[rows, :], zero), k, NT)
        place = mm(jnp.where(mask, qp_ref[rows, :], zero), rel_ref[first : first + span, :], NT)
        raw.append((content, place))
    for (top, head), (content, place) in zip(jobs, raw):
        place = pltpu.roll(place, span - (block - 1), 1, stride=1, stride_axis=0)
        scores = jnp.where(valid, content + place[:, :length], MASKED)
        top_score = jnp.max(scores, axis=1, keepdims=True)
        grown = jnp.exp(scores - top_score)
        probs = grown * (1.0 / jnp.sum(grown, axis=1, keepdims=True))
        probs_ref[head, pl.ds(top, block), :] = probs.astype(BF)
    for top in range(0, length, block):
        rows = pl.ds(top, block)
        lower, upper = mm(probs_ref[0, rows, :], v), mm(probs_ref[1, rows, :], v)
        mixed_ref[rows, :] = jnp.where(lane_mask(1, (block, pair)), upper, lower).astype(BF)


def attend(length_used, qc, qp, k, v, rel):
    length, width = qc.shape
    pair = 2 * HEAD_FEATURES
    heads = width // HEAD_FEATURES
    column = pl.BlockSpec((length, pair), lambda p: (0, p))
    return pl.pallas_call(
        attend_kernel,
        grid=(heads // 2,),
        in_specs=[pl.BlockSpec(memory_space=pltpu.SMEM)]
        + [column] * 4
        + [pl.BlockSpec((rel.shape[0], pair), lambda p: (0, p))],
        out_specs=[pl.BlockSpec((2, length, length), lambda p: (p, 0, 0)), column],
        out_shape=[
            jax.ShapeDtypeStruct((heads, length, length), BF),
            jax.ShapeDtypeStruct((length, width), BF),
        ],
        compiler_params=params(VMEM_MB),
        cost_estimate=cost(19),
        name="attend",
    )(length_used, qc, qp, k, v, rel)


def norm_parts(rows):
    mean = jnp.mean(rows, axis=1, keepdims=True)
    centred = rows - mean
    spread = jnp.mean(centred * centred, axis=1, keepdims=True)
    inverse = lax.rsqrt(spread + EPS_NORM)
    return centred * inverse, inverse


def norm_back(unit, inverse, scaled):
    return (
        scaled
        - jnp.mean(scaled, axis=1, keepdims=True)
        - unit * jnp.mean(scaled * unit, axis=1, keepdims=True)
    ) * inverse


def mlp_kernel(
    blocks, nv_ref, hb_ref, mixed_hbm, x_hbm, cot_hbm, w_hbm,
    out_hbm, unit_hbm, inv_ref, gfirst_ref, gw_hbm, hsum_ref, sums_ref,
    mixed_ref, x_ref, cot_ref, w_ref, out_ref, unit_ref, gw_ref,
    low_ref, turned_ref, act_ref, slope_ref, gffn_ref, gturned_ref, ghid_ref, in_sem, out_sem,
):
    order = [2 * blocks] + [at for i in range(blocks) for at in (i, blocks + i)]
    gathered = len(w_hbm.shape) == 4 and w_hbm.shape[0] > 2 * blocks + 1
    coming = {}

    def come(name, source, target):
        coming[name] = pltpu.make_async_copy(source, target, in_sem.at[len(coming)])
        coming[name].start()

    def matrix(at):
        if at in coming:
            coming.pop(at).wait()
        return full_matrix(w_ref.at[at])

    going = []

    def go(source, target):
        going.append(pltpu.make_async_copy(source, target, out_sem.at[len(going)]))
        going[-1].start()

    come("mixed", mixed_hbm, mixed_ref)
    for number, at in enumerate(order):
        if number == 1:
            come("x", x_hbm, x_ref)
        come(at, w_hbm.at[:, at] if gathered else w_hbm.at[at], w_ref.at[at])
    come("cot", cot_hbm, cot_ref)

    coming.pop("mixed").wait()
    attn = mm(mixed_ref[...], matrix(2 * blocks), NT)
    coming.pop("x").wait()
    unit, inverse = norm_parts(x_ref[...].astype(F32) + attn + nv_ref[4:5])
    unit_ref[...] = unit
    go(unit_ref, unit_hbm)
    inv_ref[...] = jnp.broadcast_to(inverse, inv_ref.shape)
    total = unit * nv_ref[0:1] + nv_ref[1:2]
    low_ref[...] = total.astype(BF)
    turned_ref[...] = low_ref[...].T
    total = total + nv_ref[5:6]
    for i in range(blocks):
        hidden = mm(low_ref[...], matrix(i)) + hb_ref[i]
        bell = 0.5 * (1.0 + lax.erf(hidden * 0.7071067811865476))
        act_ref[i] = (hidden * bell).astype(BF)
        slope_ref[i] = (
            bell + hidden * (jnp.exp(hidden * hidden * -0.5) * 0.3989422804014327)
        ).astype(BF)
        total += mm(act_ref[i], matrix(blocks + i), NT)
    unit, inverse = norm_parts(total)
    out_ref[...] = (unit * nv_ref[2:3] + nv_ref[3:4]).astype(BF)
    go(out_ref, out_hbm)
    coming.pop("cot").wait()
    cot = cot_ref[...].astype(F32)
    total = norm_back(unit, inverse, cot * nv_ref[2:3])
    gffn_ref[...] = total.astype(BF)
    gturned_ref[...] = gffn_ref[...].T
    sums_ref[0:1] = jnp.sum(cot * unit, axis=0, keepdims=True)
    sums_ref[1:2] = jnp.sum(cot, axis=0, keepdims=True)
    sums_ref[2:3] = jnp.sum(total, axis=0, keepdims=True)
    sums_ref[3:8] = jnp.zeros((5, sums_ref.shape[1]), F32)
    for i in range(blocks):
        gact = mm(gffn_ref[...], matrix(blocks + i))
        store_matrix(gw_ref.at[2 * i + 1], mm(gturned_ref[...], act_ref[i]))
        go(gw_ref.at[2 * i + 1], one_block(gw_hbm, 2 * i + 1))
        ghid_ref[i] = (gact * slope_ref[i].astype(F32)).astype(BF)
        hsum_ref[i] = jnp.sum(ghid_ref[i].astype(F32), axis=0, keepdims=True)
        store_matrix(gw_ref.at[2 * i], mm(turned_ref[...], ghid_ref[i]))
        go(gw_ref.at[2 * i], one_block(gw_hbm, 2 * i))
        total += mm(ghid_ref[i], matrix(i), NT)
    gfirst_ref[...] = total
    for copy in going:
        copy.wait()


def mlp(mixed, w_feed, x, nv, hb, cot, lines, rows):
    length, width = x.shape
    blocks = hb.shape[0]
    token = lambda d: jax.ShapeDtypeStruct((length, width), d)
    full = grad_shape(2 * blocks, lines, rows, width // 2)
    one_w = w_feed.shape[:1] + w_feed.shape[2:] if w_feed.shape[1] != 2 else w_feed.shape[1:]
    one_g = full[:2] + full[3:] if len(full) == 5 else full[1:]
    buffer = lambda d, *lead: pltpu.VMEM((*lead, length, width), d)
    anywhere = pl.BlockSpec(memory_space=pl.ANY)
    side = pltpu.VMEM((width, length), BF)
    return pl.pallas_call(
        functools.partial(mlp_kernel, blocks),
        grid=(1,),
        in_specs=[held(nv.shape), held(hb.shape)] + [anywhere] * 4,
        out_specs=[
            anywhere, anywhere, whole((length, 128)), whole((length, width)), anywhere,
            whole(hb.shape), whole((8, width)),
        ],
        out_shape=[
            token(BF), token(F32), jax.ShapeDtypeStruct((length, 128), F32), token(F32),
            jax.ShapeDtypeStruct(full, BF),
            jax.ShapeDtypeStruct(hb.shape, F32),
            jax.ShapeDtypeStruct((8, width), F32),
        ],
        scratch_shapes=[
            buffer(BF), buffer(BF), buffer(BF), pltpu.VMEM((2 * blocks + 1, *one_w), BF),
            buffer(BF), buffer(F32), pltpu.VMEM((2 * blocks, *one_g), BF),
            buffer(BF), side, buffer(BF, blocks), buffer(BF, blocks), buffer(BF), side,
            buffer(BF, blocks),
            pltpu.SemaphoreType.DMA((2 * blocks + 4,)), pltpu.SemaphoreType.DMA((2 * blocks + 2,)),
        ],
        compiler_params=params(VMEM_MB),
        cost_estimate=cost(25),
        name="mlp",
    )(nv, hb, mixed, x, cot, w_feed)


def norm_down_kernel(
    gfirst_ref, unit_ref, inv_ref, nv_ref, wo_ref, gh1_ref, gattn_ref, gmixed_ref, sums_ref, prod_ref
):
    def rows_back(rows):
        gfirst = gfirst_ref[rows, :]
        unit = unit_ref[rows, :]
        gh1 = norm_back(unit, inv_ref[rows, 0:1], gfirst * nv_ref[0:1])
        gh1_ref[rows, :] = gh1
        gattn_ref[rows, :] = gh1.astype(BF)
        prod_ref[rows, :] = gfirst * unit

    rows_back(slice(None))
    gmixed_ref[...] = mm(gattn_ref[...], full_matrix(wo_ref)).astype(BF)
    sums_ref[0:1] = jnp.sum(prod_ref[...], axis=0, keepdims=True)
    sums_ref[1:2] = jnp.sum(gfirst_ref[...], axis=0, keepdims=True)
    sums_ref[2:3] = jnp.sum(gh1_ref[...], axis=0, keepdims=True)
    sums_ref[3:8] = jnp.zeros((5, sums_ref.shape[1]), F32)


def norm_down(gfirst, unit, inv, nv, w_feed):
    length, width = gfirst.shape
    one = whole((length, width))
    token = lambda d: jax.ShapeDtypeStruct((length, width), d)
    return pl.pallas_call(
        norm_down_kernel,
        grid=(1,),
        in_specs=[one, one, whole(inv.shape), whole(nv.shape), weight_spec(w_feed.shape, lambda b: w_feed.shape[int(w_feed.shape[1] != 2)] - 1)],
        out_specs=[one, one, one, whole((8, width))],
        out_shape=[token(F32), token(BF), token(BF), jax.ShapeDtypeStruct((8, width), F32)],
        scratch_shapes=[pltpu.VMEM((length, width), F32)],
        compiler_params=params(VMEM_MB),
        cost_estimate=cost(5),
        name="norm_down",
    )(gfirst, unit, inv, nv, w_feed)


def attend_back_kernel(
    probs_ref, gm_ref, qc_ref, qp_ref, k_ref, v_ref, rel_ref,
    gq_ref, gk_ref, gv_ref, grel_ref, sums_ref,
    rel_acc,
):
    length, pair = gm_ref.shape
    block = ROW_BLOCK
    span = length + block
    zero = jnp.zeros((), BF)
    flip = (
        lax.broadcasted_iota(jnp.int32, (block, block), 0)
        + lax.broadcasted_iota(jnp.int32, (block, block), 1)
        == block - 1
    ).astype(F32).astype(BF)
    k = k_ref[...]
    v = v_ref[...]
    tops = range(0, length, block)
    jobs = [(top, head) for top in tops for head in range(2)]
    pick = lambda ref, top, head: jnp.where(
        lane_mask(head, (block, pair)), ref[pl.ds(top, block), :], zero
    )
    band = lambda top: pl.ds(length - block - top, span)
    gprobs = [mm(pick(gm_ref, top, head), v, NT) for top, head in jobs]
    turned_qp = {top: mm(flip, qp_ref[pl.ds(top, block), :]).astype(BF) for top in tops}
    gsums = []
    for (top, head), gprob in zip(jobs, gprobs):
        probs = probs_ref[head, pl.ds(top, block), :].astype(F32)
        product = probs * gprob
        inner = jnp.sum(product, axis=1, keepdims=True)
        gsums.append((product - probs * inner).astype(BF))
    wides = []
    for gsum in gsums:
        wide = jnp.concatenate([mm(flip, gsum), jnp.zeros((block, block), F32)], axis=1)
        wides.append(pltpu.roll(wide, 0, 1, stride=1, stride_axis=0).astype(BF))
    gk = gv = None
    gqc, gqp = {}, {}
    for (top, head), gsum in zip(jobs, gsums):
        tall = lane_mask(head, (length, pair))
        a = mm(gsum, jnp.where(tall, k, zero))
        gqc[top] = a if head == 0 else gqc[top] + a
        b = mm(gsum, pick(qc_ref, top, head), TN)
        c = mm(probs_ref[head, pl.ds(top, block), :], pick(gm_ref, top, head), TN)
        gk = b if gk is None else gk + b
        gv = c if gv is None else gv + c
    rel_acc[...] = jnp.zeros_like(rel_acc)
    for (top, head), wide in zip(jobs, wides):
        rel = jnp.where(lane_mask(head, (span, pair)), rel_ref[band(top), :], zero)
        d = mm(wide, rel)
        gqp[top] = d if head == 0 else gqp[top] + d
        mask = lane_mask(head, (block, pair))
        rel_acc[band(top), :] += mm(wide, jnp.where(mask, turned_qp[top], zero), TN)
    sum_c = sum_p = None
    for top in tops:
        c, p = gqc[top] * SCALE, gqp[top] * SCALE
        high = p.astype(BF)
        rest = (p - high.astype(F32)).astype(BF)
        straight = mm(flip, high) + mm(flip, rest)
        gq_ref[pl.ds(top, block), :] = (c + straight).astype(BF)
        e = jnp.sum(c, axis=0, keepdims=True)
        f = jnp.sum(p, axis=0, keepdims=True)
        sum_c = e if sum_c is None else sum_c + e
        sum_p = f if sum_p is None else sum_p + f
    gk_ref[...] = gk.astype(BF)
    gv_ref[...] = gv.astype(BF)
    grel_ref[...] = rel_acc[...].astype(BF)
    sums_ref[0:1] = sum_c
    sums_ref[1:2] = sum_p
    sums_ref[2:8] = jnp.zeros((6, pair), F32)


def attend_back(probs, gm, qc, qp, k, v, rel):
    length, width = qc.shape
    pair = 2 * HEAD_FEATURES
    heads = width // HEAD_FEATURES
    column = pl.BlockSpec((length, pair), lambda p: (0, p))
    tall = pl.BlockSpec((rel.shape[0], pair), lambda p: (0, p))
    token = jax.ShapeDtypeStruct((length, width), BF)
    return pl.pallas_call(
        attend_back_kernel,
        grid=(heads // 2,),
        in_specs=[pl.BlockSpec((2, length, length), lambda p: (p, 0, 0))] + [column] * 5 + [tall],
        out_specs=[column, column, column, tall, pl.BlockSpec((8, pair), lambda p: (0, p))],
        out_shape=[
            token, token, token,
            jax.ShapeDtypeStruct(rel.shape, BF),
            jax.ShapeDtypeStruct((8, width), F32),
        ],
        scratch_shapes=[pltpu.VMEM((rel.shape[0], pair), F32)],
        compiler_params=params(VMEM_MB),
        cost_estimate=cost(28),
        name="attend_back",
    )(probs, gm, qc, qp, k, v, rel)


def project_back_kernel(
    x_ref, gq_ref, gk_ref, gv_ref, grel_ref, sine_ref, gattn_ref, mixed_ref, w_ref, gh1_ref,
    gw_ref, gtok_ref,
    turned_ref,
):
    step = pl.program_id(0)

    @pl.when(step == 0)
    def _():
        turned_ref[...] = x_ref[...].T
        gtok_ref[...] = gh1_ref[...]

    for which, g_ref in enumerate((gq_ref, gk_ref, gv_ref)):

        @pl.when(step == which)
        def _():
            store_matrix(gw_ref, mm(turned_ref[...], g_ref[...]))
            gtok_ref[...] += mm(g_ref[...], full_matrix(w_ref), NT)

    @pl.when(step == 3)
    def _():
        store_matrix(gw_ref, mm(sine_ref[...], grel_ref[...], TN))

    @pl.when(step == 4)
    def _():
        store_matrix(gw_ref, mm(gattn_ref[...], mixed_ref[...], TN))


def project_back(x, gq, gk, gv, grel, sine, gattn, mixed, w, gh1, lines, rows):
    length, width = x.shape
    one = held((length, width))
    shape = grad_shape(5, lines, rows, width // 2)
    return pl.pallas_call(
        project_back_kernel,
        grid=(5,),
        in_specs=[
            one, one, one, one, held(grel.shape), held(sine.shape), one, one,
            weight_spec(w.shape, lambda b: jnp.minimum(b, 2)),
            one,
        ],
        out_specs=[grad_spec(shape), whole((length, width))],
        out_shape=[
            jax.ShapeDtypeStruct(shape, BF),
            jax.ShapeDtypeStruct((length, width), F32),
        ],
        scratch_shapes=[pltpu.VMEM((width, length), BF)],
        compiler_params=params(VMEM_MB),
        cost_estimate=cost(12),
        name="project_back",
    )(x, gq, gk, gv, grel, sine, gattn, mixed, w, gh1)


def swap_x(value):
    return lax.ppermute(value, "mp", [(0, 1), (1, 0)])


def swap_dp(value, bit):
    return lax.ppermute(value, "dp", [(d, d ^ bit) for d in range(lax.axis_size("dp"))])


def shift_line(value, step):
    dp = lax.axis_size("dp")
    return lax.ppermute(value, "dp", [(d, (d + 4 * step) % dp) for d in range(dp)])


def gather_matrices(shard):
    dp = lax.axis_size("dp")
    if shard.shape[1] % 16 == 0:
        order = [mp * dp + index for mp, index in ring_order(dp // 4)]
        return lax.all_gather(
            shard, ("mp", "dp"), axis=0, axis_index_groups=[order], tiled=False
        )
    pieces = lax.all_gather(shard, ("mp", "dp"), axis=0, tiled=False)
    return whole_matrices(pieces.reshape((2, dp) + shard.shape))


def whole_matrices(pieces):
    mp, dp, blocks, rows, columns = pieces.shape
    return pieces.transpose(2, 0, 1, 3, 4).reshape(blocks, mp, dp * rows, columns)


def gather_lines(shard, others):
    lines = lax.axis_size("dp") // 4
    if lines != 4 or shard.shape[1] % 16 != 0:
        return shard, others
    near = [shard] + [shift_line(shard, step) for step in range(1, lines)]
    near, others = lax.optimization_barrier((near, others))
    return jnp.stack(near), others


def gather_stepwise(near, shard):
    dp = lax.axis_size("dp")
    blocks, rows, columns = shard.shape
    lines = dp // 4
    if lines != 4 or rows % 16 != 0:
        pieces = lax.all_gather(shard, ("mp", "dp"), axis=0, tiled=False)
        return (whole_matrices(pieces.reshape((2, dp) + shard.shape)),)
    cut = blocks // 2
    one, two = near[:, :cut], near[:, cut:]
    one_x = swap_x(one)
    two_y = swap_dp(two, 2)
    one_y = swap_dp(one, 2)
    two_x = swap_x(two)
    one_xy = swap_dp(one_x, 2)
    two_xy = swap_x(two_y)
    lane = [one, two, one_x, two_y, one_y, two_x, one_xy, two_xy]
    return tuple(lane + [swap_dp(part, 1) for part in lane])


def own_place():
    index = lax.axis_index("dp")
    place = jnp.stack([lax.axis_index("mp"), index // 4, (index // 2) % 2, index % 2])
    return place.astype(jnp.int32)


def plane_groups(dp):
    return [
        [mp * dp + line * 4 + y * 2 + core for mp, y, core in RING] for line in range(dp // 4)
    ]


def line_groups(dp):
    return [
        [mp * dp + line * 4 + low for line in range(dp // 4)] for mp in range(2) for low in range(4)
    ]


def scatter_plane(grads):
    dp = lax.axis_size("dp")
    if grads.ndim == 4:
        blocks, _, all_rows, columns = grads.shape
        grads = grads.reshape(blocks, 2, dp // 4, 2, 2, all_rows // dp, columns)
        grads = jnp.stack([grads[:, mp, :, y, core] for mp, y, core in RING])
        grads = grads.transpose(0, 2, 1, 3, 4)
    return lax.psum_scatter(
        grads, ("mp", "dp"), scatter_dimension=0, axis_index_groups=plane_groups(dp), tiled=False
    )


def scatter_line(part):
    dp = lax.axis_size("dp")
    lines = dp // 4
    if lines != 4:
        return lax.psum_scatter(
            part, ("mp", "dp"), scatter_dimension=0, axis_index_groups=line_groups(dp), tiled=False
        ).astype(F32)
    line = lax.axis_index("dp") // 4
    pick = lambda step: lax.dynamic_index_in_dim(part, (line + step) % lines, 0, keepdims=False)
    received = [shift_line(pick(step), step) for step in range(1, lines)]
    total = pick(0).astype(F32)
    for piece in received:
        total = total + piece.astype(F32)
    return total


def sum_small(value, meanwhile):
    value = value + swap_dp(value, 1)
    value = value + swap_x(value)
    value = value + swap_dp(value, 2)
    value, meanwhile = lax.optimization_barrier((value, meanwhile))
    return sum_line(value), meanwhile


def sum_line(value):
    lines = lax.axis_size("dp") // 4
    if lines != 4:
        return lax.psum(value, ("dp",), axis_index_groups=line_only(lines))
    total = value
    for piece in [shift_line(value, step) for step in range(1, lines)]:
        total = total + piece
    return total


def line_only(lines):
    return [[line * 4 + low for line in range(lines)] for low in range(4)]


def adam_kernel(order, g_ref, p_ref, one_ref, two_ref, *refs):
    outs = refs[-3:]
    for block, at in enumerate(order):
        results = adam_update(p_ref[at], g_ref[block], one_ref[at], two_ref[at], RATE_BIG)
        for out, result in zip(outs, results):
            out[at] = result


def adam_blocks(grad, order, param, one, two, done):
    blocks, rows, columns = grad.shape
    part = whole((blocks, rows, columns) if done else param.shape)
    shape = jax.ShapeDtypeStruct(param.shape, F32)
    return pl.pallas_call(
        functools.partial(adam_kernel, order),
        grid=(1,),
        in_specs=[whole(grad.shape), part, part, part]
        + [pl.BlockSpec(memory_space=pl.ANY)] * len(done),
        out_specs=[part] * 3,
        out_shape=[shape] * 3,
        input_output_aliases={4 + i: i for i in range(len(done))},
        compiler_params=params(VMEM_MB),
        cost_estimate=cost(blocks // 2),
        name="adam",
    )(grad, param, one, two, *done)


def per_device(
    tokens,
    lengths,
    weights,
    weight_m1,
    weight_m2,
    head_vecs,
    head_m1,
    head_m2,
    norm_vecs,
    norm_m1,
    norm_m2,
    cotangent,
):
    mp_index = lax.axis_index("mp")
    seq_len = cotangent.shape[0]
    weight_rows = weights.shape[0]
    local_width = weights.shape[2]
    model_width = tokens.shape[1]
    lines = lax.axis_size("dp") // 4
    x = lax.dynamic_slice_in_dim(tokens, mp_index * seq_len, seq_len, 0)
    used = lax.dynamic_slice_in_dim(lengths, mp_index, 1, 0)
    sine = relative_embedding(seq_len, model_width).astype(BF)
    shard = weights.transpose(1, 0, 2)
    shard_low = shard.astype(BF)
    heads_all = lax.all_gather(head_vecs, "mp", axis=1, tiled=True)
    w_feed = gather_matrices(jnp.concatenate([shard_low[5:13], shard_low[4:5]]))
    near, (x, sine, heads_all) = gather_lines(shard_low[0:4], (x, sine, heads_all))
    parts = gather_stepwise(near, shard_low[0:4])

    qc, qp, k, v, rel, w = project_parts(x, parts, heads_all[0:2], sine, own_place())
    probs, mixed = attend(used, qc, qp, k, v, rel)
    hb = heads_all[2:6].reshape(4, 1, model_width)
    out, unit, inv, gfirst, gw_feed, hsum, sums2 = mlp(
        mixed, w_feed, x, norm_vecs, hb, cotangent, lines, weight_rows
    )
    part_feed = scatter_plane(gw_feed)
    gh1, gattn, gmixed, sums1 = norm_down(gfirst, unit, inv, norm_vecs, w_feed)
    gq, gk, gv, grel, sums_q = attend_back(probs, gmixed, qc, qp, k, v, rel)
    gproj, grad_tokens = project_back(
        x, gq, gk, gv, grel, sine, gattn, mixed, w, gh1, lines, weight_rows
    )
    gproj, part_feed = lax.optimization_barrier((gproj, part_feed))
    part_proj = scatter_plane(gproj)

    norm_part = jnp.concatenate([sums1[0:2], sums2[0:2], sums1[2:3], sums2[2:3]], axis=0)
    head_part = jnp.concatenate([sums_q[0:2], hsum[:, 0]], axis=0)
    line_feed = scatter_line(part_feed)
    small = jnp.concatenate([norm_part, head_part], axis=0)
    small, line_feed = sum_small(small, line_feed)
    norm_grad = small[0:6]
    head_grad = lax.dynamic_slice_in_dim(small[6:12], mp_index * local_width, local_width, 1)
    state = (shard, weight_m1.transpose(1, 0, 2), weight_m2.transpose(1, 0, 2))
    held_big = adam_blocks(line_feed, (5, 9, 6, 10, 7, 11, 8, 12), *state, ())
    new_big = adam_blocks(scatter_line(part_proj), tuple(range(5)), *state, held_big)
    new_weights, new_weight_m1, new_weight_m2 = [a.transpose(1, 0, 2) for a in new_big]
    new_head, new_head_m1, new_head_m2 = adam_update(
        head_vecs, head_grad, head_m1, head_m2, RATE_SMALL
    )
    new_norm, new_norm_m1, new_norm_m2 = adam_update(
        norm_vecs, norm_grad, norm_m1, norm_m2, RATE_SMALL
    )
    return (
        out,
        grad_tokens,
        new_weights,
        new_weight_m1,
        new_weight_m2,
        new_head,
        new_head_m1,
        new_head_m2,
        new_norm,
        new_norm_m1,
        new_norm_m2,
    )


def solution(mesh):
    shard = P("dp", None, "mp")
    return jax.shard_map(
        per_device,
        mesh=mesh,
        in_specs=(P("dp", None), P("dp"), shard, shard, shard)
        + (P(None, "mp"),) * 3
        + (P(),) * 3
        + (P(("dp", "mp"), None),),
        out_specs=(P(("dp", "mp"), None),) * 2
        + (shard,) * 3
        + (P(None, "mp"),) * 3
        + (P(),) * 3,
        check_vma=False,
    )
```

```python
import functools

import jax
import jax.numpy as jnp
from jax import lax
from jax.experimental import pallas as pl
from jax.experimental.pallas import tpu as pltpu
from jax.sharding import PartitionSpec as P

HEAD_FEATURES = 64
STEP = 5
EPS_NORM = 1e-05
EPS_ADAM = 1e-08
BETA_ONE = 0.5
BETA_TWO = 0.5
RATE_BIG = 0.03
RATE_SMALL = 0.2
DECAY = 0.01
MASKED = -1e30
SCALE = HEAD_FEATURES ** (-0.5)
ROW_BLOCK = 256
VMEM_MB = 56
BF = jnp.bfloat16
F32 = jnp.float32

NN = (((1,), (0,)), ((), ()))
NT = (((1,), (1,)), ((), ()))
TN = (((0,), (0,)), ((), ()))


def mm(a, b, dims=NN):
    return lax.dot_general(a, b, dims, preferred_element_type=F32)


def whole(shape):
    return pl.BlockSpec(shape, lambda *_: (0,) * len(shape))


def held(shape):
    return pl.BlockSpec(shape, lambda *_: (0,) * len(shape), pipeline_mode=pl.Buffered(1))


def params(mebibytes):
    return pltpu.CompilerParams(vmem_limit_bytes=mebibytes * 1024 * 1024)


def cost(micros):
    return pl.CostEstimate(flops=int(micros * 1e9), bytes_accessed=0, transcendentals=0)


def relative_embedding(length, model_width):
    distance = (length - 1 - jnp.arange(2 * length)).astype(F32)
    freq_index = jnp.arange(model_width // 2).astype(F32)
    inverse = 1.0 / 10000.0 ** (2.0 * freq_index / model_width)
    angles = distance[:, None] * inverse[None, :]
    return jnp.concatenate([jnp.sin(angles), jnp.cos(angles)], axis=1)


def adam_update(param, grad_sum, moment_one, moment_two, rate):
    new_one = BETA_ONE * moment_one + (1.0 - BETA_ONE) * grad_sum
    new_two = BETA_TWO * moment_two + (1.0 - BETA_TWO) * grad_sum * grad_sum
    corrected_one = new_one / (1.0 - BETA_ONE**STEP)
    corrected_two = new_two / (1.0 - BETA_TWO**STEP)
    new_param = param - rate * (
        corrected_one / (jnp.sqrt(corrected_two) + EPS_ADAM) + DECAY * param
    )
    return (new_param, new_one, new_two)


def weight_spec(shape, which, each=None):
    if shape[1] != 2:
        return pl.BlockSpec((shape[0], each) + shape[2:], lambda b: (0, which(b), 0, 0))
    return pl.BlockSpec((each,) + shape[1:], lambda b: (which(b), 0, 0, 0))


def one_block(ref, index):
    if len(ref.shape) == 5:
        return ref.at[:, :, index]
    return ref.at[:, index] if ref.shape[0] > 8 else ref.at[index]


def ring_order(lines):
    order = []
    for turn, (mp, y) in enumerate(((0, 0), (0, 1), (1, 1), (1, 0))):
        for line in range(lines) if turn % 2 == 0 else reversed(range(lines)):
            order += [(mp, line * 4 + y * 2), (mp, line * 4 + y * 2 + 1)]
    return order


def full_matrix(w_ref):
    if len(w_ref.shape) == 3 and w_ref.shape[0] > 2:
        places = w_ref.shape[0]
        order = ring_order(places // 8)
        sides = [
            jnp.concatenate([w_ref[order.index((mp, dp))] for dp in range(places // 2)], axis=0)
            for mp in range(2)
        ]
        return jnp.concatenate(sides, axis=1)
    return jnp.concatenate([w_ref[0], w_ref[1]], axis=1)


RING = ((0, 0, 0), (0, 0, 1), (0, 1, 1), (0, 1, 0), (1, 1, 0), (1, 1, 1), (1, 0, 1), (1, 0, 0))


SQUARE = ((0, 0), (0, 1), (1, 1), (1, 0))


def layered(lines, rows):
    return rows % 16 == 0


def grad_shape(blocks, lines, rows, columns):
    if layered(lines, rows):
        return (len(RING), lines, blocks, rows, columns)
    return (blocks, 2, lines * 4 * rows, columns)


def grad_spec(shape):
    if len(shape) == 5:
        return pl.BlockSpec(shape[:2] + (None,) + shape[3:], lambda b: (0, 0, b, 0, 0))
    return pl.BlockSpec((None,) + shape[1:], lambda b: (b, 0, 0, 0))


def store_matrix(out_ref, value):
    half = value.shape[1] // 2
    low = value.astype(BF)
    if len(out_ref.shape) == 3:
        out_ref[0] = low[:, :half]
        out_ref[1] = low[:, half:]
        return
    places, lines, rows, _ = out_ref.shape
    for place, (mp, y, core) in enumerate(RING):
        for line in range(lines):
            top = (line * 4 + y * 2 + core) * rows
            out_ref[place, line] = low[top : top + rows, mp * half : (mp + 1) * half]


def store_split(keep_ref, send_ref, core, value):
    half = value.shape[1] // 2
    low = value.astype(BF)
    places, lines, rows, _ = keep_ref.shape
    for place, (mp, y) in enumerate(SQUARE):
        for line in range(lines):
            top = (line * 4 + y * 2) * rows
            columns = slice(mp * half, (mp + 1) * half)
            lower, upper = low[top : top + rows, columns], low[top + rows : top + 2 * rows, columns]
            keep_ref[place, line] = jnp.where(core == 0, lower, upper)
            send_ref[place, line] = jnp.where(core == 0, upper, lower)


def project_kernel(x_ref, w_ref, vec_ref, sine_ref, qc_ref, qp_ref, k_ref, v_ref, rel_ref):
    step = pl.program_id(0)

    @pl.when(step == 0)
    def _():
        q = mm(x_ref[...], full_matrix(w_ref))
        qc_ref[...] = (q + vec_ref[0:1]).astype(BF) * BF(SCALE)
        qp_ref[...] = (q + vec_ref[1:2]).astype(BF) * BF(SCALE)

    @pl.when(step == 1)
    def _():
        k_ref[...] = mm(x_ref[...], full_matrix(w_ref)).astype(BF)

    @pl.when(step == 2)
    def _():
        v_ref[...] = mm(x_ref[...], full_matrix(w_ref)).astype(BF)

    @pl.when(step == 3)
    def _():
        rel_ref[...] = mm(sine_ref[...], full_matrix(w_ref)).astype(BF)


def project(x, w, vecs, sine):
    length, width = x.shape
    rows = sine.shape[0]
    shapes = [(length, width)] * 4 + [(rows, width)]
    return pl.pallas_call(
        project_kernel,
        grid=(4,),
        in_specs=[
            whole(x.shape),
            weight_spec(w.shape, lambda b: b),
            whole(vecs.shape),
            whole(sine.shape),
        ],
        out_specs=[whole(s) for s in shapes],
        out_shape=[jax.ShapeDtypeStruct(s, BF) for s in shapes],
        compiler_params=params(VMEM_MB),
        cost_estimate=cost(9),
        name="project",
    )(x, w, vecs, sine)


PARTS = [
    (half, dx, dy, dc)
    for dc in (0, 1)
    for half, dx, dy in (
        (0, 0, 0), (1, 0, 0), (0, 1, 0), (1, 0, 1), (0, 0, 1), (1, 1, 0), (0, 1, 1), (1, 1, 1),
    )
]


def project_parts_kernel(
    cut, place_ref, x_ref, vec_ref, sine_ref, *refs,
):
    parts = refs[: len(PARTS)]
    outs = refs[len(PARTS) : len(PARTS) + 6]
    buffers = refs[len(PARTS) + 6 : len(PARTS) + 12]
    in_sem, out_sem = refs[-2:]
    w_ref = buffers[5]
    mp, line, y, core = (place_ref[i] for i in range(4))
    lines, _, rows, _ = parts[0].shape
    arriving = ([], [])
    for index, (half, dx, dy, dc) in enumerate(PARTS):
        for step in range(lines):
            at = lax.rem(line + lines - step, lines) * 4 + (y ^ dy) * 2 + (core ^ dc)
            start = pl.multiple_of(at * rows, rows)
            arriving[half].append(
                pltpu.make_async_copy(
                    parts[index].at[step],
                    w_ref.at[pl.ds(half * cut, cut), mp ^ dx, pl.ds(start, rows)],
                    in_sem.at[index * lines + step],
                )
            )
    for copy in arriving[0] + arriving[1]:
        copy.start()
    leaving = []

    def leave(source, target):
        copy = pltpu.make_async_copy(source, target, out_sem.at[len(leaving)])
        copy.start()
        leaving.append(copy)

    for copy in arriving[0]:
        copy.wait()
    leave(w_ref.at[0:2], outs[5].at[0:2])
    q = mm(x_ref[...], full_matrix(w_ref.at[0]))
    buffers[0][...] = (q + vec_ref[0:1]).astype(BF) * BF(SCALE)
    leave(buffers[0], outs[0])
    buffers[1][...] = (q + vec_ref[1:2]).astype(BF) * BF(SCALE)
    leave(buffers[1], outs[1])
    buffers[2][...] = mm(x_ref[...], full_matrix(w_ref.at[1])).astype(BF)
    leave(buffers[2], outs[2])
    for copy in arriving[1]:
        copy.wait()
    leave(w_ref.at[2:3], outs[5].at[2:3])
    buffers[4][...] = mm(sine_ref[...], full_matrix(w_ref.at[3])).astype(BF)
    leave(buffers[4], outs[4])
    buffers[3][...] = mm(x_ref[...], full_matrix(w_ref.at[2])).astype(BF)
    leave(buffers[3], outs[3])
    for copy in leaving:
        copy.wait()


def project_parts(x, parts, vecs, sine, place):
    if len(parts) == 1:
        return [*project(x, parts[0], vecs, sine), parts[0]]
    length, width = x.shape
    lines, cut, rows, columns = parts[0].shape
    shapes = [(length, width)] * 4 + [sine.shape]
    matrix = (2, lines * 4 * rows, columns)
    anywhere = pl.BlockSpec(memory_space=pl.ANY)
    return pl.pallas_call(
        functools.partial(project_parts_kernel, cut),
        grid=(1,),
        in_specs=[
            pl.BlockSpec(memory_space=pltpu.SMEM), held(x.shape), held(vecs.shape), held(sine.shape),
        ]
        + [anywhere] * len(parts),
        out_specs=[anywhere] * 6,
        out_shape=[jax.ShapeDtypeStruct(shape, BF) for shape in shapes + [(3,) + matrix]],
        scratch_shapes=[pltpu.VMEM(shape, BF) for shape in shapes + [(4,) + matrix]]
        + [pltpu.SemaphoreType.DMA((len(parts) * lines,)), pltpu.SemaphoreType.DMA((7,))],
        compiler_params=params(VMEM_MB),
        cost_estimate=cost(9),
        name="project",
    )(place, x, vecs, sine, *parts)


def lane_mask(which, shape):
    lanes = lax.broadcasted_iota(jnp.int32, shape, 1)
    return (lanes >= HEAD_FEATURES) if which else (lanes < HEAD_FEATURES)


def attend_kernel(len_ref, qc_ref, qp_ref, k_ref, v_ref, rel_ref, probs_ref, mixed_ref):
    length = qc_ref.shape[0]
    block = ROW_BLOCK
    pair = qc_ref.shape[1]
    valid = lax.broadcasted_iota(jnp.int32, (1, length), 1) < len_ref[0]
    k = k_ref[...]
    v = v_ref[...]
    zero = jnp.zeros((), BF)
    span = length + block
    jobs = [(top, head) for top in range(0, length, block) for head in range(2)]
    raw = []
    for top, head in jobs:
        rows = pl.ds(top, block)
        first = length - block - top
        mask = lane_mask(head, (block, pair))
        content = mm(jnp.where(mask, qc_ref[rows, :], zero), k, NT)
        place = mm(jnp.where(mask, qp_ref[rows, :], zero), rel_ref[first : first + span, :], NT)
        raw.append((content, place))
    for (top, head), (content, place) in zip(jobs, raw):
        place = pltpu.roll(place, span - (block - 1), 1, stride=1, stride_axis=0)
        scores = jnp.where(valid, content + place[:, :length], MASKED)
        top_score = jnp.max(scores, axis=1, keepdims=True)
        grown = jnp.exp(scores - top_score)
        probs = grown * (1.0 / jnp.sum(grown, axis=1, keepdims=True))
        probs_ref[head, pl.ds(top, block), :] = probs.astype(BF)
    for top in range(0, length, block):
        rows = pl.ds(top, block)
        lower, upper = mm(probs_ref[0, rows, :], v), mm(probs_ref[1, rows, :], v)
        mixed_ref[rows, :] = jnp.where(lane_mask(1, (block, pair)), upper, lower).astype(BF)


def attend(length_used, qc, qp, k, v, rel):
    length, width = qc.shape
    pair = 2 * HEAD_FEATURES
    heads = width // HEAD_FEATURES
    column = pl.BlockSpec((length, pair), lambda p: (0, p))
    return pl.pallas_call(
        attend_kernel,
        grid=(heads // 2,),
        in_specs=[pl.BlockSpec(memory_space=pltpu.SMEM)]
        + [column] * 4
        + [pl.BlockSpec((rel.shape[0], pair), lambda p: (0, p))],
        out_specs=[pl.BlockSpec((2, length, length), lambda p: (p, 0, 0)), column],
        out_shape=[
            jax.ShapeDtypeStruct((heads, length, length), BF),
            jax.ShapeDtypeStruct((length, width), BF),
        ],
        compiler_params=params(VMEM_MB),
        cost_estimate=cost(19),
        name="attend",
    )(length_used, qc, qp, k, v, rel)


def norm_parts(rows):
    mean = jnp.mean(rows, axis=1, keepdims=True)
    centred = rows - mean
    spread = jnp.mean(centred * centred, axis=1, keepdims=True)
    inverse = lax.rsqrt(spread + EPS_NORM)
    return centred * inverse, inverse


def norm_back(unit, inverse, scaled):
    return (
        scaled
        - jnp.mean(scaled, axis=1, keepdims=True)
        - unit * jnp.mean(scaled * unit, axis=1, keepdims=True)
    ) * inverse


def mlp_kernel(
    blocks, nv_ref, hb_ref, mixed_hbm, x_hbm, cot_hbm, w_hbm,
    out_hbm, unit_hbm, inv_ref, gh2_hbm, gw_hbm, ghid_hbm, sums_ref,
    mixed_ref, x_ref, cot_ref, w_ref, out_ref, unit_ref, gh2_ref, gw_ref,
    low_ref, turned_ref, act_ref, slope_ref, gffn_ref, gturned_ref, ghid_ref, in_sem, out_sem,
):
    order = [2 * blocks] + [at for i in range(blocks) for at in (i, blocks + i)]
    coming = {}

    def come(name, source, target):
        coming[name] = pltpu.make_async_copy(source, target, in_sem.at[len(coming)])
        coming[name].start()

    def matrix(at):
        if at in coming:
            coming.pop(at).wait()
        return full_matrix(w_ref.at[at])

    going = []

    def go(source, target):
        going.append(pltpu.make_async_copy(source, target, out_sem.at[len(going)]))
        going[-1].start()

    come("mixed", mixed_hbm, mixed_ref)
    for number, at in enumerate(order):
        if number == 1:
            come("x", x_hbm, x_ref)
        come(at, stacked_block(w_hbm, at), w_ref.at[at])
    come("cot", cot_hbm, cot_ref)

    length = x_ref.shape[0]
    halves = [pl.ds(top, length // 2) for top in (0, length // 2)]
    coming.pop("mixed").wait()
    w_out = matrix(2 * blocks)
    attn = [mm(mixed_ref[rows, :], w_out, NT) for rows in halves]
    coming.pop("x").wait()
    totals = []
    for rows, part in zip(halves, attn):
        unit, inverse = norm_parts(x_ref[rows, :].astype(F32) + part + nv_ref[4:5])
        unit_ref[rows, :] = unit
        inv_ref[rows, :] = jnp.broadcast_to(inverse, (length // 2, inv_ref.shape[1]))
        first = unit * nv_ref[0:1] + nv_ref[1:2]
        low_ref[rows, :] = first.astype(BF)
        totals.append(first + nv_ref[5:6])
    go(unit_ref, unit_hbm)
    turned_ref[...] = low_ref[...].T
    for i in range(blocks):
        hidden = mm(low_ref[...], matrix(i)) + hb_ref[i]
        bell = 0.5 * (1.0 + lax.erf(hidden * 0.7071067811865476))
        act_ref[i] = (hidden * bell).astype(BF)
        slope_ref[i] = (
            bell + hidden * (jnp.exp(hidden * hidden * -0.5) * 0.3989422804014327)
        ).astype(BF)
        w_back = matrix(blocks + i)
        totals = [
            total + mm(act_ref[i, rows, :], w_back, NT) for rows, total in zip(halves, totals)
        ]
    coming.pop("cot").wait()
    sums = [0.0, 0.0, 0.0]
    for rows, total in zip(halves, totals):
        unit, inverse = norm_parts(total)
        out_ref[rows, :] = (unit * nv_ref[2:3] + nv_ref[3:4]).astype(BF)
        cot = cot_ref[rows, :].astype(F32)
        gh2 = norm_back(unit, inverse, cot * nv_ref[2:3])
        gh2_ref[rows, :] = gh2
        gffn_ref[rows, :] = gh2.astype(BF)
        for i, value in enumerate((cot * unit, cot, gh2)):
            sums[i] = sums[i] + jnp.sum(value, axis=0, keepdims=True)
    go(out_ref, out_hbm)
    go(gh2_ref, gh2_hbm)
    for i in range(3):
        sums_ref[i : i + 1] = sums[i]
    gturned_ref[...] = gffn_ref[...].T
    for i in range(blocks):
        gact = mm(gffn_ref[...], matrix(blocks + i))
        store_matrix(gw_ref.at[2 * i + 1], mm(gturned_ref[...], act_ref[i]))
        go(gw_ref.at[2 * i + 1], one_block(gw_hbm, 2 * i + 1))
        ghid_ref[i] = (gact * slope_ref[i].astype(F32)).astype(BF)
        go(ghid_ref.at[i], ghid_hbm.at[i])
        sums_ref[3 + i : 4 + i] = jnp.sum(ghid_ref[i].astype(F32), axis=0, keepdims=True)
        store_matrix(gw_ref.at[2 * i], mm(turned_ref[...], ghid_ref[i]))
        go(gw_ref.at[2 * i], one_block(gw_hbm, 2 * i))
    for copy in going:
        copy.wait()


def stacked_block(ref, at):
    return ref.at[at] if ref.shape[1] == 2 else ref.at[:, at]


def one_matrix(shape):
    return shape[1:] if shape[1] == 2 else shape[:1] + shape[2:]


def mlp(mixed, w_feed, x, nv, hb, cot, lines, rows):
    length, width = x.shape
    blocks = hb.shape[0]
    token = lambda d, *lead: jax.ShapeDtypeStruct((*lead, length, width), d)
    full = grad_shape(2 * blocks, lines, rows, width // 2)
    one_g = full[:2] + full[3:] if len(full) == 5 else full[1:]
    buffer = lambda d, *lead: pltpu.VMEM((*lead, length, width), d)
    anywhere = pl.BlockSpec(memory_space=pl.ANY)
    side = pltpu.VMEM((width, length), BF)
    return pl.pallas_call(
        functools.partial(mlp_kernel, blocks),
        grid=(1,),
        in_specs=[held(nv.shape), held(hb.shape)] + [anywhere] * 4,
        out_specs=[
            anywhere, anywhere, whole((length, 128)), anywhere, anywhere, anywhere,
            whole((3 + blocks, width)),
        ],
        out_shape=[
            token(BF), token(F32), jax.ShapeDtypeStruct((length, 128), F32), token(F32),
            jax.ShapeDtypeStruct(full, BF), token(BF, blocks),
            jax.ShapeDtypeStruct((3 + blocks, width), F32),
        ],
        scratch_shapes=[
            buffer(BF), buffer(BF), buffer(BF),
            pltpu.VMEM((2 * blocks + 1, *one_matrix(w_feed.shape)), BF),
            buffer(BF), buffer(F32), buffer(F32), pltpu.VMEM((2 * blocks, *one_g), BF),
            buffer(BF), side, buffer(BF, blocks), buffer(BF, blocks), buffer(BF), side,
            buffer(BF, blocks),
            pltpu.SemaphoreType.DMA((2 * blocks + 4,)), pltpu.SemaphoreType.DMA((3 * blocks + 3,)),
        ],
        compiler_params=params(VMEM_MB),
        cost_estimate=cost(23),
        name="mlp",
    )(nv, hb, mixed, x, cot, w_feed)


def norm_down_kernel(
    blocks, nv_ref, inv_ref, unit_hbm, gh2_hbm, ghid_hbm, w_hbm,
    gh1_ref, gattn_ref, gmixed_ref, sums_ref,
    unit_ref, gh2_ref, ghid_ref, w_ref, sem,
):
    copies = []
    for i in range(blocks):
        copies.append((ghid_hbm.at[i], ghid_ref.at[i]))
        copies.append((stacked_block(w_hbm, i), w_ref.at[i]))
    copies.append((gh2_hbm, gh2_ref))
    copies.append((unit_hbm, unit_ref))
    copies.append((stacked_block(w_hbm, 2 * blocks), w_ref.at[blocks]))
    copies = [
        pltpu.make_async_copy(source, target, sem.at[i])
        for i, (source, target) in enumerate(copies)
    ]
    for copy in copies:
        copy.start()
    total = None
    for i in range(blocks):
        copies[2 * i].wait()
        copies[2 * i + 1].wait()
        part = mm(ghid_ref[i], full_matrix(w_ref.at[i]), NT)
        total = part if total is None else total + part
    for copy in copies[2 * blocks :]:
        copy.wait()
    gfirst = total + gh2_ref[...]
    unit = unit_ref[...]
    gh1 = norm_back(unit, inv_ref[:, 0:1], gfirst * nv_ref[0:1])
    gh1_ref[...] = gh1
    gattn_ref[...] = gh1.astype(BF)
    gmixed_ref[...] = mm(gattn_ref[...], full_matrix(w_ref.at[blocks])).astype(BF)
    for i, value in enumerate((gfirst * unit, gfirst, gh1)):
        sums_ref[i : i + 1] = jnp.sum(value, axis=0, keepdims=True)


def norm_down(gh2, ghid, unit, inv, nv, w_feed):
    length, width = gh2.shape
    blocks = ghid.shape[0]
    one = whole((length, width))
    token = lambda d: jax.ShapeDtypeStruct((length, width), d)
    buffer = lambda d, *lead: pltpu.VMEM((*lead, length, width), d)
    return pl.pallas_call(
        functools.partial(norm_down_kernel, blocks),
        grid=(1,),
        in_specs=[held(nv.shape), held(inv.shape)] + [pl.BlockSpec(memory_space=pl.ANY)] * 4,
        out_specs=[one, one, one, whole((3, width))],
        out_shape=[token(F32), token(BF), token(BF), jax.ShapeDtypeStruct((3, width), F32)],
        scratch_shapes=[
            buffer(F32), buffer(F32), buffer(BF, blocks),
            pltpu.VMEM((blocks + 1, *one_matrix(w_feed.shape)), BF),
            pltpu.SemaphoreType.DMA((2 * blocks + 3,)),
        ],
        compiler_params=params(VMEM_MB),
        cost_estimate=cost(8),
        name="norm_down",
    )(nv, inv, unit, gh2, ghid, w_feed)


def attend_back_kernel(
    probs_ref, gm_ref, qc_ref, qp_ref, k_ref, v_ref, rel_ref,
    gq_ref, gk_ref, gv_ref, grel_ref, sums_ref,
    rel_acc,
):
    length, pair = gm_ref.shape
    block = ROW_BLOCK
    span = length + block
    zero = jnp.zeros((), BF)
    flip = (
        lax.broadcasted_iota(jnp.int32, (block, block), 0)
        + lax.broadcasted_iota(jnp.int32, (block, block), 1)
        == block - 1
    ).astype(F32).astype(BF)
    k = k_ref[...]
    v = v_ref[...]
    tops = range(0, length, block)
    jobs = [(top, head) for top in tops for head in range(2)]
    pick = lambda ref, top, head: jnp.where(
        lane_mask(head, (block, pair)), ref[pl.ds(top, block), :], zero
    )
    band = lambda top: pl.ds(length - block - top, span)
    gprobs = [mm(pick(gm_ref, top, head), v, NT) for top, head in jobs]
    turned_qp = {top: mm(flip, qp_ref[pl.ds(top, block), :]).astype(BF) for top in tops}
    gsums = []
    for (top, head), gprob in zip(jobs, gprobs):
        probs = probs_ref[head, pl.ds(top, block), :].astype(F32)
        product = probs * gprob
        inner = jnp.sum(product, axis=1, keepdims=True)
        gsums.append((product - probs * inner).astype(BF))
    wides = []
    for gsum in gsums:
        wide = jnp.concatenate([mm(flip, gsum), jnp.zeros((block, block), F32)], axis=1)
        wides.append(pltpu.roll(wide, 0, 1, stride=1, stride_axis=0).astype(BF))
    gk = gv = None
    gqc, gqp = {}, {}
    for (top, head), gsum in zip(jobs, gsums):
        tall = lane_mask(head, (length, pair))
        a = mm(gsum, jnp.where(tall, k, zero))
        gqc[top] = a if head == 0 else gqc[top] + a
        b = mm(gsum, pick(qc_ref, top, head), TN)
        c = mm(probs_ref[head, pl.ds(top, block), :], pick(gm_ref, top, head), TN)
        gk = b if gk is None else gk + b
        gv = c if gv is None else gv + c
    rel_acc[...] = jnp.zeros_like(rel_acc)
    for (top, head), wide in zip(jobs, wides):
        rel = jnp.where(lane_mask(head, (span, pair)), rel_ref[band(top), :], zero)
        d = mm(wide, rel)
        gqp[top] = d if head == 0 else gqp[top] + d
        mask = lane_mask(head, (block, pair))
        rel_acc[band(top), :] += mm(wide, jnp.where(mask, turned_qp[top], zero), TN)
    sum_c = sum_p = None
    for top in tops:
        c, p = gqc[top] * SCALE, gqp[top] * SCALE
        high = p.astype(BF)
        rest = (p - high.astype(F32)).astype(BF)
        straight = mm(flip, high) + mm(flip, rest)
        gq_ref[pl.ds(top, block), :] = (c + straight).astype(BF)
        e = jnp.sum(c, axis=0, keepdims=True)
        f = jnp.sum(p, axis=0, keepdims=True)
        sum_c = e if sum_c is None else sum_c + e
        sum_p = f if sum_p is None else sum_p + f
    gk_ref[...] = gk.astype(BF)
    gv_ref[...] = gv.astype(BF)
    grel_ref[...] = rel_acc[...].astype(BF)
    sums_ref[0:1] = sum_c
    sums_ref[1:2] = sum_p


def attend_back(probs, gm, qc, qp, k, v, rel):
    length, width = qc.shape
    pair = 2 * HEAD_FEATURES
    heads = width // HEAD_FEATURES
    column = pl.BlockSpec((length, pair), lambda p: (0, p))
    tall = pl.BlockSpec((rel.shape[0], pair), lambda p: (0, p))
    token = jax.ShapeDtypeStruct((length, width), BF)
    return pl.pallas_call(
        attend_back_kernel,
        grid=(heads // 2,),
        in_specs=[pl.BlockSpec((2, length, length), lambda p: (p, 0, 0))] + [column] * 5 + [tall],
        out_specs=[column, column, column, tall, pl.BlockSpec((2, pair), lambda p: (0, p))],
        out_shape=[
            token, token, token,
            jax.ShapeDtypeStruct(rel.shape, BF),
            jax.ShapeDtypeStruct((2, width), F32),
        ],
        scratch_shapes=[pltpu.VMEM((rel.shape[0], pair), F32)],
        compiler_params=params(VMEM_MB),
        cost_estimate=cost(28),
        name="attend_back",
    )(probs, gm, qc, qp, k, v, rel)


def project_back_kernel(
    core_ref, x_ref, gq_ref, gk_ref, gv_ref, grel_ref, sine_ref, gattn_ref, mixed_ref, *refs,
):
    *gw_refs, turned_ref = refs
    step = pl.program_id(0)

    def store(value):
        if len(gw_refs) == 2:
            store_split(*gw_refs, core_ref[0], value)
        else:
            store_matrix(gw_refs[0], value)

    @pl.when(step == 0)
    def _():
        turned_ref[...] = x_ref[...].T

    for which, g_ref in enumerate((gq_ref, gk_ref, gv_ref)):

        @pl.when(step == which)
        def _():
            store(mm(turned_ref[...], g_ref[...]))

    @pl.when(step == 3)
    def _():
        store(mm(sine_ref[...], grel_ref[...], TN))

    @pl.when(step == 4)
    def _():
        store(mm(gattn_ref[...], mixed_ref[...], TN))


def project_back(core, x, gq, gk, gv, grel, sine, gattn, mixed, lines, rows):
    length, width = x.shape
    one = held((length, width))
    if layered(lines, rows):
        shapes = [(len(SQUARE), lines, 5, rows, width // 2)] * 2
    else:
        shapes = [grad_shape(5, lines, rows, width // 2)]
    return pl.pallas_call(
        project_back_kernel,
        grid=(5,),
        in_specs=[
            pl.BlockSpec(memory_space=pltpu.SMEM),
            one, one, one, one, held(grel.shape), held(sine.shape), one, one,
        ],
        out_specs=[grad_spec(shape) for shape in shapes],
        out_shape=[jax.ShapeDtypeStruct(shape, BF) for shape in shapes],
        scratch_shapes=[pltpu.VMEM((width, length), BF)],
        compiler_params=params(VMEM_MB),
        cost_estimate=cost(9),
        name="project_back",
    )(core, x, gq, gk, gv, grel, sine, gattn, mixed)


def token_grad_kernel(gq_ref, gk_ref, gv_ref, w_ref, gh1_ref, gtok_ref):
    total = gh1_ref[...]
    for i, g_ref in enumerate((gq_ref, gk_ref, gv_ref)):
        total += mm(g_ref[...], full_matrix(w_ref.at[i]), NT)
    gtok_ref[...] = total


def token_grad(gq, gk, gv, w, gh1):
    one = whole(gq.shape)
    return pl.pallas_call(
        token_grad_kernel,
        grid=(1,),
        in_specs=[one, one, one, whole((3,) + w.shape[1:]), one],
        out_specs=one,
        out_shape=jax.ShapeDtypeStruct(gq.shape, F32),
        compiler_params=params(VMEM_MB),
        cost_estimate=cost(6),
        name="token_grad",
    )(gq, gk, gv, w, gh1)


def swap_x(value):
    return lax.ppermute(value, "mp", [(0, 1), (1, 0)])


def swap_dp(value, bit):
    return lax.ppermute(value, "dp", [(d, d ^ bit) for d in range(lax.axis_size("dp"))])


def shift_line(value, step):
    dp = lax.axis_size("dp")
    return lax.ppermute(value, "dp", [(d, (d + 4 * step) % dp) for d in range(dp)])


def gather_matrices(shard):
    dp = lax.axis_size("dp")
    if shard.shape[1] % 16 == 0:
        order = [mp * dp + index for mp, index in ring_order(dp // 4)]
        return lax.all_gather(
            shard, ("mp", "dp"), axis=0, axis_index_groups=[order], tiled=False
        )
    pieces = lax.all_gather(shard, ("mp", "dp"), axis=0, tiled=False)
    return whole_matrices(pieces.reshape((2, dp) + shard.shape))


def whole_matrices(pieces):
    mp, dp, blocks, rows, columns = pieces.shape
    return pieces.transpose(2, 0, 1, 3, 4).reshape(blocks, mp, dp * rows, columns)


def gather_lines(shard, others):
    lines = lax.axis_size("dp") // 4
    if lines != 4 or shard.shape[1] % 16 != 0:
        return shard, others
    near = [shard] + [shift_line(shard, step) for step in range(1, lines)]
    near, others = lax.optimization_barrier((near, others))
    return jnp.stack(near), others


def gather_stepwise(near, shard):
    dp = lax.axis_size("dp")
    blocks, rows, columns = shard.shape
    lines = dp // 4
    if lines != 4 or rows % 16 != 0:
        pieces = lax.all_gather(shard, ("mp", "dp"), axis=0, tiled=False)
        return (whole_matrices(pieces.reshape((2, dp) + shard.shape)),)
    cut = blocks // 2
    one, two = near[:, :cut], near[:, cut:]
    one_x = swap_x(one)
    two_y = swap_dp(two, 2)
    one_y = swap_dp(one, 2)
    two_x = swap_x(two)
    one_xy = swap_dp(one_x, 2)
    two_xy = swap_x(two_y)
    lane = [one, two, one_x, two_y, one_y, two_x, one_xy, two_xy]
    return tuple(lane + [swap_dp(part, 1) for part in lane])


def own_place():
    index = lax.axis_index("dp")
    place = jnp.stack([lax.axis_index("mp"), index // 4, (index // 2) % 2, index % 2])
    return place.astype(jnp.int32)


def plane_groups(dp):
    return [
        [mp * dp + line * 4 + y * 2 + core for mp, y, core in RING] for line in range(dp // 4)
    ]


def line_groups(dp):
    return [
        [mp * dp + line * 4 + low for line in range(dp // 4)] for mp in range(2) for low in range(4)
    ]


def scatter_plane(grads):
    dp = lax.axis_size("dp")
    if grads.ndim == 4:
        blocks, _, all_rows, columns = grads.shape
        grads = grads.reshape(blocks, 2, dp // 4, 2, 2, all_rows // dp, columns)
        grads = jnp.stack([grads[:, mp, :, y, core] for mp, y, core in RING])
        grads = grads.transpose(0, 2, 1, 3, 4)
    return lax.psum_scatter(
        grads, ("mp", "dp"), scatter_dimension=0, axis_index_groups=plane_groups(dp), tiled=False
    )


def scatter_square(keep, send, before):
    dp = lax.axis_size("dp")
    grads = (keep.astype(F32) + swap_dp(send, 1).astype(F32)).astype(BF)
    grads, before = lax.optimization_barrier((grads, before))
    groups = [
        [mp * dp + line * 4 + y * 2 + core for mp, y in SQUARE]
        for line in range(dp // 4)
        for core in range(2)
    ]
    part = lax.psum_scatter(
        grads, ("mp", "dp"), scatter_dimension=0, axis_index_groups=groups, tiled=False
    )
    return part, before


def line_pieces(part):
    dp = lax.axis_size("dp")
    lines = dp // 4
    if lines != 4:
        return [part]
    line = lax.axis_index("dp") // 4
    return [
        lax.dynamic_index_in_dim(part, (line + step) % lines, 0, keepdims=False)
        for step in range(lines)
    ]


def trade_pieces(pieces):
    dp = lax.axis_size("dp")
    if len(pieces) == 1:
        return [
            lax.psum_scatter(
                pieces[0], ("mp", "dp"), scatter_dimension=0, axis_index_groups=line_groups(dp),
                tiled=False,
            )
        ]
    return [pieces[0]] + [shift_line(pieces[step], step) for step in range(1, len(pieces))]


def sum_plane(value, meanwhile):
    value = value + swap_dp(value, 1)
    value = value + swap_x(value)
    value, *meanwhile = lax.optimization_barrier((value, *meanwhile))
    return value + swap_dp(value, 2), meanwhile


def sum_line(value):
    lines = lax.axis_size("dp") // 4
    if lines != 4:
        return lax.psum(value, ("dp",), axis_index_groups=line_only(lines))
    total = value
    for piece in [shift_line(value, step) for step in range(1, lines)]:
        total = total + piece
    return total


def line_only(lines):
    return [[line * 4 + low for line in range(lines)] for low in range(4)]


def adam_kernel(order, count, *refs):
    pieces = refs[:count]
    p_ref, one_ref, two_ref = refs[count : count + 3]
    outs = refs[-3:]
    for block, at in enumerate(order):
        grad = pieces[0][block].astype(F32)
        for piece in pieces[1:]:
            grad = grad + piece[block].astype(F32)
        results = adam_update(p_ref[at], grad, one_ref[at], two_ref[at], RATE_BIG)
        for out, result in zip(outs, results):
            out[at] = result


def adam_blocks(pieces, order, param, one, two, done):
    blocks, rows, columns = pieces[0].shape
    part = whole((blocks, rows, columns) if done else param.shape)
    shape = jax.ShapeDtypeStruct(param.shape, F32)
    count = len(pieces)
    return pl.pallas_call(
        functools.partial(adam_kernel, order, count),
        grid=(1,),
        in_specs=[whole(pieces[0].shape)] * count
        + [part] * 3
        + [pl.BlockSpec(memory_space=pl.ANY)] * len(done),
        out_specs=[part] * 3,
        out_shape=[shape] * 3,
        input_output_aliases={count + 3 + i: i for i in range(len(done))},
        compiler_params=params(VMEM_MB),
        cost_estimate=cost(blocks // 2),
        name="adam",
    )(*pieces, param, one, two, *done)


def per_device(
    tokens,
    lengths,
    weights,
    weight_m1,
    weight_m2,
    head_vecs,
    head_m1,
    head_m2,
    norm_vecs,
    norm_m1,
    norm_m2,
    cotangent,
):
    mp_index = lax.axis_index("mp")
    seq_len = cotangent.shape[0]
    weight_rows = weights.shape[0]
    local_width = weights.shape[2]
    model_width = tokens.shape[1]
    lines = lax.axis_size("dp") // 4
    x = lax.dynamic_slice_in_dim(tokens, mp_index * seq_len, seq_len, 0)
    used = lax.dynamic_slice_in_dim(lengths, mp_index, 1, 0)
    sine = relative_embedding(seq_len, model_width).astype(BF)
    shard = weights.transpose(1, 0, 2)
    shard_low = shard.astype(BF)
    heads_all = lax.all_gather(head_vecs, "mp", axis=1, tiled=True)
    w_feed = gather_matrices(jnp.concatenate([shard_low[5:13], shard_low[4:5]]))
    near, (x, sine, heads_all) = gather_lines(shard_low[0:4], (x, sine, heads_all))
    parts = gather_stepwise(near, shard_low[0:4])

    qc, qp, k, v, rel, w = project_parts(x, parts, heads_all[0:2], sine, own_place())
    probs, mixed = attend(used, qc, qp, k, v, rel)
    hb = heads_all[2:6].reshape(4, 1, model_width)
    out, unit, inv, gh2, gw_feed, ghid, sums2 = mlp(
        mixed, w_feed, x, norm_vecs, hb, cotangent, lines, weight_rows
    )
    part_feed = scatter_plane(gw_feed)
    gh1, gattn, gmixed, sums1 = norm_down(gh2, ghid, unit, inv, norm_vecs, w_feed)
    gq, gk, gv, grel, sums_q = attend_back(probs, gmixed, qc, qp, k, v, rel)
    small = sum_line(jnp.concatenate([sums2, sums1, sums_q], axis=0))
    place = own_place()
    gproj = project_back(
        place[3:4], x, gq, gk, gv, grel, sine, gattn, mixed, lines, weight_rows
    )
    *gproj, small = lax.optimization_barrier((*gproj, small))
    if len(gproj) == 2:
        part_proj, part_feed = scatter_square(*gproj, part_feed)
    else:
        gproj, part_feed = lax.optimization_barrier((gproj[0], part_feed))
        part_proj = scatter_plane(gproj)

    pieces_feed = line_pieces(part_feed)
    *pieces_feed, gq = lax.optimization_barrier((*pieces_feed, gq))
    grad_tokens = token_grad(gq, gk, gv, w, gh1)
    pieces_feed = trade_pieces(pieces_feed)
    small, grad_tokens = lax.optimization_barrier((small, grad_tokens))
    small, pieces_feed = sum_plane(small, pieces_feed)
    norm_grad = jnp.concatenate([small[7:9], small[0:2], small[9:10], small[2:3]], axis=0)
    head_grad = jnp.concatenate([small[10:12], small[3:7]], axis=0)
    head_grad = lax.dynamic_slice_in_dim(head_grad, mp_index * local_width, local_width, 1)
    state = (shard, weight_m1.transpose(1, 0, 2), weight_m2.transpose(1, 0, 2))
    done = adam_blocks(pieces_feed, (5, 9, 6, 10, 7, 11, 8, 12), *state, ())
    small, norm_grad, done, part_proj = lax.optimization_barrier((small, norm_grad, done, part_proj))
    pieces_proj = trade_pieces(line_pieces(part_proj))
    new_big = adam_blocks(pieces_proj, tuple(range(5)), *state, done)
    new_weights, new_weight_m1, new_weight_m2 = [a.transpose(1, 0, 2) for a in new_big]
    new_head, new_head_m1, new_head_m2 = adam_update(
        head_vecs, head_grad, head_m1, head_m2, RATE_SMALL
    )
    new_norm, new_norm_m1, new_norm_m2 = adam_update(
        norm_vecs, norm_grad, norm_m1, norm_m2, RATE_SMALL
    )
    return (
        out,
        grad_tokens,
        new_weights,
        new_weight_m1,
        new_weight_m2,
        new_head,
        new_head_m1,
        new_head_m2,
        new_norm,
        new_norm_m1,
        new_norm_m2,
    )


def solution(mesh):
    shard = P("dp", None, "mp")
    return jax.shard_map(
        per_device,
        mesh=mesh,
        in_specs=(P("dp", None), P("dp"), shard, shard, shard)
        + (P(None, "mp"),) * 3
        + (P(),) * 3
        + (P(("dp", "mp"), None),),
        out_specs=(P(("dp", "mp"), None),) * 2
        + (shard,) * 3
        + (P(None, "mp"),) * 3
        + (P(),) * 3,
        check_vma=False,
    )
```

```python
import functools

import jax
import jax.numpy as jnp
from jax import lax
from jax.experimental import pallas as pl
from jax.experimental.pallas import tpu as pltpu
from jax.sharding import PartitionSpec as P

HEAD_FEATURES = 64
STEP = 5
EPS_NORM = 1e-05
EPS_ADAM = 1e-08
BETA_ONE = 0.5
BETA_TWO = 0.5
RATE_BIG = 0.03
RATE_SMALL = 0.2
DECAY = 0.01
MASKED = -1e30
SCALE = HEAD_FEATURES ** (-0.5)
ROW_BLOCK = 256
VMEM_MB = 56
UNROLL = 1
BF = jnp.bfloat16
F32 = jnp.float32

NN = (((1,), (0,)), ((), ()))
NT = (((1,), (1,)), ((), ()))
TN = (((0,), (0,)), ((), ()))


def mm(a, b, dims=NN):
    return lax.dot_general(a, b, dims, preferred_element_type=F32)


def whole(shape):
    return pl.BlockSpec(shape, lambda *_: (0,) * len(shape))


def held(shape):
    return pl.BlockSpec(shape, lambda *_: (0,) * len(shape), pipeline_mode=pl.Buffered(1))


def params(mebibytes):
    return pltpu.CompilerParams(vmem_limit_bytes=mebibytes * 1024 * 1024)


def cost(micros):
    return pl.CostEstimate(flops=int(micros * 1e9), bytes_accessed=0, transcendentals=0)


def relative_embedding(length, model_width):
    distance = (length - 1 - jnp.arange(2 * length)).astype(F32)
    freq_index = jnp.arange(model_width // 2).astype(F32)
    inverse = 1.0 / 10000.0 ** (2.0 * freq_index / model_width)
    angles = distance[:, None] * inverse[None, :]
    return jnp.concatenate([jnp.sin(angles), jnp.cos(angles)], axis=1)


def adam_update(param, grad_sum, moment_one, moment_two, rate):
    new_one = BETA_ONE * moment_one + (1.0 - BETA_ONE) * grad_sum
    new_two = BETA_TWO * moment_two + (1.0 - BETA_TWO) * grad_sum * grad_sum
    corrected_one = new_one / (1.0 - BETA_ONE**STEP)
    corrected_two = new_two / (1.0 - BETA_TWO**STEP)
    new_param = param - rate * (
        corrected_one / (jnp.sqrt(corrected_two) + EPS_ADAM) + DECAY * param
    )
    return (new_param, new_one, new_two)


def weight_spec(shape, which, each=None):
    if shape[1] != 2:
        return pl.BlockSpec((shape[0], each) + shape[2:], lambda b: (0, which(b), 0, 0))
    return pl.BlockSpec((each,) + shape[1:], lambda b: (which(b), 0, 0, 0))


def one_block(ref, index):
    if len(ref.shape) == 5:
        return ref.at[:, :, index]
    return ref.at[:, index] if ref.shape[0] > 8 else ref.at[index]


def ring_order(lines):
    order = []
    for turn, (mp, y) in enumerate(((0, 0), (0, 1), (1, 1), (1, 0))):
        for line in range(lines) if turn % 2 == 0 else reversed(range(lines)):
            order += [(mp, line * 4 + y * 2), (mp, line * 4 + y * 2 + 1)]
    return order


def full_matrix(w_ref):
    if len(w_ref.shape) == 3 and w_ref.shape[0] > 2:
        places = w_ref.shape[0]
        order = ring_order(places // 8)
        sides = [
            jnp.concatenate([w_ref[order.index((mp, dp))] for dp in range(places // 2)], axis=0)
            for mp in range(2)
        ]
        return jnp.concatenate(sides, axis=1)
    return jnp.concatenate([w_ref[0], w_ref[1]], axis=1)


RING = ((0, 0, 0), (0, 0, 1), (0, 1, 1), (0, 1, 0), (1, 1, 0), (1, 1, 1), (1, 0, 1), (1, 0, 0))


SQUARE = ((0, 0), (0, 1), (1, 1), (1, 0))


def layered(lines, rows):
    return rows % 16 == 0


def grad_shape(blocks, lines, rows, columns):
    if layered(lines, rows):
        return (len(RING), lines, blocks, rows, columns)
    return (blocks, 2, lines * 4 * rows, columns)


def grad_spec(shape):
    if len(shape) == 5:
        return pl.BlockSpec(shape[:2] + (None,) + shape[3:], lambda b: (0, 0, b, 0, 0))
    return pl.BlockSpec((None,) + shape[1:], lambda b: (b, 0, 0, 0))


def store_matrix(out_ref, value):
    half = value.shape[1] // 2
    low = value.astype(BF)
    if len(out_ref.shape) == 3:
        out_ref[0] = low[:, :half]
        out_ref[1] = low[:, half:]
        return
    places, lines, rows, _ = out_ref.shape
    for place, (mp, y, core) in enumerate(RING):
        for line in range(lines):
            top = (line * 4 + y * 2 + core) * rows
            out_ref[place, line] = low[top : top + rows, mp * half : (mp + 1) * half]


def store_split(keep_ref, send_ref, core, value):
    half = value.shape[1] // 2
    low = value.astype(BF)
    places, lines, rows, _ = keep_ref.shape
    for place, (mp, y) in enumerate(SQUARE):
        for line in range(lines):
            top = (line * 4 + y * 2) * rows
            columns = slice(mp * half, (mp + 1) * half)
            lower, upper = low[top : top + rows, columns], low[top + rows : top + 2 * rows, columns]
            keep_ref[place, line] = jnp.where(core == 0, lower, upper)
            send_ref[place, line] = jnp.where(core == 0, upper, lower)


def project_kernel(x_ref, w_ref, vec_ref, sine_ref, qc_ref, qp_ref, k_ref, v_ref, rel_ref):
    step = pl.program_id(0)

    @pl.when(step == 0)
    def _():
        q = mm(x_ref[...], full_matrix(w_ref))
        qc_ref[...] = (q + vec_ref[0:1]).astype(BF) * BF(SCALE)
        qp_ref[...] = (q + vec_ref[1:2]).astype(BF) * BF(SCALE)

    @pl.when(step == 1)
    def _():
        k_ref[...] = mm(x_ref[...], full_matrix(w_ref)).astype(BF)

    @pl.when(step == 2)
    def _():
        v_ref[...] = mm(x_ref[...], full_matrix(w_ref)).astype(BF)

    @pl.when(step == 3)
    def _():
        rel_ref[...] = mm(sine_ref[...], full_matrix(w_ref)).astype(BF)


def project(x, w, vecs, sine):
    length, width = x.shape
    rows = sine.shape[0]
    shapes = [(length, width)] * 4 + [(rows, width)]
    return pl.pallas_call(
        project_kernel,
        grid=(4,),
        in_specs=[
            whole(x.shape),
            weight_spec(w.shape, lambda b: b),
            whole(vecs.shape),
            whole(sine.shape),
        ],
        out_specs=[whole(s) for s in shapes],
        out_shape=[jax.ShapeDtypeStruct(s, BF) for s in shapes],
        compiler_params=params(VMEM_MB),
        cost_estimate=cost(9),
        name="project",
    )(x, w, vecs, sine)


PARTS = [
    (half, dx, dy, dc)
    for dc in (0, 1)
    for half, dx, dy in (
        (0, 0, 0), (1, 0, 0), (0, 1, 0), (1, 0, 1), (0, 0, 1), (1, 1, 0), (0, 1, 1), (1, 1, 1),
    )
]


def project_parts_kernel(
    cut, place_ref, x_ref, vec_ref, sine_ref, *refs,
):
    parts = refs[: len(PARTS)]
    outs = refs[len(PARTS) : len(PARTS) + 6]
    buffers = refs[len(PARTS) + 6 : len(PARTS) + 12]
    in_sem, out_sem = refs[-2:]
    w_ref = buffers[5]
    mp, line, y, core = (place_ref[i] for i in range(4))
    lines, _, rows, _ = parts[0].shape
    arriving = ([], [])
    for index, (half, dx, dy, dc) in enumerate(PARTS):
        for step in range(lines):
            at = lax.rem(line + lines - step, lines) * 4 + (y ^ dy) * 2 + (core ^ dc)
            start = pl.multiple_of(at * rows, rows)
            arriving[half].append(
                pltpu.make_async_copy(
                    parts[index].at[step],
                    w_ref.at[pl.ds(half * cut, cut), mp ^ dx, pl.ds(start, rows)],
                    in_sem.at[index * lines + step],
                )
            )
    for copy in arriving[0] + arriving[1]:
        copy.start()
    leaving = []

    def leave(source, target):
        copy = pltpu.make_async_copy(source, target, out_sem.at[len(leaving)])
        copy.start()
        leaving.append(copy)

    for copy in arriving[0]:
        copy.wait()
    leave(w_ref.at[0:2], outs[5].at[0:2])
    q = mm(x_ref[...], full_matrix(w_ref.at[0]))
    buffers[0][...] = (q + vec_ref[0:1]).astype(BF) * BF(SCALE)
    leave(buffers[0], outs[0])
    buffers[1][...] = (q + vec_ref[1:2]).astype(BF) * BF(SCALE)
    leave(buffers[1], outs[1])
    buffers[2][...] = mm(x_ref[...], full_matrix(w_ref.at[1])).astype(BF)
    leave(buffers[2], outs[2])
    for copy in arriving[1]:
        copy.wait()
    leave(w_ref.at[2:3], outs[5].at[2:3])
    buffers[4][...] = mm(sine_ref[...], full_matrix(w_ref.at[3])).astype(BF)
    leave(buffers[4], outs[4])
    buffers[3][...] = mm(x_ref[...], full_matrix(w_ref.at[2])).astype(BF)
    leave(buffers[3], outs[3])
    for copy in leaving:
        copy.wait()


def project_parts(x, parts, vecs, sine, place):
    if len(parts) == 1:
        return [*project(x, parts[0], vecs, sine), parts[0]]
    length, width = x.shape
    lines, cut, rows, columns = parts[0].shape
    shapes = [(length, width)] * 4 + [sine.shape]
    matrix = (2, lines * 4 * rows, columns)
    anywhere = pl.BlockSpec(memory_space=pl.ANY)
    return pl.pallas_call(
        functools.partial(project_parts_kernel, cut),
        grid=(1,),
        in_specs=[
            pl.BlockSpec(memory_space=pltpu.SMEM), held(x.shape), held(vecs.shape), held(sine.shape),
        ]
        + [anywhere] * len(parts),
        out_specs=[anywhere] * 6,
        out_shape=[jax.ShapeDtypeStruct(shape, BF) for shape in shapes + [(3,) + matrix]],
        scratch_shapes=[pltpu.VMEM(shape, BF) for shape in shapes + [(4,) + matrix]]
        + [pltpu.SemaphoreType.DMA((len(parts) * lines,)), pltpu.SemaphoreType.DMA((7,))],
        compiler_params=params(VMEM_MB),
        cost_estimate=cost(9),
        name="project",
    )(place, x, vecs, sine, *parts)


def lane_mask(which, shape):
    lanes = lax.broadcasted_iota(jnp.int32, shape, 1)
    return (lanes >= HEAD_FEATURES) if which else (lanes < HEAD_FEATURES)


def attend_kernel(len_ref, qc_ref, qp_ref, k_ref, v_ref, rel_ref, probs_ref, mixed_ref):
    length = qc_ref.shape[0]
    block = ROW_BLOCK
    pair = qc_ref.shape[1]
    valid = lax.broadcasted_iota(jnp.int32, (1, length), 1) < len_ref[0]
    k = k_ref[...]
    v = v_ref[...]
    zero = jnp.zeros((), BF)
    span = length + block
    jobs = [(top, head) for top in range(0, length, block) for head in range(2)]
    raw = []
    for top, head in jobs:
        rows = pl.ds(top, block)
        first = length - block - top
        mask = lane_mask(head, (block, pair))
        content = mm(jnp.where(mask, qc_ref[rows, :], zero), k, NT)
        place = mm(jnp.where(mask, qp_ref[rows, :], zero), rel_ref[first : first + span, :], NT)
        raw.append((content, place))
    for (top, head), (content, place) in zip(jobs, raw):
        place = pltpu.roll(place, span - (block - 1), 1, stride=1, stride_axis=0)
        scores = jnp.where(valid, content + place[:, :length], MASKED)
        top_score = jnp.max(scores, axis=1, keepdims=True)
        grown = jnp.exp(scores - top_score)
        probs = grown * (1.0 / jnp.sum(grown, axis=1, keepdims=True))
        probs_ref[head, pl.ds(top, block), :] = probs.astype(BF)
    for top in range(0, length, block):
        rows = pl.ds(top, block)
        lower, upper = mm(probs_ref[0, rows, :], v), mm(probs_ref[1, rows, :], v)
        mixed_ref[rows, :] = jnp.where(lane_mask(1, (block, pair)), upper, lower).astype(BF)


def attend(length_used, qc, qp, k, v, rel):
    length, width = qc.shape
    pair = 2 * HEAD_FEATURES
    heads = width // HEAD_FEATURES
    column = pl.BlockSpec((length, pair), lambda p: (0, p))
    return pl.pallas_call(
        attend_kernel,
        grid=(heads // 2,),
        in_specs=[pl.BlockSpec(memory_space=pltpu.SMEM)]
        + [column] * 4
        + [pl.BlockSpec((rel.shape[0], pair), lambda p: (0, p))],
        out_specs=[pl.BlockSpec((2, length, length), lambda p: (p, 0, 0)), column],
        out_shape=[
            jax.ShapeDtypeStruct((heads, length, length), BF),
            jax.ShapeDtypeStruct((length, width), BF),
        ],
        compiler_params=params(VMEM_MB),
        cost_estimate=cost(19),
        name="attend",
    )(length_used, qc, qp, k, v, rel)


def norm_parts(rows):
    mean = jnp.mean(rows, axis=1, keepdims=True)
    centred = rows - mean
    spread = jnp.mean(centred * centred, axis=1, keepdims=True)
    inverse = lax.rsqrt(spread + EPS_NORM)
    return centred * inverse, inverse


def norm_back(unit, inverse, scaled):
    return (
        scaled
        - jnp.mean(scaled, axis=1, keepdims=True)
        - unit * jnp.mean(scaled * unit, axis=1, keepdims=True)
    ) * inverse


def mlp_kernel(
    blocks, nv_ref, hb_ref, mixed_hbm, x_hbm, cot_hbm, w_hbm,
    out_hbm, unit_hbm, inv_ref, gh2_hbm, gw_hbm, ghid_hbm, sums_ref,
    mixed_ref, x_ref, cot_ref, w_ref, out_ref, unit_ref, gh2_ref, gw_ref,
    low_ref, turned_ref, act_ref, slope_ref, gffn_ref, gturned_ref, ghid_ref, total_ref, hsum_ref,
    in_sem, out_sem,
):
    copy_in = lambda source, target, at: pltpu.make_async_copy(source, target, in_sem.at[at])
    copy_w = lambda at: copy_in(stacked_block(w_hbm, at), w_ref.at[at], at)
    copy_mixed = copy_in(mixed_hbm, mixed_ref, 2 * blocks + 1)
    copy_x = copy_in(x_hbm, x_ref, 2 * blocks + 2)
    copy_cot = copy_in(cot_hbm, cot_ref, 2 * blocks + 3)
    copy_mixed.start()
    copy_w(2 * blocks).start()
    copy_x.start()
    for i in range(blocks):
        copy_w(i).start()
        copy_w(blocks + i).start()
    copy_cot.start()

    copy_out = lambda source, target, at: pltpu.make_async_copy(source, target, out_sem.at[at])
    copy_g = lambda at: copy_out(gw_ref.at[at], one_block(gw_hbm, at), at)
    copy_h = lambda at: copy_out(ghid_ref.at[at], ghid_hbm.at[at], 2 * blocks + at)
    copy_unit = copy_out(unit_ref, unit_hbm, 3 * blocks)
    copy_result = copy_out(out_ref, out_hbm, 3 * blocks + 1)
    copy_gh2 = copy_out(gh2_ref, gh2_hbm, 3 * blocks + 2)

    copy_mixed.wait()
    copy_w(2 * blocks).wait()
    attn = mm(mixed_ref[...], full_matrix(w_ref.at[2 * blocks]), NT)
    copy_x.wait()
    unit, inverse = norm_parts(x_ref[...].astype(F32) + attn + nv_ref[4:5])
    unit_ref[...] = unit
    copy_unit.start()
    inv_ref[...] = jnp.broadcast_to(inverse, inv_ref.shape)
    first = unit * nv_ref[0:1] + nv_ref[1:2]
    low_ref[...] = first.astype(BF)
    total_ref[...] = first + nv_ref[5:6]
    turned_ref[...] = low_ref[...].T

    def forward(i, carry):
        copy_w(i).wait()
        hidden = mm(low_ref[...], full_matrix(w_ref.at[i])) + hb_ref[i]
        bell = 0.5 * (1.0 + lax.erf(hidden * 0.7071067811865476))
        act_ref[i] = (hidden * bell).astype(BF)
        slope_ref[i] = (
            bell + hidden * (jnp.exp(hidden * hidden * -0.5) * 0.3989422804014327)
        ).astype(BF)
        copy_w(blocks + i).wait()
        total_ref[...] += mm(act_ref[i], full_matrix(w_ref.at[blocks + i]), NT)
        return carry

    lax.fori_loop(0, blocks, forward, 0, unroll=UNROLL)
    copy_cot.wait()
    unit, inverse = norm_parts(total_ref[...])
    out_ref[...] = (unit * nv_ref[2:3] + nv_ref[3:4]).astype(BF)
    copy_result.start()
    cot = cot_ref[...].astype(F32)
    gh2 = norm_back(unit, inverse, cot * nv_ref[2:3])
    gh2_ref[...] = gh2
    copy_gh2.start()
    gffn_ref[...] = gh2.astype(BF)
    for i, value in enumerate((cot * unit, cot, gh2)):
        sums_ref[i : i + 1] = jnp.sum(value, axis=0, keepdims=True)
    gturned_ref[...] = gffn_ref[...].T

    def backward(i, carry):
        gact = mm(gffn_ref[...], full_matrix(w_ref.at[blocks + i]))
        store_matrix(gw_ref.at[2 * i + 1], mm(gturned_ref[...], act_ref[i]))
        copy_g(2 * i + 1).start()
        ghid = (gact * slope_ref[i].astype(F32)).astype(BF)
        ghid_ref[i] = ghid
        copy_h(i).start()
        hsum_ref[i] = jnp.sum(ghid.astype(F32), axis=0, keepdims=True)
        store_matrix(gw_ref.at[2 * i], mm(turned_ref[...], ghid_ref[i]))
        copy_g(2 * i).start()
        return carry

    lax.fori_loop(0, blocks, backward, 0, unroll=UNROLL)
    for i in range(blocks):
        sums_ref[3 + i : 4 + i] = hsum_ref[i]
    copy_unit.wait()
    copy_result.wait()
    copy_gh2.wait()
    for i in range(blocks):
        copy_h(i).wait()
        copy_g(2 * i).wait()
        copy_g(2 * i + 1).wait()


def stacked_block(ref, at):
    return ref.at[at] if ref.shape[1] == 2 else ref.at[:, at]


def one_matrix(shape):
    return shape[1:] if shape[1] == 2 else shape[:1] + shape[2:]


def mlp(mixed, w_feed, x, nv, hb, cot, lines, rows):
    length, width = x.shape
    blocks = hb.shape[0]
    token = lambda d, *lead: jax.ShapeDtypeStruct((*lead, length, width), d)
    full = grad_shape(2 * blocks, lines, rows, width // 2)
    one_g = full[:2] + full[3:] if len(full) == 5 else full[1:]
    buffer = lambda d, *lead: pltpu.VMEM((*lead, length, width), d)
    anywhere = pl.BlockSpec(memory_space=pl.ANY)
    side = pltpu.VMEM((width, length), BF)
    return pl.pallas_call(
        functools.partial(mlp_kernel, blocks),
        grid=(1,),
        in_specs=[held(nv.shape), held(hb.shape)] + [anywhere] * 4,
        out_specs=[
            anywhere, anywhere, whole((length, 128)), anywhere, anywhere, anywhere,
            whole((3 + blocks, width)),
        ],
        out_shape=[
            token(BF), token(F32), jax.ShapeDtypeStruct((length, 128), F32), token(F32),
            jax.ShapeDtypeStruct(full, BF), token(BF, blocks),
            jax.ShapeDtypeStruct((3 + blocks, width), F32),
        ],
        scratch_shapes=[
            buffer(BF), buffer(BF), buffer(BF),
            pltpu.VMEM((2 * blocks + 1, *one_matrix(w_feed.shape)), BF),
            buffer(BF), buffer(F32), buffer(F32), pltpu.VMEM((2 * blocks, *one_g), BF),
            buffer(BF), side, buffer(BF, blocks), buffer(BF, blocks), buffer(BF), side,
            buffer(BF, blocks), buffer(F32), pltpu.VMEM((blocks, 1, width), F32),
            pltpu.SemaphoreType.DMA((2 * blocks + 4,)), pltpu.SemaphoreType.DMA((3 * blocks + 3,)),
        ],
        compiler_params=params(VMEM_MB),
        cost_estimate=cost(23),
        name="mlp",
    )(nv, hb, mixed, x, cot, w_feed)


def norm_down_kernel(
    blocks, nv_ref, inv_ref, unit_hbm, gh2_hbm, ghid_hbm, w_hbm,
    gh1_ref, gattn_ref, gmixed_ref, sums_ref,
    unit_ref, total_ref, ghid_ref, w_ref, sem,
):
    copy_in = lambda source, target, at: pltpu.make_async_copy(source, target, sem.at[at])
    copy_h = lambda i: copy_in(ghid_hbm.at[i], ghid_ref.at[i], i)
    copy_w = lambda i: copy_in(stacked_block(w_hbm, i), w_ref.at[i], blocks + i)
    copy_gh2 = copy_in(gh2_hbm, total_ref, 2 * blocks)
    copy_unit = copy_in(unit_hbm, unit_ref, 2 * blocks + 1)
    copy_last = copy_in(stacked_block(w_hbm, 2 * blocks), w_ref.at[blocks], 2 * blocks + 2)
    copy_gh2.start()
    for i in range(blocks):
        copy_h(i).start()
        copy_w(i).start()
    copy_unit.start()
    copy_last.start()
    copy_gh2.wait()

    def add(i, carry):
        copy_h(i).wait()
        copy_w(i).wait()
        total_ref[...] += mm(ghid_ref[i], full_matrix(w_ref.at[i]), NT)
        return carry

    lax.fori_loop(0, blocks, add, 0)
    copy_unit.wait()
    gfirst = total_ref[...]
    unit = unit_ref[...]
    gh1 = norm_back(unit, inv_ref[:, 0:1], gfirst * nv_ref[0:1])
    gh1_ref[...] = gh1
    gattn_ref[...] = gh1.astype(BF)
    copy_last.wait()
    gmixed_ref[...] = mm(gattn_ref[...], full_matrix(w_ref.at[blocks])).astype(BF)
    for i, value in enumerate((gfirst * unit, gfirst, gh1)):
        sums_ref[i : i + 1] = jnp.sum(value, axis=0, keepdims=True)


def norm_down(gh2, ghid, unit, inv, nv, w_feed):
    length, width = gh2.shape
    blocks = ghid.shape[0]
    one = whole((length, width))
    token = lambda d: jax.ShapeDtypeStruct((length, width), d)
    buffer = lambda d, *lead: pltpu.VMEM((*lead, length, width), d)
    return pl.pallas_call(
        functools.partial(norm_down_kernel, blocks),
        grid=(1,),
        in_specs=[held(nv.shape), held(inv.shape)] + [pl.BlockSpec(memory_space=pl.ANY)] * 4,
        out_specs=[one, one, one, whole((3, width))],
        out_shape=[token(F32), token(BF), token(BF), jax.ShapeDtypeStruct((3, width), F32)],
        scratch_shapes=[
            buffer(F32), buffer(F32), buffer(BF, blocks),
            pltpu.VMEM((blocks + 1, *one_matrix(w_feed.shape)), BF),
            pltpu.SemaphoreType.DMA((2 * blocks + 3,)),
        ],
        compiler_params=params(VMEM_MB),
        cost_estimate=cost(8),
        name="norm_down",
    )(nv, inv, unit, gh2, ghid, w_feed)


def attend_back_kernel(
    probs_ref, gm_ref, qc_ref, qp_ref, k_ref, v_ref, rel_ref,
    gq_ref, gk_ref, gv_ref, grel_ref, sums_ref,
    rel_acc,
):
    length, pair = gm_ref.shape
    block = ROW_BLOCK
    span = length + block
    zero = jnp.zeros((), BF)
    flip = (
        lax.broadcasted_iota(jnp.int32, (block, block), 0)
        + lax.broadcasted_iota(jnp.int32, (block, block), 1)
        == block - 1
    ).astype(F32).astype(BF)
    k = k_ref[...]
    v = v_ref[...]
    tops = range(0, length, block)
    jobs = [(top, head) for top in tops for head in range(2)]
    pick = lambda ref, top, head: jnp.where(
        lane_mask(head, (block, pair)), ref[pl.ds(top, block), :], zero
    )
    band = lambda top: pl.ds(length - block - top, span)
    gprobs = [mm(pick(gm_ref, top, head), v, NT) for top, head in jobs]
    turned_qp = {top: mm(flip, qp_ref[pl.ds(top, block), :]).astype(BF) for top in tops}
    gsums = []
    for (top, head), gprob in zip(jobs, gprobs):
        probs = probs_ref[head, pl.ds(top, block), :].astype(F32)
        product = probs * gprob
        inner = jnp.sum(product, axis=1, keepdims=True)
        gsums.append((product - probs * inner).astype(BF))
    wides = []
    for gsum in gsums:
        wide = jnp.concatenate([mm(flip, gsum), jnp.zeros((block, block), F32)], axis=1)
        wides.append(pltpu.roll(wide, 0, 1, stride=1, stride_axis=0).astype(BF))
    gk = gv = None
    gqc, gqp = {}, {}
    for (top, head), gsum in zip(jobs, gsums):
        tall = lane_mask(head, (length, pair))
        a = mm(gsum, jnp.where(tall, k, zero))
        gqc[top] = a if head == 0 else gqc[top] + a
        b = mm(gsum, pick(qc_ref, top, head), TN)
        c = mm(probs_ref[head, pl.ds(top, block), :], pick(gm_ref, top, head), TN)
        gk = b if gk is None else gk + b
        gv = c if gv is None else gv + c
    rel_acc[...] = jnp.zeros_like(rel_acc)
    for (top, head), wide in zip(jobs, wides):
        rel = jnp.where(lane_mask(head, (span, pair)), rel_ref[band(top), :], zero)
        d = mm(wide, rel)
        gqp[top] = d if head == 0 else gqp[top] + d
        mask = lane_mask(head, (block, pair))
        rel_acc[band(top), :] += mm(wide, jnp.where(mask, turned_qp[top], zero), TN)
    sum_c = sum_p = None
    for top in tops:
        c, p = gqc[top] * SCALE, gqp[top] * SCALE
        high = p.astype(BF)
        rest = (p - high.astype(F32)).astype(BF)
        straight = mm(flip, high) + mm(flip, rest)
        gq_ref[pl.ds(top, block), :] = (c + straight).astype(BF)
        e = jnp.sum(c, axis=0, keepdims=True)
        f = jnp.sum(p, axis=0, keepdims=True)
        sum_c = e if sum_c is None else sum_c + e
        sum_p = f if sum_p is None else sum_p + f
    gk_ref[...] = gk.astype(BF)
    gv_ref[...] = gv.astype(BF)
    grel_ref[...] = rel_acc[...].astype(BF)
    sums_ref[0:1] = sum_c
    sums_ref[1:2] = sum_p


def attend_back(probs, gm, qc, qp, k, v, rel):
    length, width = qc.shape
    pair = 2 * HEAD_FEATURES
    heads = width // HEAD_FEATURES
    column = pl.BlockSpec((length, pair), lambda p: (0, p))
    tall = pl.BlockSpec((rel.shape[0], pair), lambda p: (0, p))
    token = jax.ShapeDtypeStruct((length, width), BF)
    return pl.pallas_call(
        attend_back_kernel,
        grid=(heads // 2,),
        in_specs=[pl.BlockSpec((2, length, length), lambda p: (p, 0, 0))] + [column] * 5 + [tall],
        out_specs=[column, column, column, tall, pl.BlockSpec((2, pair), lambda p: (0, p))],
        out_shape=[
            token, token, token,
            jax.ShapeDtypeStruct(rel.shape, BF),
            jax.ShapeDtypeStruct((2, width), F32),
        ],
        scratch_shapes=[pltpu.VMEM((rel.shape[0], pair), F32)],
        compiler_params=params(VMEM_MB),
        cost_estimate=cost(28),
        name="attend_back",
    )(probs, gm, qc, qp, k, v, rel)


def project_back_kernel(
    core_ref, x_ref, gq_ref, gk_ref, gv_ref, grel_ref, sine_ref, gattn_ref, mixed_ref, *refs,
):
    *gw_refs, turned_ref = refs
    step = pl.program_id(0)

    def store(value):
        if len(gw_refs) == 2:
            store_split(*gw_refs, core_ref[0], value)
        else:
            store_matrix(gw_refs[0], value)

    @pl.when(step == 0)
    def _():
        turned_ref[...] = x_ref[...].T

    for which, g_ref in enumerate((gq_ref, gk_ref, gv_ref)):

        @pl.when(step == which)
        def _():
            store(mm(turned_ref[...], g_ref[...]))

    @pl.when(step == 3)
    def _():
        store(mm(sine_ref[...], grel_ref[...], TN))

    @pl.when(step == 4)
    def _():
        store(mm(gattn_ref[...], mixed_ref[...], TN))


def project_back(core, x, gq, gk, gv, grel, sine, gattn, mixed, lines, rows):
    length, width = x.shape
    one = held((length, width))
    if layered(lines, rows):
        shapes = [(len(SQUARE), lines, 5, rows, width // 2)] * 2
    else:
        shapes = [grad_shape(5, lines, rows, width // 2)]
    return pl.pallas_call(
        project_back_kernel,
        grid=(5,),
        in_specs=[
            pl.BlockSpec(memory_space=pltpu.SMEM),
            one, one, one, one, held(grel.shape), held(sine.shape), one, one,
        ],
        out_specs=[grad_spec(shape) for shape in shapes],
        out_shape=[jax.ShapeDtypeStruct(shape, BF) for shape in shapes],
        scratch_shapes=[pltpu.VMEM((width, length), BF)],
        compiler_params=params(VMEM_MB),
        cost_estimate=cost(9),
        name="project_back",
    )(core, x, gq, gk, gv, grel, sine, gattn, mixed)


def token_grad_kernel(gq_ref, gk_ref, gv_ref, w_ref, gh1_ref, gtok_ref):
    total = gh1_ref[...]
    for i, g_ref in enumerate((gq_ref, gk_ref, gv_ref)):
        total += mm(g_ref[...], full_matrix(w_ref.at[i]), NT)
    gtok_ref[...] = total


def token_grad(gq, gk, gv, w, gh1):
    one = whole(gq.shape)
    return pl.pallas_call(
        token_grad_kernel,
        grid=(1,),
        in_specs=[one, one, one, whole((3,) + w.shape[1:]), one],
        out_specs=one,
        out_shape=jax.ShapeDtypeStruct(gq.shape, F32),
        compiler_params=params(VMEM_MB),
        cost_estimate=cost(6),
        name="token_grad",
    )(gq, gk, gv, w, gh1)


def swap_x(value):
    return lax.ppermute(value, "mp", [(0, 1), (1, 0)])


def swap_dp(value, bit):
    return lax.ppermute(value, "dp", [(d, d ^ bit) for d in range(lax.axis_size("dp"))])


def shift_line(value, step):
    dp = lax.axis_size("dp")
    return lax.ppermute(value, "dp", [(d, (d + 4 * step) % dp) for d in range(dp)])


def gather_matrices(shard):
    dp = lax.axis_size("dp")
    if shard.shape[1] % 16 == 0:
        order = [mp * dp + index for mp, index in ring_order(dp // 4)]
        return lax.all_gather(
            shard, ("mp", "dp"), axis=0, axis_index_groups=[order], tiled=False
        )
    pieces = lax.all_gather(shard, ("mp", "dp"), axis=0, tiled=False)
    return whole_matrices(pieces.reshape((2, dp) + shard.shape))


def whole_matrices(pieces):
    mp, dp, blocks, rows, columns = pieces.shape
    return pieces.transpose(2, 0, 1, 3, 4).reshape(blocks, mp, dp * rows, columns)


def gather_lines(shard, others):
    lines = lax.axis_size("dp") // 4
    if lines != 4 or shard.shape[1] % 16 != 0:
        return shard, others
    near = [shard] + [shift_line(shard, step) for step in range(1, lines)]
    near, others = lax.optimization_barrier((near, others))
    return jnp.stack(near), others


def gather_stepwise(near, shard):
    dp = lax.axis_size("dp")
    blocks, rows, columns = shard.shape
    lines = dp // 4
    if lines != 4 or rows % 16 != 0:
        pieces = lax.all_gather(shard, ("mp", "dp"), axis=0, tiled=False)
        return (whole_matrices(pieces.reshape((2, dp) + shard.shape)),)
    cut = blocks // 2
    one, two = near[:, :cut], near[:, cut:]
    one_x = swap_x(one)
    two_y = swap_dp(two, 2)
    one_y = swap_dp(one, 2)
    two_x = swap_x(two)
    one_xy = swap_dp(one_x, 2)
    two_xy = swap_x(two_y)
    lane = [one, two, one_x, two_y, one_y, two_x, one_xy, two_xy]
    return tuple(lane + [swap_dp(part, 1) for part in lane])


def own_place():
    index = lax.axis_index("dp")
    place = jnp.stack([lax.axis_index("mp"), index // 4, (index // 2) % 2, index % 2])
    return place.astype(jnp.int32)


def plane_groups(dp):
    return [
        [mp * dp + line * 4 + y * 2 + core for mp, y, core in RING] for line in range(dp // 4)
    ]


def line_groups(dp):
    return [
        [mp * dp + line * 4 + low for line in range(dp // 4)] for mp in range(2) for low in range(4)
    ]


def scatter_plane(grads):
    dp = lax.axis_size("dp")
    if grads.ndim == 4:
        blocks, _, all_rows, columns = grads.shape
        grads = grads.reshape(blocks, 2, dp // 4, 2, 2, all_rows // dp, columns)
        grads = jnp.stack([grads[:, mp, :, y, core] for mp, y, core in RING])
        grads = grads.transpose(0, 2, 1, 3, 4)
    return lax.psum_scatter(
        grads, ("mp", "dp"), scatter_dimension=0, axis_index_groups=plane_groups(dp), tiled=False
    )


def scatter_square(keep, send, before):
    dp = lax.axis_size("dp")
    grads = (keep.astype(F32) + swap_dp(send, 1).astype(F32)).astype(BF)
    grads, before = lax.optimization_barrier((grads, before))
    groups = [
        [mp * dp + line * 4 + y * 2 + core for mp, y in SQUARE]
        for line in range(dp // 4)
        for core in range(2)
    ]
    part = lax.psum_scatter(
        grads, ("mp", "dp"), scatter_dimension=0, axis_index_groups=groups, tiled=False
    )
    return part, before


def line_pieces(part):
    dp = lax.axis_size("dp")
    lines = dp // 4
    if lines != 4:
        return [part]
    line = lax.axis_index("dp") // 4
    return [
        lax.dynamic_index_in_dim(part, (line + step) % lines, 0, keepdims=False)
        for step in range(lines)
    ]


def trade_pieces(pieces):
    dp = lax.axis_size("dp")
    if len(pieces) == 1:
        return [
            lax.psum_scatter(
                pieces[0], ("mp", "dp"), scatter_dimension=0, axis_index_groups=line_groups(dp),
                tiled=False,
            )
        ]
    return [pieces[0]] + [shift_line(pieces[step], step) for step in range(1, len(pieces))]


def sum_plane(value, meanwhile):
    value = value + swap_dp(value, 1)
    value = value + swap_x(value)
    value, *meanwhile = lax.optimization_barrier((value, *meanwhile))
    return value + swap_dp(value, 2), meanwhile


def sum_line(value):
    lines = lax.axis_size("dp") // 4
    if lines != 4:
        return lax.psum(value, ("dp",), axis_index_groups=line_only(lines))
    total = value
    for piece in [shift_line(value, step) for step in range(1, lines)]:
        total = total + piece
    return total


def line_only(lines):
    return [[line * 4 + low for line in range(lines)] for low in range(4)]


def adam_kernel(order, count, *refs):
    pieces = refs[:count]
    p_ref, one_ref, two_ref = refs[count : count + 3]
    outs = refs[-3:]
    for block, at in enumerate(order):
        grad = pieces[0][block].astype(F32)
        for piece in pieces[1:]:
            grad = grad + piece[block].astype(F32)
        results = adam_update(p_ref[at], grad, one_ref[at], two_ref[at], RATE_BIG)
        for out, result in zip(outs, results):
            out[at] = result


def adam_blocks(pieces, order, param, one, two, done):
    blocks, rows, columns = pieces[0].shape
    part = whole((blocks, rows, columns) if done else param.shape)
    shape = jax.ShapeDtypeStruct(param.shape, F32)
    count = len(pieces)
    return pl.pallas_call(
        functools.partial(adam_kernel, order, count),
        grid=(1,),
        in_specs=[whole(pieces[0].shape)] * count
        + [part] * 3
        + [pl.BlockSpec(memory_space=pl.ANY)] * len(done),
        out_specs=[part] * 3,
        out_shape=[shape] * 3,
        input_output_aliases={count + 3 + i: i for i in range(len(done))},
        compiler_params=params(VMEM_MB),
        cost_estimate=cost(blocks // 2),
        name="adam",
    )(*pieces, param, one, two, *done)


def per_device(
    tokens,
    lengths,
    weights,
    weight_m1,
    weight_m2,
    head_vecs,
    head_m1,
    head_m2,
    norm_vecs,
    norm_m1,
    norm_m2,
    cotangent,
):
    mp_index = lax.axis_index("mp")
    seq_len = cotangent.shape[0]
    weight_rows = weights.shape[0]
    local_width = weights.shape[2]
    model_width = tokens.shape[1]
    lines = lax.axis_size("dp") // 4
    x = lax.dynamic_slice_in_dim(tokens, mp_index * seq_len, seq_len, 0)
    used = lax.dynamic_slice_in_dim(lengths, mp_index, 1, 0)
    sine = relative_embedding(seq_len, model_width).astype(BF)
    shard = weights.transpose(1, 0, 2)
    shard_low = shard.astype(BF)
    heads_all = lax.all_gather(head_vecs, "mp", axis=1, tiled=True)
    w_feed = gather_matrices(jnp.concatenate([shard_low[5:13], shard_low[4:5]]))
    near, (x, sine, heads_all) = gather_lines(shard_low[0:4], (x, sine, heads_all))
    parts = gather_stepwise(near, shard_low[0:4])

    qc, qp, k, v, rel, w = project_parts(x, parts, heads_all[0:2], sine, own_place())
    probs, mixed = attend(used, qc, qp, k, v, rel)
    hb = heads_all[2:6].reshape(4, 1, model_width)
    out, unit, inv, gh2, gw_feed, ghid, sums2 = mlp(
        mixed, w_feed, x, norm_vecs, hb, cotangent, lines, weight_rows
    )
    part_feed = scatter_plane(gw_feed)
    gh1, gattn, gmixed, sums1 = norm_down(gh2, ghid, unit, inv, norm_vecs, w_feed)
    gq, gk, gv, grel, sums_q = attend_back(probs, gmixed, qc, qp, k, v, rel)
    small = sum_line(jnp.concatenate([sums2, sums1, sums_q], axis=0))
    place = own_place()
    gproj = project_back(
        place[3:4], x, gq, gk, gv, grel, sine, gattn, mixed, lines, weight_rows
    )
    *gproj, small = lax.optimization_barrier((*gproj, small))
    if len(gproj) == 2:
        part_proj, part_feed = scatter_square(*gproj, part_feed)
    else:
        gproj, part_feed = lax.optimization_barrier((gproj[0], part_feed))
        part_proj = scatter_plane(gproj)

    pieces_feed = line_pieces(part_feed)
    *pieces_feed, gq = lax.optimization_barrier((*pieces_feed, gq))
    grad_tokens = token_grad(gq, gk, gv, w, gh1)
    pieces_feed = trade_pieces(pieces_feed)
    small, grad_tokens = lax.optimization_barrier((small, grad_tokens))
    small, pieces_feed = sum_plane(small, pieces_feed)
    norm_grad = jnp.concatenate([small[7:9], small[0:2], small[9:10], small[2:3]], axis=0)
    head_grad = jnp.concatenate([small[10:12], small[3:7]], axis=0)
    head_grad = lax.dynamic_slice_in_dim(head_grad, mp_index * local_width, local_width, 1)
    state = (shard, weight_m1.transpose(1, 0, 2), weight_m2.transpose(1, 0, 2))
    done = adam_blocks(pieces_feed, (5, 9, 6, 10, 7, 11, 8, 12), *state, ())
    small, norm_grad, done, part_proj = lax.optimization_barrier((small, norm_grad, done, part_proj))
    pieces_proj = trade_pieces(line_pieces(part_proj))
    new_big = adam_blocks(pieces_proj, tuple(range(5)), *state, done)
    new_weights, new_weight_m1, new_weight_m2 = [a.transpose(1, 0, 2) for a in new_big]
    new_head, new_head_m1, new_head_m2 = adam_update(
        head_vecs, head_grad, head_m1, head_m2, RATE_SMALL
    )
    new_norm, new_norm_m1, new_norm_m2 = adam_update(
        norm_vecs, norm_grad, norm_m1, norm_m2, RATE_SMALL
    )
    return (
        out,
        grad_tokens,
        new_weights,
        new_weight_m1,
        new_weight_m2,
        new_head,
        new_head_m1,
        new_head_m2,
        new_norm,
        new_norm_m1,
        new_norm_m2,
    )


def solution(mesh):
    shard = P("dp", None, "mp")
    return jax.shard_map(
        per_device,
        mesh=mesh,
        in_specs=(P("dp", None), P("dp"), shard, shard, shard)
        + (P(None, "mp"),) * 3
        + (P(),) * 3
        + (P(("dp", "mp"), None),),
        out_specs=(P(("dp", "mp"), None),) * 2
        + (shard,) * 3
        + (P(None, "mp"),) * 3
        + (P(),) * 3,
        check_vma=False,
    )
```

```python
import functools

import jax
import jax.numpy as jnp
from jax import lax
from jax.experimental import pallas as pl
from jax.experimental.pallas import tpu as pltpu
from jax.sharding import PartitionSpec as P

HEAD_FEATURES = 64
STEP = 5
EPS_NORM = 1e-05
EPS_ADAM = 1e-08
BETA_ONE = 0.5
BETA_TWO = 0.5
RATE_BIG = 0.03
RATE_SMALL = 0.2
DECAY = 0.01
MASKED = -1e30
SCALE = HEAD_FEATURES ** (-0.5)
ROW_BLOCK = 256
VMEM_MB = 56
ADAM_MB = 16
UNROLL = 1
BF = jnp.bfloat16
F32 = jnp.float32

NN = (((1,), (0,)), ((), ()))
NT = (((1,), (1,)), ((), ()))
TN = (((0,), (0,)), ((), ()))


def mm(a, b, dims=NN):
    return lax.dot_general(a, b, dims, preferred_element_type=F32)


def whole(shape):
    return pl.BlockSpec(shape, lambda *_: (0,) * len(shape))


def held(shape):
    return pl.BlockSpec(shape, lambda *_: (0,) * len(shape), pipeline_mode=pl.Buffered(1))


def params(mebibytes):
    return pltpu.CompilerParams(vmem_limit_bytes=mebibytes * 1024 * 1024)


def cost(micros):
    return pl.CostEstimate(flops=int(micros * 1e9), bytes_accessed=0, transcendentals=0)


def relative_embedding(length, model_width):
    distance = (length - 1 - jnp.arange(2 * length)).astype(F32)
    freq_index = jnp.arange(model_width // 2).astype(F32)
    inverse = 1.0 / 10000.0 ** (2.0 * freq_index / model_width)
    angles = distance[:, None] * inverse[None, :]
    return jnp.concatenate([jnp.sin(angles), jnp.cos(angles)], axis=1)


def adam_update(param, grad_sum, moment_one, moment_two, rate):
    new_one = BETA_ONE * moment_one + (1.0 - BETA_ONE) * grad_sum
    new_two = BETA_TWO * moment_two + (1.0 - BETA_TWO) * grad_sum * grad_sum
    corrected_one = new_one / (1.0 - BETA_ONE**STEP)
    corrected_two = new_two / (1.0 - BETA_TWO**STEP)
    new_param = param - rate * (
        corrected_one / (jnp.sqrt(corrected_two) + EPS_ADAM) + DECAY * param
    )
    return (new_param, new_one, new_two)


def weight_spec(shape, which, each=None):
    if shape[1] != 2:
        return pl.BlockSpec((shape[0], each) + shape[2:], lambda b: (0, which(b), 0, 0))
    return pl.BlockSpec((each,) + shape[1:], lambda b: (which(b), 0, 0, 0))


def one_block(ref, index):
    if len(ref.shape) == 5:
        return ref.at[:, :, index]
    return ref.at[:, index] if ref.shape[0] > 8 else ref.at[index]


def ring_order(lines):
    order = []
    for turn, (mp, y) in enumerate(((0, 0), (0, 1), (1, 1), (1, 0))):
        for line in range(lines) if turn % 2 == 0 else reversed(range(lines)):
            order += [(mp, line * 4 + y * 2), (mp, line * 4 + y * 2 + 1)]
    return order


def full_matrix(w_ref):
    if len(w_ref.shape) == 3 and w_ref.shape[0] > 2:
        places = w_ref.shape[0]
        order = ring_order(places // 8)
        sides = [
            jnp.concatenate([w_ref[order.index((mp, dp))] for dp in range(places // 2)], axis=0)
            for mp in range(2)
        ]
        return jnp.concatenate(sides, axis=1)
    return jnp.concatenate([w_ref[0], w_ref[1]], axis=1)


RING = ((0, 0, 0), (0, 0, 1), (0, 1, 1), (0, 1, 0), (1, 1, 0), (1, 1, 1), (1, 0, 1), (1, 0, 0))


SQUARE = ((0, 0), (0, 1), (1, 1), (1, 0))


def layered(lines, rows):
    return rows % 16 == 0


def grad_shape(blocks, lines, rows, columns):
    if layered(lines, rows):
        return (len(RING), lines, blocks, rows, columns)
    return (blocks, 2, lines * 4 * rows, columns)


def grad_spec(shape):
    if len(shape) == 5:
        return pl.BlockSpec(shape[:2] + (None,) + shape[3:], lambda b: (0, 0, b, 0, 0))
    return pl.BlockSpec((None,) + shape[1:], lambda b: (b, 0, 0, 0))


def store_matrix(out_ref, value):
    half = value.shape[1] // 2
    low = value.astype(BF)
    if len(out_ref.shape) == 3:
        out_ref[0] = low[:, :half]
        out_ref[1] = low[:, half:]
        return
    places, lines, rows, _ = out_ref.shape
    for place, (mp, y, core) in enumerate(RING):
        for line in range(lines):
            top = (line * 4 + y * 2 + core) * rows
            out_ref[place, line] = low[top : top + rows, mp * half : (mp + 1) * half]


def store_split(keep_ref, send_ref, core, value):
    half = value.shape[1] // 2
    low = value.astype(BF)
    places, lines, rows, _ = keep_ref.shape
    for place, (mp, y) in enumerate(SQUARE):
        for line in range(lines):
            top = (line * 4 + y * 2) * rows
            columns = slice(mp * half, (mp + 1) * half)
            lower, upper = low[top : top + rows, columns], low[top + rows : top + 2 * rows, columns]
            keep_ref[place, line] = jnp.where(core == 0, lower, upper)
            send_ref[place, line] = jnp.where(core == 0, upper, lower)


def project_kernel(x_ref, w_ref, vec_ref, sine_ref, qc_ref, qp_ref, k_ref, v_ref, rel_ref):
    step = pl.program_id(0)

    @pl.when(step == 0)
    def _():
        q = mm(x_ref[...], full_matrix(w_ref))
        qc_ref[...] = (q + vec_ref[0:1]).astype(BF) * BF(SCALE)
        qp_ref[...] = (q + vec_ref[1:2]).astype(BF) * BF(SCALE)

    @pl.when(step == 1)
    def _():
        k_ref[...] = mm(x_ref[...], full_matrix(w_ref)).astype(BF)

    @pl.when(step == 2)
    def _():
        v_ref[...] = mm(x_ref[...], full_matrix(w_ref)).astype(BF)

    @pl.when(step == 3)
    def _():
        rel_ref[...] = mm(sine_ref[...], full_matrix(w_ref)).astype(BF)


def project(x, w, vecs, sine):
    length, width = x.shape
    rows = sine.shape[0]
    shapes = [(length, width)] * 4 + [(rows, width)]
    return pl.pallas_call(
        project_kernel,
        grid=(4,),
        in_specs=[
            whole(x.shape),
            weight_spec(w.shape, lambda b: b),
            whole(vecs.shape),
            whole(sine.shape),
        ],
        out_specs=[whole(s) for s in shapes],
        out_shape=[jax.ShapeDtypeStruct(s, BF) for s in shapes],
        compiler_params=params(VMEM_MB),
        cost_estimate=cost(9),
        name="project",
    )(x, w, vecs, sine)


PARTS = [
    (half, dx, dy, dc)
    for dc in (0, 1)
    for half, dx, dy in (
        (0, 0, 0), (1, 0, 0), (0, 1, 0), (1, 0, 1), (0, 0, 1), (1, 1, 0), (0, 1, 1), (1, 1, 1),
    )
]


def project_parts_kernel(
    cut, place_ref, x_ref, vec_ref, sine_ref, *refs,
):
    parts = refs[: len(PARTS)]
    outs = refs[len(PARTS) : len(PARTS) + 6]
    buffers = refs[len(PARTS) + 6 : len(PARTS) + 12]
    in_sem, out_sem = refs[-2:]
    w_ref = buffers[5]
    mp, line, y, core = (place_ref[i] for i in range(4))
    lines, _, rows, _ = parts[0].shape
    arriving = ([], [])
    for index, (half, dx, dy, dc) in enumerate(PARTS):
        for step in range(lines):
            at = lax.rem(line + lines - step, lines) * 4 + (y ^ dy) * 2 + (core ^ dc)
            start = pl.multiple_of(at * rows, rows)
            arriving[half].append(
                pltpu.make_async_copy(
                    parts[index].at[step],
                    w_ref.at[pl.ds(half * cut, cut), mp ^ dx, pl.ds(start, rows)],
                    in_sem.at[index * lines + step],
                )
            )
    for copy in arriving[0] + arriving[1]:
        copy.start()
    leaving = []

    def leave(source, target):
        copy = pltpu.make_async_copy(source, target, out_sem.at[len(leaving)])
        copy.start()
        leaving.append(copy)

    for copy in arriving[0]:
        copy.wait()
    leave(w_ref.at[0:2], outs[5].at[0:2])
    q = mm(x_ref[...], full_matrix(w_ref.at[0]))
    buffers[0][...] = (q + vec_ref[0:1]).astype(BF) * BF(SCALE)
    leave(buffers[0], outs[0])
    buffers[1][...] = (q + vec_ref[1:2]).astype(BF) * BF(SCALE)
    leave(buffers[1], outs[1])
    buffers[2][...] = mm(x_ref[...], full_matrix(w_ref.at[1])).astype(BF)
    leave(buffers[2], outs[2])
    for copy in arriving[1]:
        copy.wait()
    leave(w_ref.at[2:3], outs[5].at[2:3])
    buffers[4][...] = mm(sine_ref[...], full_matrix(w_ref.at[3])).astype(BF)
    leave(buffers[4], outs[4])
    buffers[3][...] = mm(x_ref[...], full_matrix(w_ref.at[2])).astype(BF)
    leave(buffers[3], outs[3])
    for copy in leaving:
        copy.wait()


def project_parts(x, parts, vecs, sine, place):
    if len(parts) == 1:
        return [*project(x, parts[0], vecs, sine), parts[0]]
    length, width = x.shape
    lines, cut, rows, columns = parts[0].shape
    shapes = [(length, width)] * 4 + [sine.shape]
    matrix = (2, lines * 4 * rows, columns)
    anywhere = pl.BlockSpec(memory_space=pl.ANY)
    return pl.pallas_call(
        functools.partial(project_parts_kernel, cut),
        grid=(1,),
        in_specs=[
            pl.BlockSpec(memory_space=pltpu.SMEM), held(x.shape), held(vecs.shape), held(sine.shape),
        ]
        + [anywhere] * len(parts),
        out_specs=[anywhere] * 6,
        out_shape=[jax.ShapeDtypeStruct(shape, BF) for shape in shapes + [(3,) + matrix]],
        scratch_shapes=[pltpu.VMEM(shape, BF) for shape in shapes + [(4,) + matrix]]
        + [pltpu.SemaphoreType.DMA((len(parts) * lines,)), pltpu.SemaphoreType.DMA((7,))],
        compiler_params=params(VMEM_MB),
        cost_estimate=cost(9),
        name="project",
    )(place, x, vecs, sine, *parts)


def lane_mask(which, shape):
    lanes = lax.broadcasted_iota(jnp.int32, shape, 1)
    return (lanes >= HEAD_FEATURES) if which else (lanes < HEAD_FEATURES)


def attend_kernel(len_ref, qc_ref, qp_ref, k_ref, v_ref, rel_ref, probs_ref, mixed_ref):
    length = qc_ref.shape[0]
    block = ROW_BLOCK
    pair = qc_ref.shape[1]
    valid = lax.broadcasted_iota(jnp.int32, (1, length), 1) < len_ref[0]
    k = k_ref[...]
    v = v_ref[...]
    zero = jnp.zeros((), BF)
    span = length + block
    jobs = [(top, head) for top in range(0, length, block) for head in range(2)]
    raw = []
    for top, head in jobs:
        rows = pl.ds(top, block)
        first = length - block - top
        mask = lane_mask(head, (block, pair))
        content = mm(jnp.where(mask, qc_ref[rows, :], zero), k, NT)
        place = mm(jnp.where(mask, qp_ref[rows, :], zero), rel_ref[first : first + span, :], NT)
        raw.append((content, place))
    for (top, head), (content, place) in zip(jobs, raw):
        place = pltpu.roll(place, span - (block - 1), 1, stride=1, stride_axis=0)
        scores = jnp.where(valid, content + place[:, :length], MASKED)
        top_score = jnp.max(scores, axis=1, keepdims=True)
        grown = jnp.exp(scores - top_score)
        probs = grown * (1.0 / jnp.sum(grown, axis=1, keepdims=True))
        probs_ref[head, pl.ds(top, block), :] = probs.astype(BF)
    for top in range(0, length, block):
        rows = pl.ds(top, block)
        lower, upper = mm(probs_ref[0, rows, :], v), mm(probs_ref[1, rows, :], v)
        mixed_ref[rows, :] = jnp.where(lane_mask(1, (block, pair)), upper, lower).astype(BF)


def attend(length_used, qc, qp, k, v, rel):
    length, width = qc.shape
    pair = 2 * HEAD_FEATURES
    heads = width // HEAD_FEATURES
    column = pl.BlockSpec((length, pair), lambda p: (0, p))
    return pl.pallas_call(
        attend_kernel,
        grid=(heads // 2,),
        in_specs=[pl.BlockSpec(memory_space=pltpu.SMEM)]
        + [column] * 4
        + [pl.BlockSpec((rel.shape[0], pair), lambda p: (0, p))],
        out_specs=[pl.BlockSpec((2, length, length), lambda p: (p, 0, 0)), column],
        out_shape=[
            jax.ShapeDtypeStruct((heads, length, length), BF),
            jax.ShapeDtypeStruct((length, width), BF),
        ],
        compiler_params=params(VMEM_MB),
        cost_estimate=cost(19),
        name="attend",
    )(length_used, qc, qp, k, v, rel)


def norm_parts(rows):
    mean = jnp.mean(rows, axis=1, keepdims=True)
    centred = rows - mean
    spread = jnp.mean(centred * centred, axis=1, keepdims=True)
    inverse = lax.rsqrt(spread + EPS_NORM)
    return centred * inverse, inverse


def norm_back(unit, inverse, scaled):
    return (
        scaled
        - jnp.mean(scaled, axis=1, keepdims=True)
        - unit * jnp.mean(scaled * unit, axis=1, keepdims=True)
    ) * inverse


def mlp_kernel(
    blocks, nv_ref, hb_ref, mixed_hbm, x_hbm, cot_hbm, w_hbm,
    out_hbm, unit_hbm, inv_ref, gh2_hbm, gw_hbm, ghid_hbm, sums_ref,
    mixed_ref, x_ref, cot_ref, w_ref, out_ref, unit_ref, gh2_ref, gw_ref,
    low_ref, turned_ref, act_ref, slope_ref, gffn_ref, gturned_ref, ghid_ref, total_ref, hsum_ref,
    in_sem, out_sem,
):
    copy_in = lambda source, target, at: pltpu.make_async_copy(source, target, in_sem.at[at])
    copy_w = lambda at: copy_in(stacked_block(w_hbm, at), w_ref.at[at], at)
    copy_mixed = copy_in(mixed_hbm, mixed_ref, 2 * blocks + 1)
    copy_x = copy_in(x_hbm, x_ref, 2 * blocks + 2)
    copy_cot = copy_in(cot_hbm, cot_ref, 2 * blocks + 3)
    copy_mixed.start()
    copy_w(2 * blocks).start()
    copy_x.start()
    for i in range(blocks):
        copy_w(i).start()
        copy_w(blocks + i).start()
    copy_cot.start()

    copy_out = lambda source, target, at: pltpu.make_async_copy(source, target, out_sem.at[at])
    copy_g = lambda at: copy_out(gw_ref.at[at], one_block(gw_hbm, at), at)
    copy_h = lambda at: copy_out(ghid_ref.at[at], ghid_hbm.at[at], 2 * blocks + at)
    copy_unit = copy_out(unit_ref, unit_hbm, 3 * blocks)
    copy_result = copy_out(out_ref, out_hbm, 3 * blocks + 1)
    copy_gh2 = copy_out(gh2_ref, gh2_hbm, 3 * blocks + 2)

    copy_mixed.wait()
    copy_w(2 * blocks).wait()
    attn = mm(mixed_ref[...], full_matrix(w_ref.at[2 * blocks]), NT)
    copy_x.wait()
    unit, inverse = norm_parts(x_ref[...].astype(F32) + attn + nv_ref[4:5])
    unit_ref[...] = unit
    copy_unit.start()
    inv_ref[...] = jnp.broadcast_to(inverse, inv_ref.shape)
    first = unit * nv_ref[0:1] + nv_ref[1:2]
    low_ref[...] = first.astype(BF)
    total_ref[...] = first + nv_ref[5:6]
    turned_ref[...] = low_ref[...].T

    def forward(i, carry):
        copy_w(i).wait()
        hidden = mm(low_ref[...], full_matrix(w_ref.at[i])) + hb_ref[i]
        bell = 0.5 * (1.0 + lax.erf(hidden * 0.7071067811865476))
        act_ref[i] = (hidden * bell).astype(BF)
        slope_ref[i] = (
            bell + hidden * (jnp.exp(hidden * hidden * -0.5) * 0.3989422804014327)
        ).astype(BF)
        copy_w(blocks + i).wait()
        total_ref[...] += mm(act_ref[i], full_matrix(w_ref.at[blocks + i]), NT)
        return carry

    lax.fori_loop(0, blocks, forward, 0, unroll=UNROLL)
    copy_cot.wait()
    unit, inverse = norm_parts(total_ref[...])
    out_ref[...] = (unit * nv_ref[2:3] + nv_ref[3:4]).astype(BF)
    copy_result.start()
    cot = cot_ref[...].astype(F32)
    gh2 = norm_back(unit, inverse, cot * nv_ref[2:3])
    gh2_ref[...] = gh2
    copy_gh2.start()
    gffn_ref[...] = gh2.astype(BF)
    for i, value in enumerate((cot * unit, cot, gh2)):
        sums_ref[i : i + 1] = jnp.sum(value, axis=0, keepdims=True)
    gturned_ref[...] = gffn_ref[...].T

    def backward(i, carry):
        gact = mm(gffn_ref[...], full_matrix(w_ref.at[blocks + i]))
        store_matrix(gw_ref.at[2 * i + 1], mm(gturned_ref[...], act_ref[i]))
        copy_g(2 * i + 1).start()
        ghid = (gact * slope_ref[i].astype(F32)).astype(BF)
        ghid_ref[i] = ghid
        copy_h(i).start()
        hsum_ref[i] = jnp.sum(ghid.astype(F32), axis=0, keepdims=True)
        store_matrix(gw_ref.at[2 * i], mm(turned_ref[...], ghid_ref[i]))
        copy_g(2 * i).start()
        return carry

    lax.fori_loop(0, blocks, backward, 0, unroll=UNROLL)
    for i in range(blocks):
        sums_ref[3 + i : 4 + i] = hsum_ref[i]
    copy_unit.wait()
    copy_result.wait()
    copy_gh2.wait()
    for i in range(blocks):
        copy_h(i).wait()
        copy_g(2 * i).wait()
        copy_g(2 * i + 1).wait()


def stacked_block(ref, at):
    return ref.at[at] if ref.shape[1] == 2 else ref.at[:, at]


def one_matrix(shape):
    return shape[1:] if shape[1] == 2 else shape[:1] + shape[2:]


def mlp(mixed, w_feed, x, nv, hb, cot, lines, rows):
    length, width = x.shape
    blocks = hb.shape[0]
    token = lambda d, *lead: jax.ShapeDtypeStruct((*lead, length, width), d)
    full = grad_shape(2 * blocks, lines, rows, width // 2)
    one_g = full[:2] + full[3:] if len(full) == 5 else full[1:]
    buffer = lambda d, *lead: pltpu.VMEM((*lead, length, width), d)
    anywhere = pl.BlockSpec(memory_space=pl.ANY)
    side = pltpu.VMEM((width, length), BF)
    return pl.pallas_call(
        functools.partial(mlp_kernel, blocks),
        grid=(1,),
        in_specs=[held(nv.shape), held(hb.shape)] + [anywhere] * 4,
        out_specs=[
            anywhere, anywhere, whole((length, 128)), anywhere, anywhere, anywhere,
            whole((3 + blocks, width)),
        ],
        out_shape=[
            token(BF), token(F32), jax.ShapeDtypeStruct((length, 128), F32), token(F32),
            jax.ShapeDtypeStruct(full, BF), token(BF, blocks),
            jax.ShapeDtypeStruct((3 + blocks, width), F32),
        ],
        scratch_shapes=[
            buffer(BF), buffer(BF), buffer(BF),
            pltpu.VMEM((2 * blocks + 1, *one_matrix(w_feed.shape)), BF),
            buffer(BF), buffer(F32), buffer(F32), pltpu.VMEM((2 * blocks, *one_g), BF),
            buffer(BF), side, buffer(BF, blocks), buffer(BF, blocks), buffer(BF), side,
            buffer(BF, blocks), buffer(F32), pltpu.VMEM((blocks, 1, width), F32),
            pltpu.SemaphoreType.DMA((2 * blocks + 4,)), pltpu.SemaphoreType.DMA((3 * blocks + 3,)),
        ],
        compiler_params=params(VMEM_MB),
        cost_estimate=cost(23),
        name="mlp",
    )(nv, hb, mixed, x, cot, w_feed)


def norm_down_kernel(
    blocks, nv_ref, inv_ref, unit_hbm, gh2_hbm, ghid_hbm, w_hbm,
    gh1_ref, gattn_ref, gmixed_ref, sums_ref,
    unit_ref, total_ref, ghid_ref, w_ref, sem,
):
    copy_in = lambda source, target, at: pltpu.make_async_copy(source, target, sem.at[at])
    copy_h = lambda i: copy_in(ghid_hbm.at[i], ghid_ref.at[i], i)
    copy_w = lambda i: copy_in(stacked_block(w_hbm, i), w_ref.at[i], blocks + i)
    copy_gh2 = copy_in(gh2_hbm, total_ref, 2 * blocks)
    copy_unit = copy_in(unit_hbm, unit_ref, 2 * blocks + 1)
    copy_last = copy_in(stacked_block(w_hbm, 2 * blocks), w_ref.at[blocks], 2 * blocks + 2)
    copy_gh2.start()
    for i in range(blocks):
        copy_h(i).start()
        copy_w(i).start()
    copy_unit.start()
    copy_last.start()
    copy_gh2.wait()

    def add(i, carry):
        copy_h(i).wait()
        copy_w(i).wait()
        total_ref[...] += mm(ghid_ref[i], full_matrix(w_ref.at[i]), NT)
        return carry

    lax.fori_loop(0, blocks, add, 0)
    copy_unit.wait()
    gfirst = total_ref[...]
    unit = unit_ref[...]
    gh1 = norm_back(unit, inv_ref[:, 0:1], gfirst * nv_ref[0:1])
    gh1_ref[...] = gh1
    gattn_ref[...] = gh1.astype(BF)
    copy_last.wait()
    gmixed_ref[...] = mm(gattn_ref[...], full_matrix(w_ref.at[blocks])).astype(BF)
    for i, value in enumerate((gfirst * unit, gfirst, gh1)):
        sums_ref[i : i + 1] = jnp.sum(value, axis=0, keepdims=True)


def norm_down(gh2, ghid, unit, inv, nv, w_feed):
    length, width = gh2.shape
    blocks = ghid.shape[0]
    one = whole((length, width))
    token = lambda d: jax.ShapeDtypeStruct((length, width), d)
    buffer = lambda d, *lead: pltpu.VMEM((*lead, length, width), d)
    return pl.pallas_call(
        functools.partial(norm_down_kernel, blocks),
        grid=(1,),
        in_specs=[held(nv.shape), held(inv.shape)] + [pl.BlockSpec(memory_space=pl.ANY)] * 4,
        out_specs=[one, one, one, whole((3, width))],
        out_shape=[token(F32), token(BF), token(BF), jax.ShapeDtypeStruct((3, width), F32)],
        scratch_shapes=[
            buffer(F32), buffer(F32), buffer(BF, blocks),
            pltpu.VMEM((blocks + 1, *one_matrix(w_feed.shape)), BF),
            pltpu.SemaphoreType.DMA((2 * blocks + 3,)),
        ],
        compiler_params=params(VMEM_MB),
        cost_estimate=cost(8),
        name="norm_down",
    )(nv, inv, unit, gh2, ghid, w_feed)


def attend_back_kernel(
    probs_ref, gm_ref, qc_ref, qp_ref, k_ref, v_ref, rel_ref,
    gq_ref, gk_ref, gv_ref, grel_ref, sums_ref,
    rel_acc,
):
    length, pair = gm_ref.shape
    block = ROW_BLOCK
    span = length + block
    zero = jnp.zeros((), BF)
    flip = (
        lax.broadcasted_iota(jnp.int32, (block, block), 0)
        + lax.broadcasted_iota(jnp.int32, (block, block), 1)
        == block - 1
    ).astype(F32).astype(BF)
    k = k_ref[...]
    v = v_ref[...]
    tops = range(0, length, block)
    jobs = [(top, head) for top in tops for head in range(2)]
    pick = lambda ref, top, head: jnp.where(
        lane_mask(head, (block, pair)), ref[pl.ds(top, block), :], zero
    )
    band = lambda top: pl.ds(length - block - top, span)
    gprobs = [mm(pick(gm_ref, top, head), v, NT) for top, head in jobs]
    turned_qp = {top: mm(flip, qp_ref[pl.ds(top, block), :]).astype(BF) for top in tops}
    gsums = []
    for (top, head), gprob in zip(jobs, gprobs):
        probs = probs_ref[head, pl.ds(top, block), :].astype(F32)
        product = probs * gprob
        inner = jnp.sum(product, axis=1, keepdims=True)
        gsums.append((product - probs * inner).astype(BF))
    wides = []
    for gsum in gsums:
        wide = jnp.concatenate([mm(flip, gsum), jnp.zeros((block, block), F32)], axis=1)
        wides.append(pltpu.roll(wide, 0, 1, stride=1, stride_axis=0).astype(BF))
    gk = gv = None
    gqc, gqp = {}, {}
    for (top, head), gsum in zip(jobs, gsums):
        tall = lane_mask(head, (length, pair))
        a = mm(gsum, jnp.where(tall, k, zero))
        gqc[top] = a if head == 0 else gqc[top] + a
        b = mm(gsum, pick(qc_ref, top, head), TN)
        c = mm(probs_ref[head, pl.ds(top, block), :], pick(gm_ref, top, head), TN)
        gk = b if gk is None else gk + b
        gv = c if gv is None else gv + c
    rel_acc[...] = jnp.zeros_like(rel_acc)
    for (top, head), wide in zip(jobs, wides):
        rel = jnp.where(lane_mask(head, (span, pair)), rel_ref[band(top), :], zero)
        d = mm(wide, rel)
        gqp[top] = d if head == 0 else gqp[top] + d
        mask = lane_mask(head, (block, pair))
        rel_acc[band(top), :] += mm(wide, jnp.where(mask, turned_qp[top], zero), TN)
    sum_c = sum_p = None
    for top in tops:
        c, p = gqc[top] * SCALE, gqp[top] * SCALE
        high = p.astype(BF)
        rest = (p - high.astype(F32)).astype(BF)
        straight = mm(flip, high) + mm(flip, rest)
        gq_ref[pl.ds(top, block), :] = (c + straight).astype(BF)
        e = jnp.sum(c, axis=0, keepdims=True)
        f = jnp.sum(p, axis=0, keepdims=True)
        sum_c = e if sum_c is None else sum_c + e
        sum_p = f if sum_p is None else sum_p + f
    gk_ref[...] = gk.astype(BF)
    gv_ref[...] = gv.astype(BF)
    grel_ref[...] = rel_acc[...].astype(BF)
    sums_ref[0:1] = sum_c
    sums_ref[1:2] = sum_p


def attend_back(probs, gm, qc, qp, k, v, rel):
    length, width = qc.shape
    pair = 2 * HEAD_FEATURES
    heads = width // HEAD_FEATURES
    column = pl.BlockSpec((length, pair), lambda p: (0, p))
    tall = pl.BlockSpec((rel.shape[0], pair), lambda p: (0, p))
    token = jax.ShapeDtypeStruct((length, width), BF)
    return pl.pallas_call(
        attend_back_kernel,
        grid=(heads // 2,),
        in_specs=[pl.BlockSpec((2, length, length), lambda p: (p, 0, 0))] + [column] * 5 + [tall],
        out_specs=[column, column, column, tall, pl.BlockSpec((2, pair), lambda p: (0, p))],
        out_shape=[
            token, token, token,
            jax.ShapeDtypeStruct(rel.shape, BF),
            jax.ShapeDtypeStruct((2, width), F32),
        ],
        scratch_shapes=[pltpu.VMEM((rel.shape[0], pair), F32)],
        compiler_params=params(VMEM_MB),
        cost_estimate=cost(28),
        name="attend_back",
    )(probs, gm, qc, qp, k, v, rel)


def project_back_kernel(
    core_ref, x_ref, gq_ref, gk_ref, gv_ref, grel_ref, sine_ref, gattn_ref, mixed_ref, *refs,
):
    *gw_refs, turned_ref = refs
    step = pl.program_id(0)

    def store(value):
        if len(gw_refs) == 2:
            store_split(*gw_refs, core_ref[0], value)
        else:
            store_matrix(gw_refs[0], value)

    @pl.when(step == 0)
    def _():
        turned_ref[...] = x_ref[...].T

    for which, g_ref in enumerate((gq_ref, gk_ref, gv_ref)):

        @pl.when(step == which)
        def _():
            store(mm(turned_ref[...], g_ref[...]))

    @pl.when(step == 3)
    def _():
        store(mm(sine_ref[...], grel_ref[...], TN))

    @pl.when(step == 4)
    def _():
        store(mm(gattn_ref[...], mixed_ref[...], TN))


def project_back(core, x, gq, gk, gv, grel, sine, gattn, mixed, lines, rows):
    length, width = x.shape
    one = held((length, width))
    if layered(lines, rows):
        shapes = [(len(SQUARE), lines, 5, rows, width // 2)] * 2
    else:
        shapes = [grad_shape(5, lines, rows, width // 2)]
    return pl.pallas_call(
        project_back_kernel,
        grid=(5,),
        in_specs=[
            pl.BlockSpec(memory_space=pltpu.SMEM),
            one, one, one, one, held(grel.shape), held(sine.shape), one, one,
        ],
        out_specs=[grad_spec(shape) for shape in shapes],
        out_shape=[jax.ShapeDtypeStruct(shape, BF) for shape in shapes],
        scratch_shapes=[pltpu.VMEM((width, length), BF)],
        compiler_params=params(VMEM_MB),
        cost_estimate=cost(9),
        name="project_back",
    )(core, x, gq, gk, gv, grel, sine, gattn, mixed)


def token_grad_kernel(gq_ref, gk_ref, gv_ref, w_ref, gh1_ref, gtok_ref):
    total = gh1_ref[...]
    for i, g_ref in enumerate((gq_ref, gk_ref, gv_ref)):
        total += mm(g_ref[...], full_matrix(w_ref.at[i]), NT)
    gtok_ref[...] = total


def token_grad(gq, gk, gv, w, gh1):
    one = whole(gq.shape)
    return pl.pallas_call(
        token_grad_kernel,
        grid=(1,),
        in_specs=[one, one, one, whole((3,) + w.shape[1:]), one],
        out_specs=one,
        out_shape=jax.ShapeDtypeStruct(gq.shape, F32),
        compiler_params=params(VMEM_MB),
        cost_estimate=cost(6),
        name="token_grad",
    )(gq, gk, gv, w, gh1)


def swap_x(value):
    return lax.ppermute(value, "mp", [(0, 1), (1, 0)])


def swap_dp(value, bit):
    return lax.ppermute(value, "dp", [(d, d ^ bit) for d in range(lax.axis_size("dp"))])


def shift_line(value, step):
    dp = lax.axis_size("dp")
    return lax.ppermute(value, "dp", [(d, (d + 4 * step) % dp) for d in range(dp)])


def gather_matrices(shard):
    dp = lax.axis_size("dp")
    if shard.shape[1] % 16 == 0:
        order = [mp * dp + index for mp, index in ring_order(dp // 4)]
        return lax.all_gather(
            shard, ("mp", "dp"), axis=0, axis_index_groups=[order], tiled=False
        )
    pieces = lax.all_gather(shard, ("mp", "dp"), axis=0, tiled=False)
    return whole_matrices(pieces.reshape((2, dp) + shard.shape))


def whole_matrices(pieces):
    mp, dp, blocks, rows, columns = pieces.shape
    return pieces.transpose(2, 0, 1, 3, 4).reshape(blocks, mp, dp * rows, columns)


def gather_lines(shard, others):
    lines = lax.axis_size("dp") // 4
    if lines != 4 or shard.shape[1] % 16 != 0:
        return shard, others
    near = [shard] + [shift_line(shard, step) for step in range(1, lines)]
    near, others = lax.optimization_barrier((near, others))
    return jnp.stack(near), others


def gather_stepwise(near, shard):
    dp = lax.axis_size("dp")
    blocks, rows, columns = shard.shape
    lines = dp // 4
    if lines != 4 or rows % 16 != 0:
        pieces = lax.all_gather(shard, ("mp", "dp"), axis=0, tiled=False)
        return (whole_matrices(pieces.reshape((2, dp) + shard.shape)),)
    cut = blocks // 2
    one, two = near[:, :cut], near[:, cut:]
    one_x = swap_x(one)
    two_y = swap_dp(two, 2)
    one_y = swap_dp(one, 2)
    two_x = swap_x(two)
    one_xy = swap_dp(one_x, 2)
    two_xy = swap_x(two_y)
    lane = [one, two, one_x, two_y, one_y, two_x, one_xy, two_xy]
    return tuple(lane + [swap_dp(part, 1) for part in lane])


def own_place():
    index = lax.axis_index("dp")
    place = jnp.stack([lax.axis_index("mp"), index // 4, (index // 2) % 2, index % 2])
    return place.astype(jnp.int32)


def plane_groups(dp):
    return [
        [mp * dp + line * 4 + y * 2 + core for mp, y, core in RING] for line in range(dp // 4)
    ]


def line_groups(dp):
    return [
        [mp * dp + line * 4 + low for line in range(dp // 4)] for mp in range(2) for low in range(4)
    ]


def scatter_plane(grads):
    dp = lax.axis_size("dp")
    if grads.ndim == 4:
        blocks, _, all_rows, columns = grads.shape
        grads = grads.reshape(blocks, 2, dp // 4, 2, 2, all_rows // dp, columns)
        grads = jnp.stack([grads[:, mp, :, y, core] for mp, y, core in RING])
        grads = grads.transpose(0, 2, 1, 3, 4)
    return lax.psum_scatter(
        grads, ("mp", "dp"), scatter_dimension=0, axis_index_groups=plane_groups(dp), tiled=False
    )


def scatter_square(keep, send, before):
    dp = lax.axis_size("dp")
    grads = (keep.astype(F32) + swap_dp(send, 1).astype(F32)).astype(BF)
    grads, before = lax.optimization_barrier((grads, before))
    groups = [
        [mp * dp + line * 4 + y * 2 + core for mp, y in SQUARE]
        for line in range(dp // 4)
        for core in range(2)
    ]
    part = lax.psum_scatter(
        grads, ("mp", "dp"), scatter_dimension=0, axis_index_groups=groups, tiled=False
    )
    return part, before


def line_pieces(part):
    dp = lax.axis_size("dp")
    lines = dp // 4
    if lines != 4:
        return [part]
    line = lax.axis_index("dp") // 4
    return [
        lax.dynamic_index_in_dim(part, (line + step) % lines, 0, keepdims=False)
        for step in range(lines)
    ]


def trade_pieces(pieces):
    dp = lax.axis_size("dp")
    if len(pieces) == 1:
        return [
            lax.psum_scatter(
                pieces[0], ("mp", "dp"), scatter_dimension=0, axis_index_groups=line_groups(dp),
                tiled=False,
            )
        ]
    return [pieces[0]] + [shift_line(pieces[step], step) for step in range(1, len(pieces))]


def sum_plane(value, meanwhile):
    value = value + swap_dp(value, 1)
    value = value + swap_x(value)
    value, *meanwhile = lax.optimization_barrier((value, *meanwhile))
    return value + swap_dp(value, 2), meanwhile


def sum_line(value):
    lines = lax.axis_size("dp") // 4
    if lines != 4:
        return lax.psum(value, ("dp",), axis_index_groups=line_only(lines))
    total = value
    for piece in [shift_line(value, step) for step in range(1, lines)]:
        total = total + piece
    return total


def line_only(lines):
    return [[line * 4 + low for line in range(lines)] for low in range(4)]


def adam_kernel(order, count, *refs):
    pieces = refs[:count]
    p_ref, one_ref, two_ref = refs[count : count + 3]
    outs = refs[-3:]
    for block, at in enumerate(order):
        grad = pieces[0][block].astype(F32)
        for piece in pieces[1:]:
            grad = grad + piece[block].astype(F32)
        results = adam_update(p_ref[at], grad, one_ref[at], two_ref[at], RATE_BIG)
        for out, result in zip(outs, results):
            out[at] = result


def adam_blocks(pieces, order, param, one, two, done):
    blocks, rows, columns = pieces[0].shape
    shape = jax.ShapeDtypeStruct(param.shape, F32)
    part = whole((blocks, rows, columns) if done else param.shape)
    if done:
        param, one, two = param[:blocks], one[:blocks], two[:blocks]
    count = len(pieces)
    return pl.pallas_call(
        functools.partial(adam_kernel, order, count),
        grid=(1,),
        in_specs=[whole(pieces[0].shape)] * count
        + [part] * 3
        + [pl.BlockSpec(memory_space=pl.ANY)] * len(done),
        out_specs=[part] * 3,
        out_shape=[shape] * 3,
        input_output_aliases={count + 3 + i: i for i in range(len(done))},
        compiler_params=params(ADAM_MB),
        cost_estimate=cost(blocks // 2),
        name="adam",
    )(*pieces, param, one, two, *done)


def per_device(
    tokens,
    lengths,
    weights,
    weight_m1,
    weight_m2,
    head_vecs,
    head_m1,
    head_m2,
    norm_vecs,
    norm_m1,
    norm_m2,
    cotangent,
):
    mp_index = lax.axis_index("mp")
    seq_len = cotangent.shape[0]
    weight_rows = weights.shape[0]
    local_width = weights.shape[2]
    model_width = tokens.shape[1]
    lines = lax.axis_size("dp") // 4
    x = lax.dynamic_slice_in_dim(tokens, mp_index * seq_len, seq_len, 0)
    used = lax.dynamic_slice_in_dim(lengths, mp_index, 1, 0)
    sine = relative_embedding(seq_len, model_width).astype(BF)
    shard = weights.transpose(1, 0, 2)
    shard_low = shard.astype(BF)
    heads_all = lax.all_gather(head_vecs, "mp", axis=1, tiled=True)
    w_feed = gather_matrices(jnp.concatenate([shard_low[5:13], shard_low[4:5]]))
    near, (x, sine, heads_all) = gather_lines(shard_low[0:4], (x, sine, heads_all))
    parts = gather_stepwise(near, shard_low[0:4])

    qc, qp, k, v, rel, w = project_parts(x, parts, heads_all[0:2], sine, own_place())
    probs, mixed = attend(used, qc, qp, k, v, rel)
    hb = heads_all[2:6].reshape(4, 1, model_width)
    out, unit, inv, gh2, gw_feed, ghid, sums2 = mlp(
        mixed, w_feed, x, norm_vecs, hb, cotangent, lines, weight_rows
    )
    part_feed = scatter_plane(gw_feed)
    gh1, gattn, gmixed, sums1 = norm_down(gh2, ghid, unit, inv, norm_vecs, w_feed)
    gq, gk, gv, grel, sums_q = attend_back(probs, gmixed, qc, qp, k, v, rel)
    small = sum_line(jnp.concatenate([sums2, sums1, sums_q], axis=0))
    place = own_place()
    gproj = project_back(
        place[3:4], x, gq, gk, gv, grel, sine, gattn, mixed, lines, weight_rows
    )
    *gproj, small = lax.optimization_barrier((*gproj, small))
    if len(gproj) == 2:
        part_proj, part_feed = scatter_square(*gproj, part_feed)
    else:
        gproj, part_feed = lax.optimization_barrier((gproj[0], part_feed))
        part_proj = scatter_plane(gproj)

    pieces_feed = line_pieces(part_feed)
    *pieces_feed, gq = lax.optimization_barrier((*pieces_feed, gq))
    grad_tokens = token_grad(gq, gk, gv, w, gh1)
    pieces_feed = trade_pieces(pieces_feed)
    small, grad_tokens = lax.optimization_barrier((small, grad_tokens))
    small, pieces_feed = sum_plane(small, pieces_feed)
    norm_grad = jnp.concatenate([small[7:9], small[0:2], small[9:10], small[2:3]], axis=0)
    head_grad = jnp.concatenate([small[10:12], small[3:7]], axis=0)
    head_grad = lax.dynamic_slice_in_dim(head_grad, mp_index * local_width, local_width, 1)
    state = (shard, weight_m1.transpose(1, 0, 2), weight_m2.transpose(1, 0, 2))
    done = adam_blocks(pieces_feed, (5, 9, 6, 10, 7, 11, 8, 12), *state, ())
    small, norm_grad, done, part_proj = lax.optimization_barrier((small, norm_grad, done, part_proj))
    pieces_proj = trade_pieces(line_pieces(part_proj))
    new_big = adam_blocks(pieces_proj, tuple(range(5)), *state, done)
    new_weights, new_weight_m1, new_weight_m2 = [a.transpose(1, 0, 2) for a in new_big]
    new_head, new_head_m1, new_head_m2 = adam_update(
        head_vecs, head_grad, head_m1, head_m2, RATE_SMALL
    )
    new_norm, new_norm_m1, new_norm_m2 = adam_update(
        norm_vecs, norm_grad, norm_m1, norm_m2, RATE_SMALL
    )
    return (
        out,
        grad_tokens,
        new_weights,
        new_weight_m1,
        new_weight_m2,
        new_head,
        new_head_m1,
        new_head_m2,
        new_norm,
        new_norm_m1,
        new_norm_m2,
    )


def solution(mesh):
    shard = P("dp", None, "mp")
    return jax.shard_map(
        per_device,
        mesh=mesh,
        in_specs=(P("dp", None), P("dp"), shard, shard, shard)
        + (P(None, "mp"),) * 3
        + (P(),) * 3
        + (P(("dp", "mp"), None),),
        out_specs=(P(("dp", "mp"), None),) * 2
        + (shard,) * 3
        + (P(None, "mp"),) * 3
        + (P(),) * 3,
        check_vma=False,
    )
```

```python
import functools

import jax
import jax.numpy as jnp
from jax import lax
from jax.experimental import pallas as pl
from jax.experimental.pallas import tpu as pltpu
from jax.sharding import PartitionSpec as P

HEAD_FEATURES = 64
STEP = 5
EPS_NORM = 1e-05
EPS_ADAM = 1e-08
BETA_ONE = 0.5
BETA_TWO = 0.5
RATE_BIG = 0.03
RATE_SMALL = 0.2
DECAY = 0.01
MASKED = -1e30
SCALE = HEAD_FEATURES ** (-0.5)
ROW_BLOCK = 256
VMEM_MB = 56
ADAM_MB = 16
UNROLL = 1
BF = jnp.bfloat16
F32 = jnp.float32

NN = (((1,), (0,)), ((), ()))
NT = (((1,), (1,)), ((), ()))
TN = (((0,), (0,)), ((), ()))


def mm(a, b, dims=NN):
    return lax.dot_general(a, b, dims, preferred_element_type=F32)


def whole(shape):
    return pl.BlockSpec(shape, lambda *_: (0,) * len(shape))


def held(shape):
    return pl.BlockSpec(shape, lambda *_: (0,) * len(shape), pipeline_mode=pl.Buffered(1))


def params(mebibytes):
    return pltpu.CompilerParams(vmem_limit_bytes=mebibytes * 1024 * 1024)


def cost(micros):
    return pl.CostEstimate(flops=int(micros * 1e9), bytes_accessed=0, transcendentals=0)


def relative_embedding(length, model_width):
    distance = (length - 1 - jnp.arange(2 * length)).astype(F32)
    freq_index = jnp.arange(model_width // 2).astype(F32)
    inverse = 1.0 / 10000.0 ** (2.0 * freq_index / model_width)
    angles = distance[:, None] * inverse[None, :]
    return jnp.concatenate([jnp.sin(angles), jnp.cos(angles)], axis=1)


def adam_update(param, grad_sum, moment_one, moment_two, rate):
    new_one = BETA_ONE * moment_one + (1.0 - BETA_ONE) * grad_sum
    new_two = BETA_TWO * moment_two + (1.0 - BETA_TWO) * grad_sum * grad_sum
    corrected_one = new_one / (1.0 - BETA_ONE**STEP)
    corrected_two = new_two / (1.0 - BETA_TWO**STEP)
    new_param = param - rate * (
        corrected_one / (jnp.sqrt(corrected_two) + EPS_ADAM) + DECAY * param
    )
    return (new_param, new_one, new_two)


def weight_spec(shape, which, each=None):
    if shape[1] != 2:
        return pl.BlockSpec((shape[0], each) + shape[2:], lambda b: (0, which(b), 0, 0))
    return pl.BlockSpec((each,) + shape[1:], lambda b: (which(b), 0, 0, 0))


def one_block(ref, index):
    if len(ref.shape) == 5:
        return ref.at[:, :, index]
    return ref.at[:, index] if ref.shape[0] > 8 else ref.at[index]


def ring_order(lines):
    order = []
    for turn, (mp, y) in enumerate(((0, 0), (0, 1), (1, 1), (1, 0))):
        for line in range(lines) if turn % 2 == 0 else reversed(range(lines)):
            order += [(mp, line * 4 + y * 2), (mp, line * 4 + y * 2 + 1)]
    return order


def full_matrix(w_ref):
    if len(w_ref.shape) == 3 and w_ref.shape[0] > 2:
        places = w_ref.shape[0]
        order = ring_order(places // 8)
        sides = [
            jnp.concatenate([w_ref[order.index((mp, dp))] for dp in range(places // 2)], axis=0)
            for mp in range(2)
        ]
        return jnp.concatenate(sides, axis=1)
    return jnp.concatenate([w_ref[0], w_ref[1]], axis=1)


RING = ((0, 0, 0), (0, 0, 1), (0, 1, 0), (0, 1, 1), (1, 1, 0), (1, 1, 1), (1, 0, 0), (1, 0, 1))


SQUARE = ((0, 0), (0, 1), (1, 1), (1, 0))


def layered(lines, rows):
    return rows % 16 == 0


def grad_shape(blocks, lines, rows, columns):
    if layered(lines, rows):
        return (len(RING), lines, blocks, rows, columns)
    return (blocks, 2, lines * 4 * rows, columns)


def grad_spec(shape):
    if len(shape) == 5:
        return pl.BlockSpec(shape[:2] + (None,) + shape[3:], lambda b: (0, 0, b, 0, 0))
    return pl.BlockSpec((None,) + shape[1:], lambda b: (b, 0, 0, 0))


def store_matrix(out_ref, value):
    half = value.shape[1] // 2
    low = value.astype(BF)
    if len(out_ref.shape) == 3:
        out_ref[0] = low[:, :half]
        out_ref[1] = low[:, half:]
        return
    places, lines, rows, _ = out_ref.shape
    for place, (mp, y, core) in enumerate(RING):
        for line in range(lines):
            top = (line * 4 + y * 2 + core) * rows
            out_ref[place, line] = low[top : top + rows, mp * half : (mp + 1) * half]


def store_split(keep_ref, send_ref, core, value):
    half = value.shape[1] // 2
    low = value.astype(BF)
    places, lines, rows, _ = keep_ref.shape
    for place, (mp, y) in enumerate(SQUARE):
        for line in range(lines):
            top = (line * 4 + y * 2) * rows
            columns = slice(mp * half, (mp + 1) * half)
            lower, upper = low[top : top + rows, columns], low[top + rows : top + 2 * rows, columns]
            keep_ref[place, line] = jnp.where(core == 0, lower, upper)
            send_ref[place, line] = jnp.where(core == 0, upper, lower)


def round_kernel(shard_ref, low_ref, feed_ref):
    low_ref[...] = shard_ref[0:4].astype(BF)
    feed_ref[0:8] = shard_ref[5:13].astype(BF)
    feed_ref[8] = shard_ref[4].astype(BF)


def round_shard(shard):
    rest = shard.shape[1:]
    return pl.pallas_call(
        round_kernel,
        grid=(1,),
        in_specs=[whole(shard.shape)],
        out_specs=[whole((4,) + rest), whole((9,) + rest)],
        out_shape=[jax.ShapeDtypeStruct((n,) + rest, BF) for n in (4, 9)],
        compiler_params=params(16),
        cost_estimate=cost(1),
        name="round_shard",
    )(shard)


def project_kernel(x_ref, w_ref, vec_ref, sine_ref, qc_ref, qp_ref, k_ref, v_ref, rel_ref):
    step = pl.program_id(0)

    @pl.when(step == 0)
    def _():
        q = mm(x_ref[...], full_matrix(w_ref))
        qc_ref[...] = (q + vec_ref[0:1]).astype(BF) * BF(SCALE)
        qp_ref[...] = (q + vec_ref[1:2]).astype(BF) * BF(SCALE)

    @pl.when(step == 1)
    def _():
        k_ref[...] = mm(x_ref[...], full_matrix(w_ref)).astype(BF)

    @pl.when(step == 2)
    def _():
        v_ref[...] = mm(x_ref[...], full_matrix(w_ref)).astype(BF)

    @pl.when(step == 3)
    def _():
        rel_ref[...] = mm(sine_ref[...], full_matrix(w_ref)).astype(BF)


def project(x, w, vecs, sine):
    length, width = x.shape
    rows = sine.shape[0]
    shapes = [(length, width)] * 4 + [(rows, width)]
    return pl.pallas_call(
        project_kernel,
        grid=(4,),
        in_specs=[
            whole(x.shape),
            weight_spec(w.shape, lambda b: b),
            whole(vecs.shape),
            whole(sine.shape),
        ],
        out_specs=[whole(s) for s in shapes],
        out_shape=[jax.ShapeDtypeStruct(s, BF) for s in shapes],
        compiler_params=params(VMEM_MB),
        cost_estimate=cost(9),
        name="project",
    )(x, w, vecs, sine)


PARTS = [
    (half, dx, dy, dc)
    for dc in (0, 1)
    for half, dx, dy in (
        (0, 0, 0), (1, 0, 0), (0, 1, 0), (1, 0, 1), (0, 0, 1), (1, 1, 0), (0, 1, 1), (1, 1, 1),
    )
]


def project_parts_kernel(
    cut, place_ref, x_ref, vec_ref, sine_ref, *refs,
):
    parts = refs[: len(PARTS)]
    outs = refs[len(PARTS) : len(PARTS) + 6]
    buffers = refs[len(PARTS) + 6 : len(PARTS) + 12]
    in_sem, out_sem = refs[-2:]
    w_ref = buffers[5]
    mp, line, y, core = (place_ref[i] for i in range(4))
    lines, _, rows, _ = parts[0].shape
    arriving = ([], [])
    for index, (half, dx, dy, dc) in enumerate(PARTS):
        for step in range(lines):
            at = lax.rem(line + lines - step, lines) * 4 + (y ^ dy) * 2 + (core ^ dc)
            start = pl.multiple_of(at * rows, rows)
            arriving[half].append(
                pltpu.make_async_copy(
                    parts[index].at[step],
                    w_ref.at[pl.ds(half * cut, cut), mp ^ dx, pl.ds(start, rows)],
                    in_sem.at[index * lines + step],
                )
            )
    for copy in arriving[0] + arriving[1]:
        copy.start()
    leaving = []

    def leave(source, target):
        copy = pltpu.make_async_copy(source, target, out_sem.at[len(leaving)])
        copy.start()
        leaving.append(copy)

    for copy in arriving[0]:
        copy.wait()
    leave(w_ref.at[0:2], outs[5].at[0:2])
    q = mm(x_ref[...], full_matrix(w_ref.at[0]))
    buffers[0][...] = (q + vec_ref[0:1]).astype(BF) * BF(SCALE)
    leave(buffers[0], outs[0])
    buffers[1][...] = (q + vec_ref[1:2]).astype(BF) * BF(SCALE)
    leave(buffers[1], outs[1])
    buffers[2][...] = mm(x_ref[...], full_matrix(w_ref.at[1])).astype(BF)
    leave(buffers[2], outs[2])
    for copy in arriving[1]:
        copy.wait()
    leave(w_ref.at[2:3], outs[5].at[2:3])
    buffers[4][...] = mm(sine_ref[...], full_matrix(w_ref.at[3])).astype(BF)
    leave(buffers[4], outs[4])
    buffers[3][...] = mm(x_ref[...], full_matrix(w_ref.at[2])).astype(BF)
    leave(buffers[3], outs[3])
    for copy in leaving:
        copy.wait()


def project_parts(x, parts, vecs, sine, place):
    if len(parts) == 1:
        return [*project(x, parts[0], vecs, sine), parts[0]]
    length, width = x.shape
    lines, cut, rows, columns = parts[0].shape
    shapes = [(length, width)] * 4 + [sine.shape]
    matrix = (2, lines * 4 * rows, columns)
    anywhere = pl.BlockSpec(memory_space=pl.ANY)
    return pl.pallas_call(
        functools.partial(project_parts_kernel, cut),
        grid=(1,),
        in_specs=[
            pl.BlockSpec(memory_space=pltpu.SMEM), held(x.shape), held(vecs.shape), held(sine.shape),
        ]
        + [anywhere] * len(parts),
        out_specs=[anywhere] * 6,
        out_shape=[jax.ShapeDtypeStruct(shape, BF) for shape in shapes + [(3,) + matrix]],
        scratch_shapes=[pltpu.VMEM(shape, BF) for shape in shapes + [(4,) + matrix]]
        + [pltpu.SemaphoreType.DMA((len(parts) * lines,)), pltpu.SemaphoreType.DMA((7,))],
        compiler_params=params(VMEM_MB),
        cost_estimate=cost(9),
        name="project",
    )(place, x, vecs, sine, *parts)


def lane_mask(which, shape):
    lanes = lax.broadcasted_iota(jnp.int32, shape, 1)
    return (lanes >= HEAD_FEATURES) if which else (lanes < HEAD_FEATURES)


def attend_kernel(len_ref, qc_ref, qp_ref, k_ref, v_ref, rel_ref, probs_ref, mixed_ref):
    length = qc_ref.shape[0]
    block = ROW_BLOCK
    pair = qc_ref.shape[1]
    valid = lax.broadcasted_iota(jnp.int32, (1, length), 1) < len_ref[0]
    k = k_ref[...]
    v = v_ref[...]
    zero = jnp.zeros((), BF)
    span = length + block
    jobs = [(top, head) for top in range(0, length, block) for head in range(2)]
    raw = []
    for top, head in jobs:
        rows = pl.ds(top, block)
        first = length - block - top
        mask = lane_mask(head, (block, pair))
        content = mm(jnp.where(mask, qc_ref[rows, :], zero), k, NT)
        place = mm(jnp.where(mask, qp_ref[rows, :], zero), rel_ref[first : first + span, :], NT)
        raw.append((content, place))
    for (top, head), (content, place) in zip(jobs, raw):
        place = pltpu.roll(place, span - (block - 1), 1, stride=1, stride_axis=0)
        scores = jnp.where(valid, content + place[:, :length], MASKED)
        top_score = jnp.max(scores, axis=1, keepdims=True)
        grown = jnp.exp(scores - top_score)
        probs = grown * (1.0 / jnp.sum(grown, axis=1, keepdims=True))
        probs_ref[head, pl.ds(top, block), :] = probs.astype(BF)
    for top in range(0, length, block):
        rows = pl.ds(top, block)
        lower, upper = mm(probs_ref[0, rows, :], v), mm(probs_ref[1, rows, :], v)
        mixed_ref[rows, :] = jnp.where(lane_mask(1, (block, pair)), upper, lower).astype(BF)


def attend(length_used, qc, qp, k, v, rel):
    length, width = qc.shape
    pair = 2 * HEAD_FEATURES
    heads = width // HEAD_FEATURES
    column = pl.BlockSpec((length, pair), lambda p: (0, p))
    return pl.pallas_call(
        attend_kernel,
        grid=(heads // 2,),
        in_specs=[pl.BlockSpec(memory_space=pltpu.SMEM)]
        + [column] * 4
        + [pl.BlockSpec((rel.shape[0], pair), lambda p: (0, p))],
        out_specs=[pl.BlockSpec((2, length, length), lambda p: (p, 0, 0)), column],
        out_shape=[
            jax.ShapeDtypeStruct((heads, length, length), BF),
            jax.ShapeDtypeStruct((length, width), BF),
        ],
        compiler_params=params(VMEM_MB),
        cost_estimate=cost(19),
        name="attend",
    )(length_used, qc, qp, k, v, rel)


def norm_parts(rows):
    mean = jnp.mean(rows, axis=1, keepdims=True)
    centred = rows - mean
    spread = jnp.mean(centred * centred, axis=1, keepdims=True)
    inverse = lax.rsqrt(spread + EPS_NORM)
    return centred * inverse, inverse


def norm_back(unit, inverse, scaled):
    return (
        scaled
        - jnp.mean(scaled, axis=1, keepdims=True)
        - unit * jnp.mean(scaled * unit, axis=1, keepdims=True)
    ) * inverse


def mlp_kernel(
    blocks, nv_ref, hb_ref, mixed_hbm, x_hbm, cot_hbm, w_hbm,
    out_hbm, unit_hbm, inv_ref, gh2_hbm, gw_hbm, ghid_hbm, sums_ref,
    mixed_ref, x_ref, cot_ref, w_ref, out_ref, unit_ref, gh2_ref, gw_ref,
    low_ref, turned_ref, act_ref, slope_ref, gffn_ref, gturned_ref, ghid_ref, total_ref, hsum_ref,
    in_sem, out_sem,
):
    copy_in = lambda source, target, at: pltpu.make_async_copy(source, target, in_sem.at[at])
    copy_w = lambda at: copy_in(stacked_block(w_hbm, at), w_ref.at[at], at)
    copy_mixed = copy_in(mixed_hbm, mixed_ref, 2 * blocks + 1)
    copy_x = copy_in(x_hbm, x_ref, 2 * blocks + 2)
    copy_cot = copy_in(cot_hbm, cot_ref, 2 * blocks + 3)
    copy_mixed.start()
    copy_w(2 * blocks).start()
    copy_x.start()
    for i in range(blocks):
        copy_w(i).start()
        copy_w(blocks + i).start()
    copy_cot.start()

    copy_out = lambda source, target, at: pltpu.make_async_copy(source, target, out_sem.at[at])
    copy_g = lambda at: copy_out(gw_ref.at[at], one_block(gw_hbm, at), at)
    copy_h = lambda at: copy_out(ghid_ref.at[at], ghid_hbm.at[at], 2 * blocks + at)
    copy_unit = copy_out(unit_ref, unit_hbm, 3 * blocks)
    copy_result = copy_out(out_ref, out_hbm, 3 * blocks + 1)
    copy_gh2 = copy_out(gh2_ref, gh2_hbm, 3 * blocks + 2)

    copy_mixed.wait()
    copy_w(2 * blocks).wait()
    attn = mm(mixed_ref[...], full_matrix(w_ref.at[2 * blocks]), NT)
    copy_x.wait()
    unit, inverse = norm_parts(x_ref[...].astype(F32) + attn + nv_ref[4:5])
    unit_ref[...] = unit
    copy_unit.start()
    inv_ref[...] = jnp.broadcast_to(inverse, inv_ref.shape)
    first = unit * nv_ref[0:1] + nv_ref[1:2]
    low_ref[...] = first.astype(BF)
    total_ref[...] = first + nv_ref[5:6]
    turned_ref[...] = low_ref[...].T

    def forward(i, carry):
        copy_w(i).wait()
        hidden = mm(low_ref[...], full_matrix(w_ref.at[i])) + hb_ref[i]
        bell = 0.5 * (1.0 + lax.erf(hidden * 0.7071067811865476))
        act_ref[i] = (hidden * bell).astype(BF)
        slope_ref[i] = (
            bell + hidden * (jnp.exp(hidden * hidden * -0.5) * 0.3989422804014327)
        ).astype(BF)
        copy_w(blocks + i).wait()
        total_ref[...] += mm(act_ref[i], full_matrix(w_ref.at[blocks + i]), NT)
        return carry

    lax.fori_loop(0, blocks, forward, 0, unroll=UNROLL)
    copy_cot.wait()
    unit, inverse = norm_parts(total_ref[...])
    out_ref[...] = (unit * nv_ref[2:3] + nv_ref[3:4]).astype(BF)
    copy_result.start()
    cot = cot_ref[...].astype(F32)
    gh2 = norm_back(unit, inverse, cot * nv_ref[2:3])
    gh2_ref[...] = gh2
    copy_gh2.start()
    gffn_ref[...] = gh2.astype(BF)
    for i, value in enumerate((cot * unit, cot, gh2)):
        sums_ref[i : i + 1] = jnp.sum(value, axis=0, keepdims=True)
    gturned_ref[...] = gffn_ref[...].T

    def backward(i, carry):
        gact = mm(gffn_ref[...], full_matrix(w_ref.at[blocks + i]))
        store_matrix(gw_ref.at[2 * i + 1], mm(gturned_ref[...], act_ref[i]))
        copy_g(2 * i + 1).start()
        ghid = (gact * slope_ref[i].astype(F32)).astype(BF)
        ghid_ref[i] = ghid
        copy_h(i).start()
        hsum_ref[i] = jnp.sum(ghid.astype(F32), axis=0, keepdims=True)
        store_matrix(gw_ref.at[2 * i], mm(turned_ref[...], ghid_ref[i]))
        copy_g(2 * i).start()
        return carry

    lax.fori_loop(0, blocks, backward, 0, unroll=UNROLL)
    for i in range(blocks):
        sums_ref[3 + i : 4 + i] = hsum_ref[i]
    copy_unit.wait()
    copy_result.wait()
    copy_gh2.wait()
    for i in range(blocks):
        copy_h(i).wait()
        copy_g(2 * i).wait()
        copy_g(2 * i + 1).wait()


def stacked_block(ref, at):
    return ref.at[at] if ref.shape[1] == 2 else ref.at[:, at]


def one_matrix(shape):
    return shape[1:] if shape[1] == 2 else shape[:1] + shape[2:]


def mlp(mixed, w_feed, x, nv, hb, cot, lines, rows):
    length, width = x.shape
    blocks = hb.shape[0]
    token = lambda d, *lead: jax.ShapeDtypeStruct((*lead, length, width), d)
    full = grad_shape(2 * blocks, lines, rows, width // 2)
    one_g = full[:2] + full[3:] if len(full) == 5 else full[1:]
    buffer = lambda d, *lead: pltpu.VMEM((*lead, length, width), d)
    anywhere = pl.BlockSpec(memory_space=pl.ANY)
    side = pltpu.VMEM((width, length), BF)
    return pl.pallas_call(
        functools.partial(mlp_kernel, blocks),
        grid=(1,),
        in_specs=[held(nv.shape), held(hb.shape)] + [anywhere] * 4,
        out_specs=[
            anywhere, anywhere, whole((length, 128)), anywhere, anywhere, anywhere,
            whole((3 + blocks, width)),
        ],
        out_shape=[
            token(BF), token(F32), jax.ShapeDtypeStruct((length, 128), F32), token(F32),
            jax.ShapeDtypeStruct(full, BF), token(BF, blocks),
            jax.ShapeDtypeStruct((3 + blocks, width), F32),
        ],
        scratch_shapes=[
            buffer(BF), buffer(BF), buffer(BF),
            pltpu.VMEM((2 * blocks + 1, *one_matrix(w_feed.shape)), BF),
            buffer(BF), buffer(F32), buffer(F32), pltpu.VMEM((2 * blocks, *one_g), BF),
            buffer(BF), side, buffer(BF, blocks), buffer(BF, blocks), buffer(BF), side,
            buffer(BF, blocks), buffer(F32), pltpu.VMEM((blocks, 1, width), F32),
            pltpu.SemaphoreType.DMA((2 * blocks + 4,)), pltpu.SemaphoreType.DMA((3 * blocks + 3,)),
        ],
        compiler_params=params(VMEM_MB),
        cost_estimate=cost(23),
        name="mlp",
    )(nv, hb, mixed, x, cot, w_feed)


def norm_down_kernel(
    blocks, nv_ref, inv_ref, unit_hbm, gh2_hbm, ghid_hbm, w_hbm,
    gh1_ref, gattn_ref, gmixed_ref, sums_ref,
    unit_ref, total_ref, ghid_ref, w_ref, sem,
):
    copy_in = lambda source, target, at: pltpu.make_async_copy(source, target, sem.at[at])
    copy_h = lambda i: copy_in(ghid_hbm.at[i], ghid_ref.at[i], i)
    copy_w = lambda i: copy_in(stacked_block(w_hbm, i), w_ref.at[i], blocks + i)
    copy_gh2 = copy_in(gh2_hbm, total_ref, 2 * blocks)
    copy_unit = copy_in(unit_hbm, unit_ref, 2 * blocks + 1)
    copy_last = copy_in(stacked_block(w_hbm, 2 * blocks), w_ref.at[blocks], 2 * blocks + 2)
    copy_gh2.start()
    for i in range(blocks):
        copy_h(i).start()
        copy_w(i).start()
    copy_unit.start()
    copy_last.start()
    copy_gh2.wait()

    def add(i, carry):
        copy_h(i).wait()
        copy_w(i).wait()
        total_ref[...] += mm(ghid_ref[i], full_matrix(w_ref.at[i]), NT)
        return carry

    lax.fori_loop(0, blocks, add, 0)
    copy_unit.wait()
    gfirst = total_ref[...]
    unit = unit_ref[...]
    gh1 = norm_back(unit, inv_ref[:, 0:1], gfirst * nv_ref[0:1])
    gh1_ref[...] = gh1
    gattn_ref[...] = gh1.astype(BF)
    copy_last.wait()
    gmixed_ref[...] = mm(gattn_ref[...], full_matrix(w_ref.at[blocks])).astype(BF)
    for i, value in enumerate((gfirst * unit, gfirst, gh1)):
        sums_ref[i : i + 1] = jnp.sum(value, axis=0, keepdims=True)


def norm_down(gh2, ghid, unit, inv, nv, w_feed):
    length, width = gh2.shape
    blocks = ghid.shape[0]
    one = whole((length, width))
    token = lambda d: jax.ShapeDtypeStruct((length, width), d)
    buffer = lambda d, *lead: pltpu.VMEM((*lead, length, width), d)
    return pl.pallas_call(
        functools.partial(norm_down_kernel, blocks),
        grid=(1,),
        in_specs=[held(nv.shape), held(inv.shape)] + [pl.BlockSpec(memory_space=pl.ANY)] * 4,
        out_specs=[one, one, one, whole((3, width))],
        out_shape=[token(F32), token(BF), token(BF), jax.ShapeDtypeStruct((3, width), F32)],
        scratch_shapes=[
            buffer(F32), buffer(F32), buffer(BF, blocks),
            pltpu.VMEM((blocks + 1, *one_matrix(w_feed.shape)), BF),
            pltpu.SemaphoreType.DMA((2 * blocks + 3,)),
        ],
        compiler_params=params(VMEM_MB),
        cost_estimate=cost(8),
        name="norm_down",
    )(nv, inv, unit, gh2, ghid, w_feed)


def attend_back_kernel(
    probs_ref, gm_ref, qc_ref, qp_ref, k_ref, v_ref, rel_ref,
    gqkv_ref, grel_ref, sums_ref,
    rel_acc,
):
    length, pair = gm_ref.shape
    block = ROW_BLOCK
    span = length + block
    zero = jnp.zeros((), BF)
    flip = (
        lax.broadcasted_iota(jnp.int32, (block, block), 0)
        + lax.broadcasted_iota(jnp.int32, (block, block), 1)
        == block - 1
    ).astype(F32).astype(BF)
    k = k_ref[...]
    v = v_ref[...]
    tops = range(0, length, block)
    jobs = [(top, head) for top in tops for head in range(2)]
    pick = lambda ref, top, head: jnp.where(
        lane_mask(head, (block, pair)), ref[pl.ds(top, block), :], zero
    )
    band = lambda top: pl.ds(length - block - top, span)
    gprobs = [mm(pick(gm_ref, top, head), v, NT) for top, head in jobs]
    turned_qp = {top: mm(flip, qp_ref[pl.ds(top, block), :]).astype(BF) for top in tops}
    gsums = []
    for (top, head), gprob in zip(jobs, gprobs):
        probs = probs_ref[head, pl.ds(top, block), :].astype(F32)
        product = probs * gprob
        inner = jnp.sum(product, axis=1, keepdims=True)
        gsums.append((product - probs * inner).astype(BF))
    wides = []
    for gsum in gsums:
        wide = jnp.concatenate([mm(flip, gsum), jnp.zeros((block, block), F32)], axis=1)
        wides.append(pltpu.roll(wide, 0, 1, stride=1, stride_axis=0).astype(BF))
    gk = gv = None
    gqc, gqp = {}, {}
    for (top, head), gsum in zip(jobs, gsums):
        tall = lane_mask(head, (length, pair))
        a = mm(gsum, jnp.where(tall, k, zero))
        gqc[top] = a if head == 0 else gqc[top] + a
        b = mm(gsum, pick(qc_ref, top, head), TN)
        c = mm(probs_ref[head, pl.ds(top, block), :], pick(gm_ref, top, head), TN)
        gk = b if gk is None else gk + b
        gv = c if gv is None else gv + c
    rel_acc[...] = jnp.zeros_like(rel_acc)
    for (top, head), wide in zip(jobs, wides):
        rel = jnp.where(lane_mask(head, (span, pair)), rel_ref[band(top), :], zero)
        d = mm(wide, rel)
        gqp[top] = d if head == 0 else gqp[top] + d
        mask = lane_mask(head, (block, pair))
        rel_acc[band(top), :] += mm(wide, jnp.where(mask, turned_qp[top], zero), TN)
    sum_c = sum_p = None
    for top in tops:
        c, p = gqc[top] * SCALE, gqp[top] * SCALE
        high = p.astype(BF)
        rest = (p - high.astype(F32)).astype(BF)
        straight = mm(flip, high) + mm(flip, rest)
        gqkv_ref[0, pl.ds(top, block), :] = (c + straight).astype(BF)
        e = jnp.sum(c, axis=0, keepdims=True)
        f = jnp.sum(p, axis=0, keepdims=True)
        sum_c = e if sum_c is None else sum_c + e
        sum_p = f if sum_p is None else sum_p + f
    gqkv_ref[1] = gk.astype(BF)
    gqkv_ref[2] = gv.astype(BF)
    grel_ref[...] = rel_acc[...].astype(BF)
    sums_ref[0:1] = sum_c
    sums_ref[1:2] = sum_p


def attend_back(probs, gm, qc, qp, k, v, rel):
    length, width = qc.shape
    pair = 2 * HEAD_FEATURES
    heads = width // HEAD_FEATURES
    column = pl.BlockSpec((length, pair), lambda p: (0, p))
    tall = pl.BlockSpec((rel.shape[0], pair), lambda p: (0, p))
    return pl.pallas_call(
        attend_back_kernel,
        grid=(heads // 2,),
        in_specs=[pl.BlockSpec((2, length, length), lambda p: (p, 0, 0))] + [column] * 5 + [tall],
        out_specs=[
            pl.BlockSpec((3, length, pair), lambda p: (0, 0, p)),
            tall,
            pl.BlockSpec((2, pair), lambda p: (0, p)),
        ],
        out_shape=[
            jax.ShapeDtypeStruct((3, length, width), BF),
            jax.ShapeDtypeStruct(rel.shape, BF),
            jax.ShapeDtypeStruct((2, width), F32),
        ],
        scratch_shapes=[pltpu.VMEM((rel.shape[0], pair), F32)],
        compiler_params=params(VMEM_MB),
        cost_estimate=cost(28),
        name="attend_back",
    )(probs, gm, qc, qp, k, v, rel)


def project_back_kernel(
    core_ref, x_ref, gqkv_ref, grel_hbm, sine_hbm, gattn_hbm, mixed_hbm, *refs,
):
    *gw_refs, turned_ref, grel_ref, sine_ref, gattn_ref, mixed_ref, sem = refs
    step = pl.program_id(0)
    late = (grel_hbm, grel_ref), (sine_hbm, sine_ref), (gattn_hbm, gattn_ref), (mixed_hbm, mixed_ref)
    late = [pltpu.make_async_copy(*pair, sem.at[i]) for i, pair in enumerate(late)]

    def store(value):
        if len(gw_refs) == 2:
            store_split(*gw_refs, core_ref[0], value)
        else:
            store_matrix(gw_refs[0], value)

    @pl.when(step == 0)
    def _():
        for copy in late:
            copy.start()
        turned_ref[...] = x_ref[...].T

    @pl.when(step < 3)
    def _():
        store(mm(turned_ref[...], gqkv_ref[...]))

    @pl.when(step == 3)
    def _():
        for copy in late:
            copy.wait()
        store(mm(sine_ref[...], grel_ref[...], TN))

    @pl.when(step == 4)
    def _():
        store(mm(gattn_ref[...], mixed_ref[...], TN))


def project_back(core, x, gqkv, grel, sine, gattn, mixed, lines, rows):
    length, width = x.shape
    if layered(lines, rows):
        shapes = [(len(SQUARE), lines, 5, rows, width // 2)] * 2
    else:
        shapes = [grad_shape(5, lines, rows, width // 2)]
    return pl.pallas_call(
        project_back_kernel,
        grid=(5,),
        in_specs=[
            pl.BlockSpec(memory_space=pltpu.SMEM),
            held((length, width)),
            pl.BlockSpec((None, length, width), lambda b: (jnp.minimum(b, 2), 0, 0)),
        ]
        + [pl.BlockSpec(memory_space=pl.ANY)] * 4,
        out_specs=[grad_spec(shape) for shape in shapes],
        out_shape=[jax.ShapeDtypeStruct(shape, BF) for shape in shapes],
        scratch_shapes=[pltpu.VMEM((width, length), BF)]
        + [pltpu.VMEM(a.shape, BF) for a in (grel, sine, gattn, mixed)]
        + [pltpu.SemaphoreType.DMA((4,))],
        compiler_params=params(VMEM_MB),
        cost_estimate=cost(9),
        name="project_back",
    )(core, x, gqkv, grel, sine, gattn, mixed)


def token_grad_kernel(gqkv_ref, w_ref, gh1_ref, gtok_ref):
    total = gh1_ref[...]
    for i in range(3):
        total += mm(gqkv_ref[i], full_matrix(w_ref.at[i]), NT)
    gtok_ref[...] = total


def token_grad(gqkv, w, gh1):
    one = whole(gh1.shape)
    return pl.pallas_call(
        token_grad_kernel,
        grid=(1,),
        in_specs=[whole(gqkv.shape), whole((3,) + w.shape[1:]), one],
        out_specs=one,
        out_shape=jax.ShapeDtypeStruct(gh1.shape, F32),
        compiler_params=params(VMEM_MB),
        cost_estimate=cost(6),
        name="token_grad",
    )(gqkv, w, gh1)


def swap_x(value):
    return lax.ppermute(value, "mp", [(0, 1), (1, 0)])


def swap_dp(value, bit):
    return lax.ppermute(value, "dp", [(d, d ^ bit) for d in range(lax.axis_size("dp"))])


def shift_line(value, step):
    dp = lax.axis_size("dp")
    return lax.ppermute(value, "dp", [(d, (d + 4 * step) % dp) for d in range(dp)])


def gather_matrices(shard):
    dp = lax.axis_size("dp")
    if shard.shape[1] % 16 == 0:
        order = [mp * dp + index for mp, index in ring_order(dp // 4)]
        return lax.all_gather(
            shard, ("mp", "dp"), axis=0, axis_index_groups=[order], tiled=False
        )
    pieces = lax.all_gather(shard, ("mp", "dp"), axis=0, tiled=False)
    return whole_matrices(pieces.reshape((2, dp) + shard.shape))


def whole_matrices(pieces):
    mp, dp, blocks, rows, columns = pieces.shape
    return pieces.transpose(2, 0, 1, 3, 4).reshape(blocks, mp, dp * rows, columns)


def gather_lines(shard, others):
    lines = lax.axis_size("dp") // 4
    if lines != 4 or shard.shape[1] % 16 != 0:
        return shard, others
    near = [shard] + [shift_line(shard, step) for step in range(1, lines)]
    near, others = lax.optimization_barrier((near, others))
    return jnp.stack(near), others


def gather_stepwise(near, shard):
    dp = lax.axis_size("dp")
    blocks, rows, columns = shard.shape
    lines = dp // 4
    if lines != 4 or rows % 16 != 0:
        pieces = lax.all_gather(shard, ("mp", "dp"), axis=0, tiled=False)
        return (whole_matrices(pieces.reshape((2, dp) + shard.shape)),)
    cut = blocks // 2
    one, two = near[:, :cut], near[:, cut:]
    one_x = swap_x(one)
    two_y = swap_dp(two, 2)
    one_y = swap_dp(one, 2)
    two_x = swap_x(two)
    one_xy = swap_dp(one_x, 2)
    two_xy = swap_x(two_y)
    lane = [one, two, one_x, two_y, one_y, two_x, one_xy, two_xy]
    return tuple(lane + [swap_dp(part, 1) for part in lane])


def own_place():
    index = lax.axis_index("dp")
    place = jnp.stack([lax.axis_index("mp"), index // 4, (index // 2) % 2, index % 2])
    return place.astype(jnp.int32)


def plane_groups(dp):
    return [
        [mp * dp + line * 4 + y * 2 + core for mp, y, core in RING] for line in range(dp // 4)
    ]


def line_groups(dp):
    return [
        [mp * dp + line * 4 + low for line in range(dp // 4)] for mp in range(2) for low in range(4)
    ]


def scatter_plane(grads):
    dp = lax.axis_size("dp")
    if grads.ndim == 4:
        blocks, _, all_rows, columns = grads.shape
        grads = grads.reshape(blocks, 2, dp // 4, 2, 2, all_rows // dp, columns)
        grads = jnp.stack([grads[:, mp, :, y, core] for mp, y, core in RING])
        grads = grads.transpose(0, 2, 1, 3, 4)
    return lax.psum_scatter(
        grads, ("mp", "dp"), scatter_dimension=0, axis_index_groups=plane_groups(dp), tiled=False
    )


def scatter_square(keep, send, before):
    dp = lax.axis_size("dp")
    grads = (keep.astype(F32) + swap_dp(send, 1).astype(F32)).astype(BF)
    grads, before = lax.optimization_barrier((grads, before))
    groups = [
        [mp * dp + line * 4 + y * 2 + core for mp, y in SQUARE]
        for line in range(dp // 4)
        for core in range(2)
    ]
    part = lax.psum_scatter(
        grads, ("mp", "dp"), scatter_dimension=0, axis_index_groups=groups, tiled=False
    )
    return part, before


def line_pieces(part):
    dp = lax.axis_size("dp")
    lines = dp // 4
    if lines != 4:
        return [part]
    line = lax.axis_index("dp") // 4
    return [
        lax.dynamic_index_in_dim(part, (line + step) % lines, 0, keepdims=False)
        for step in range(lines)
    ]


def trade_pieces(pieces):
    dp = lax.axis_size("dp")
    if len(pieces) == 1:
        return [
            lax.psum_scatter(
                pieces[0], ("mp", "dp"), scatter_dimension=0, axis_index_groups=line_groups(dp),
                tiled=False,
            )
        ]
    return [pieces[0]] + [shift_line(pieces[step], step) for step in range(1, len(pieces))]


def sum_plane(value, meanwhile):
    value = value + swap_dp(value, 1)
    value = value + swap_x(value)
    value, *meanwhile = lax.optimization_barrier((value, *meanwhile))
    return value + swap_dp(value, 2), meanwhile


def sum_line(value):
    lines = lax.axis_size("dp") // 4
    if lines != 4:
        return lax.psum(value, ("dp",), axis_index_groups=line_only(lines))
    total = value
    for piece in [shift_line(value, step) for step in range(1, lines)]:
        total = total + piece
    return total


def line_only(lines):
    return [[line * 4 + low for line in range(lines)] for low in range(4)]


def adam_kernel(order, count, *refs):
    pieces = refs[:count]
    p_ref, one_ref, two_ref = refs[count : count + 3]
    outs = refs[-3:]
    for block, at in enumerate(order):
        grad = pieces[0][block].astype(F32)
        for piece in pieces[1:]:
            grad = grad + piece[block].astype(F32)
        results = adam_update(p_ref[at], grad, one_ref[at], two_ref[at], RATE_BIG)
        for out, result in zip(outs, results):
            out[at] = result


def adam_blocks(pieces, order, param, one, two, done):
    blocks, rows, columns = pieces[0].shape
    shape = jax.ShapeDtypeStruct(param.shape, F32)
    part = whole((blocks, rows, columns) if done else param.shape)
    if done:
        param, one, two = param[:blocks], one[:blocks], two[:blocks]
    count = len(pieces)
    return pl.pallas_call(
        functools.partial(adam_kernel, order, count),
        grid=(1,),
        in_specs=[whole(pieces[0].shape)] * count
        + [part] * 3
        + [pl.BlockSpec(memory_space=pl.ANY)] * len(done),
        out_specs=[part] * 3,
        out_shape=[shape] * 3,
        input_output_aliases={count + 3 + i: i for i in range(len(done))},
        compiler_params=params(ADAM_MB),
        cost_estimate=cost(blocks // 2),
        name="adam",
    )(*pieces, param, one, two, *done)


def per_device(
    tokens,
    lengths,
    weights,
    weight_m1,
    weight_m2,
    head_vecs,
    head_m1,
    head_m2,
    norm_vecs,
    norm_m1,
    norm_m2,
    cotangent,
):
    mp_index = lax.axis_index("mp")
    seq_len = cotangent.shape[0]
    weight_rows = weights.shape[0]
    local_width = weights.shape[2]
    model_width = tokens.shape[1]
    lines = lax.axis_size("dp") // 4
    x = lax.dynamic_slice_in_dim(tokens, mp_index * seq_len, seq_len, 0)
    used = lax.dynamic_slice_in_dim(lengths, mp_index, 1, 0)
    sine = relative_embedding(seq_len, model_width).astype(BF)
    shard = weights.transpose(1, 0, 2)
    shard_low, shard_feed = round_shard(shard)
    heads_all = lax.all_gather(head_vecs, "mp", axis=1, tiled=True)
    w_feed = gather_matrices(shard_feed)
    near, (x, sine, heads_all) = gather_lines(shard_low, (x, sine, heads_all))
    parts = gather_stepwise(near, shard_low)

    qc, qp, k, v, rel, w = project_parts(x, parts, heads_all[0:2], sine, own_place())
    probs, mixed = attend(used, qc, qp, k, v, rel)
    hb = heads_all[2:6].reshape(4, 1, model_width)
    out, unit, inv, gh2, gw_feed, ghid, sums2 = mlp(
        mixed, w_feed, x, norm_vecs, hb, cotangent, lines, weight_rows
    )
    part_feed = scatter_plane(gw_feed)
    gh1, gattn, gmixed, sums1 = norm_down(gh2, ghid, unit, inv, norm_vecs, w_feed)
    gqkv, grel, sums_q = attend_back(probs, gmixed, qc, qp, k, v, rel)
    small = sum_line(jnp.concatenate([sums2, sums1, sums_q], axis=0))
    place = own_place()
    gproj = project_back(
        place[3:4], x, gqkv, grel, sine, gattn, mixed, lines, weight_rows
    )
    *gproj, small = lax.optimization_barrier((*gproj, small))
    if len(gproj) == 2:
        part_proj, part_feed = scatter_square(*gproj, part_feed)
    else:
        gproj, part_feed = lax.optimization_barrier((gproj[0], part_feed))
        part_proj = scatter_plane(gproj)

    pieces_feed = line_pieces(part_feed)
    *pieces_feed, gqkv = lax.optimization_barrier((*pieces_feed, gqkv))
    grad_tokens = token_grad(gqkv, w, gh1)
    pieces_feed = trade_pieces(pieces_feed)
    small, grad_tokens = lax.optimization_barrier((small, grad_tokens))
    small, pieces_feed = sum_plane(small, pieces_feed)
    norm_grad = jnp.concatenate([small[7:9], small[0:2], small[9:10], small[2:3]], axis=0)
    head_grad = jnp.concatenate([small[10:12], small[3:7]], axis=0)
    head_grad = lax.dynamic_slice_in_dim(head_grad, mp_index * local_width, local_width, 1)
    state = (shard, weight_m1.transpose(1, 0, 2), weight_m2.transpose(1, 0, 2))
    done = adam_blocks(pieces_feed, (5, 9, 6, 10, 7, 11, 8, 12), *state, ())
    small, norm_grad, done, part_proj = lax.optimization_barrier((small, norm_grad, done, part_proj))
    pieces_proj = trade_pieces(line_pieces(part_proj))
    new_big = adam_blocks(pieces_proj, tuple(range(5)), *state, done)
    new_weights, new_weight_m1, new_weight_m2 = [a.transpose(1, 0, 2) for a in new_big]
    new_head, new_head_m1, new_head_m2 = adam_update(
        head_vecs, head_grad, head_m1, head_m2, RATE_SMALL
    )
    new_norm, new_norm_m1, new_norm_m2 = adam_update(
        norm_vecs, norm_grad, norm_m1, norm_m2, RATE_SMALL
    )
    return (
        out,
        grad_tokens,
        new_weights,
        new_weight_m1,
        new_weight_m2,
        new_head,
        new_head_m1,
        new_head_m2,
        new_norm,
        new_norm_m1,
        new_norm_m2,
    )


def solution(mesh):
    shard = P("dp", None, "mp")
    return jax.shard_map(
        per_device,
        mesh=mesh,
        in_specs=(P("dp", None), P("dp"), shard, shard, shard)
        + (P(None, "mp"),) * 3
        + (P(),) * 3
        + (P(("dp", "mp"), None),),
        out_specs=(P(("dp", "mp"), None),) * 2
        + (shard,) * 3
        + (P(None, "mp"),) * 3
        + (P(),) * 3,
        check_vma=False,
    )
```

```python
import functools

import jax
import jax.numpy as jnp
from jax import lax
from jax.experimental import pallas as pl
from jax.experimental.pallas import tpu as pltpu
from jax.sharding import PartitionSpec as P

HEAD_FEATURES = 64
STEP = 5
EPS_NORM = 1e-05
EPS_ADAM = 1e-08
BETA_ONE = 0.5
BETA_TWO = 0.5
RATE_BIG = 0.03
RATE_SMALL = 0.2
DECAY = 0.01
MASKED = -1e30
SCALE = HEAD_FEATURES ** (-0.5)
ROW_BLOCK = 256
VMEM_MB = 56
ADAM_MB = 16
UNROLL = 1
BF = jnp.bfloat16
F32 = jnp.float32

NN = (((1,), (0,)), ((), ()))
NT = (((1,), (1,)), ((), ()))
TN = (((0,), (0,)), ((), ()))


def mm(a, b, dims=NN):
    return lax.dot_general(a, b, dims, preferred_element_type=F32)


def whole(shape):
    return pl.BlockSpec(shape, lambda *_: (0,) * len(shape))


def held(shape):
    return pl.BlockSpec(shape, lambda *_: (0,) * len(shape), pipeline_mode=pl.Buffered(1))


def params(mebibytes):
    return pltpu.CompilerParams(vmem_limit_bytes=mebibytes * 1024 * 1024)


def cost(micros):
    return pl.CostEstimate(flops=int(micros * 1e9), bytes_accessed=0, transcendentals=0)


def relative_embedding(length, model_width):
    distance = (length - 1 - jnp.arange(2 * length)).astype(F32)
    freq_index = jnp.arange(model_width // 2).astype(F32)
    inverse = 1.0 / 10000.0 ** (2.0 * freq_index / model_width)
    angles = distance[:, None] * inverse[None, :]
    return jnp.concatenate([jnp.sin(angles), jnp.cos(angles)], axis=1)


def adam_update(param, grad_sum, moment_one, moment_two, rate):
    new_one = BETA_ONE * moment_one + (1.0 - BETA_ONE) * grad_sum
    new_two = BETA_TWO * moment_two + (1.0 - BETA_TWO) * grad_sum * grad_sum
    corrected_one = new_one / (1.0 - BETA_ONE**STEP)
    corrected_two = new_two / (1.0 - BETA_TWO**STEP)
    new_param = param - rate * (
        corrected_one / (jnp.sqrt(corrected_two) + EPS_ADAM) + DECAY * param
    )
    return (new_param, new_one, new_two)


def weight_spec(shape, which, each=None):
    if shape[1] != 2:
        return pl.BlockSpec((shape[0], each) + shape[2:], lambda b: (0, which(b), 0, 0))
    return pl.BlockSpec((each,) + shape[1:], lambda b: (which(b), 0, 0, 0))


def one_block(ref, index):
    if len(ref.shape) == 5:
        return ref.at[:, :, index]
    return ref.at[:, index] if ref.shape[0] > 8 else ref.at[index]


def ring_order(lines):
    order = []
    for turn, (mp, y) in enumerate(((0, 0), (0, 1), (1, 1), (1, 0))):
        for line in range(lines) if turn % 2 == 0 else reversed(range(lines)):
            order += [(mp, line * 4 + y * 2), (mp, line * 4 + y * 2 + 1)]
    return order


def full_matrix(w_ref):
    if len(w_ref.shape) == 3 and w_ref.shape[0] > 2:
        places = w_ref.shape[0]
        order = ring_order(places // 8)
        sides = [
            jnp.concatenate([w_ref[order.index((mp, dp))] for dp in range(places // 2)], axis=0)
            for mp in range(2)
        ]
        return jnp.concatenate(sides, axis=1)
    return jnp.concatenate([w_ref[0], w_ref[1]], axis=1)


RING = ((0, 0, 0), (0, 0, 1), (0, 1, 0), (0, 1, 1), (1, 1, 0), (1, 1, 1), (1, 0, 0), (1, 0, 1))


SQUARE = ((0, 0), (0, 1), (1, 1), (1, 0))


def layered(lines, rows):
    return rows % 16 == 0


def grad_shape(blocks, lines, rows, columns):
    if layered(lines, rows):
        return (len(RING), lines, blocks, rows, columns)
    return (blocks, 2, lines * 4 * rows, columns)


def grad_spec(shape):
    if len(shape) == 5:
        return pl.BlockSpec(shape[:2] + (None,) + shape[3:], lambda b: (0, 0, b, 0, 0))
    return pl.BlockSpec((None,) + shape[1:], lambda b: (b, 0, 0, 0))


def store_matrix(out_ref, value):
    half = value.shape[1] // 2
    low = value.astype(BF)
    if len(out_ref.shape) == 3:
        out_ref[0] = low[:, :half]
        out_ref[1] = low[:, half:]
        return
    places, lines, rows, _ = out_ref.shape
    for place, (mp, y, core) in enumerate(RING):
        for line in range(lines):
            top = (line * 4 + y * 2 + core) * rows
            out_ref[place, line] = low[top : top + rows, mp * half : (mp + 1) * half]


def store_split(keep_ref, send_ref, core, value):
    half = value.shape[1] // 2
    low = value.astype(BF)
    places, lines, rows, _ = keep_ref.shape
    for place, (mp, y) in enumerate(SQUARE):
        for line in range(lines):
            top = (line * 4 + y * 2) * rows
            columns = slice(mp * half, (mp + 1) * half)
            lower, upper = low[top : top + rows, columns], low[top + rows : top + 2 * rows, columns]
            keep_ref[place, line] = jnp.where(core == 0, lower, upper)
            send_ref[place, line] = jnp.where(core == 0, upper, lower)


def round_kernel(shard_ref, low_ref, feed_ref):
    low_ref[...] = shard_ref[0:4].astype(BF)
    feed_ref[0:8] = shard_ref[5:13].astype(BF)
    feed_ref[8] = shard_ref[4].astype(BF)


def round_shard(shard):
    rest = shard.shape[1:]
    return pl.pallas_call(
        round_kernel,
        grid=(1,),
        in_specs=[whole(shard.shape)],
        out_specs=[whole((4,) + rest), whole((9,) + rest)],
        out_shape=[jax.ShapeDtypeStruct((n,) + rest, BF) for n in (4, 9)],
        compiler_params=params(16),
        cost_estimate=cost(1),
        name="round_shard",
    )(shard)


def project_kernel(x_ref, w_ref, vec_ref, sine_ref, qc_ref, qp_ref, k_ref, v_ref, rel_ref):
    step = pl.program_id(0)

    @pl.when(step == 0)
    def _():
        q = mm(x_ref[...], full_matrix(w_ref))
        qc_ref[...] = (q + vec_ref[0:1]).astype(BF) * BF(SCALE)
        qp_ref[...] = (q + vec_ref[1:2]).astype(BF) * BF(SCALE)

    @pl.when(step == 1)
    def _():
        k_ref[...] = mm(x_ref[...], full_matrix(w_ref)).astype(BF)

    @pl.when(step == 2)
    def _():
        v_ref[...] = mm(x_ref[...], full_matrix(w_ref)).astype(BF)

    @pl.when(step == 3)
    def _():
        rel_ref[...] = mm(sine_ref[...], full_matrix(w_ref)).astype(BF)


def project(x, w, vecs, sine):
    length, width = x.shape
    rows = sine.shape[0]
    shapes = [(length, width)] * 4 + [(rows, width)]
    return pl.pallas_call(
        project_kernel,
        grid=(4,),
        in_specs=[
            whole(x.shape),
            weight_spec(w.shape, lambda b: b),
            whole(vecs.shape),
            whole(sine.shape),
        ],
        out_specs=[whole(s) for s in shapes],
        out_shape=[jax.ShapeDtypeStruct(s, BF) for s in shapes],
        compiler_params=params(VMEM_MB),
        cost_estimate=cost(9),
        name="project",
    )(x, w, vecs, sine)


PARTS = [
    (half, dx, dy, dc)
    for dc in (0, 1)
    for half, dx, dy in (
        (0, 0, 0), (1, 0, 0), (0, 1, 0), (1, 0, 1), (0, 0, 1), (1, 1, 0), (0, 1, 1), (1, 1, 1),
    )
]


def project_parts_kernel(
    cut, place_ref, x_ref, vec_ref, sine_ref, *refs,
):
    parts = refs[: len(PARTS)]
    outs = refs[len(PARTS) : len(PARTS) + 6]
    buffers = refs[len(PARTS) + 6 : len(PARTS) + 12]
    in_sem, out_sem = refs[-2:]
    w_ref = buffers[5]
    mp, line, y, core = (place_ref[i] for i in range(4))
    lines, _, rows, _ = parts[0].shape
    arriving = ([], [])
    for index, (half, dx, dy, dc) in enumerate(PARTS):
        for step in range(lines):
            at = lax.rem(line + lines - step, lines) * 4 + (y ^ dy) * 2 + (core ^ dc)
            start = pl.multiple_of(at * rows, rows)
            arriving[half].append(
                pltpu.make_async_copy(
                    parts[index].at[step],
                    w_ref.at[pl.ds(half * cut, cut), mp ^ dx, pl.ds(start, rows)],
                    in_sem.at[index * lines + step],
                )
            )
    for copy in arriving[0] + arriving[1]:
        copy.start()
    leaving = []

    def leave(source, target):
        copy = pltpu.make_async_copy(source, target, out_sem.at[len(leaving)])
        copy.start()
        leaving.append(copy)

    for copy in arriving[0]:
        copy.wait()
    leave(w_ref.at[0:2], outs[5].at[0:2])
    q = mm(x_ref[...], full_matrix(w_ref.at[0]))
    buffers[0][...] = (q + vec_ref[0:1]).astype(BF) * BF(SCALE)
    leave(buffers[0], outs[0])
    buffers[1][...] = (q + vec_ref[1:2]).astype(BF) * BF(SCALE)
    leave(buffers[1], outs[1])
    buffers[2][...] = mm(x_ref[...], full_matrix(w_ref.at[1])).astype(BF)
    leave(buffers[2], outs[2])
    for copy in arriving[1]:
        copy.wait()
    leave(w_ref.at[2:3], outs[5].at[2:3])
    buffers[4][...] = mm(sine_ref[...], full_matrix(w_ref.at[3])).astype(BF)
    leave(buffers[4], outs[4])
    buffers[3][...] = mm(x_ref[...], full_matrix(w_ref.at[2])).astype(BF)
    leave(buffers[3], outs[3])
    for copy in leaving:
        copy.wait()


def project_parts(x, parts, vecs, sine, place):
    if len(parts) == 1:
        return [*project(x, parts[0], vecs, sine), parts[0]]
    length, width = x.shape
    lines, cut, rows, columns = parts[0].shape
    shapes = [(length, width)] * 4 + [sine.shape]
    matrix = (2, lines * 4 * rows, columns)
    anywhere = pl.BlockSpec(memory_space=pl.ANY)
    return pl.pallas_call(
        functools.partial(project_parts_kernel, cut),
        grid=(1,),
        in_specs=[
            pl.BlockSpec(memory_space=pltpu.SMEM), held(x.shape), held(vecs.shape), held(sine.shape),
        ]
        + [anywhere] * len(parts),
        out_specs=[anywhere] * 6,
        out_shape=[jax.ShapeDtypeStruct(shape, BF) for shape in shapes + [(3,) + matrix]],
        scratch_shapes=[pltpu.VMEM(shape, BF) for shape in shapes + [(4,) + matrix]]
        + [pltpu.SemaphoreType.DMA((len(parts) * lines,)), pltpu.SemaphoreType.DMA((7,))],
        compiler_params=params(VMEM_MB),
        cost_estimate=cost(9),
        name="project",
    )(place, x, vecs, sine, *parts)


def lane_mask(which, shape):
    lanes = lax.broadcasted_iota(jnp.int32, shape, 1)
    return (lanes >= HEAD_FEATURES) if which else (lanes < HEAD_FEATURES)


def attend_kernel(len_ref, qc_ref, qp_ref, k_ref, v_ref, rel_ref, probs_ref, mixed_ref):
    length = qc_ref.shape[0]
    block = ROW_BLOCK
    pair = qc_ref.shape[1]
    valid = lax.broadcasted_iota(jnp.int32, (1, length), 1) < len_ref[0]
    k = k_ref[...]
    v = v_ref[...]
    zero = jnp.zeros((), BF)
    span = length + block
    jobs = [(top, head) for top in range(0, length, block) for head in range(2)]
    raw = []
    for top, head in jobs:
        rows = pl.ds(top, block)
        first = length - block - top
        mask = lane_mask(head, (block, pair))
        content = mm(jnp.where(mask, qc_ref[rows, :], zero), k, NT)
        place = mm(jnp.where(mask, qp_ref[rows, :], zero), rel_ref[first : first + span, :], NT)
        raw.append((content, place))
    for (top, head), (content, place) in zip(jobs, raw):
        place = pltpu.roll(place, span - (block - 1), 1, stride=1, stride_axis=0)
        scores = jnp.where(valid, content + place[:, :length], MASKED)
        top_score = jnp.max(scores, axis=1, keepdims=True)
        grown = jnp.exp(scores - top_score)
        probs = grown * (1.0 / jnp.sum(grown, axis=1, keepdims=True))
        probs_ref[head, pl.ds(top, block), :] = probs.astype(BF)
    for top in range(0, length, block):
        rows = pl.ds(top, block)
        lower, upper = mm(probs_ref[0, rows, :], v), mm(probs_ref[1, rows, :], v)
        mixed_ref[rows, :] = jnp.where(lane_mask(1, (block, pair)), upper, lower).astype(BF)


def attend(length_used, qc, qp, k, v, rel):
    length, width = qc.shape
    pair = 2 * HEAD_FEATURES
    heads = width // HEAD_FEATURES
    column = pl.BlockSpec((length, pair), lambda p: (0, p))
    return pl.pallas_call(
        attend_kernel,
        grid=(heads // 2,),
        in_specs=[pl.BlockSpec(memory_space=pltpu.SMEM)]
        + [column] * 4
        + [pl.BlockSpec((rel.shape[0], pair), lambda p: (0, p))],
        out_specs=[pl.BlockSpec((2, length, length), lambda p: (p, 0, 0)), column],
        out_shape=[
            jax.ShapeDtypeStruct((heads, length, length), BF),
            jax.ShapeDtypeStruct((length, width), BF),
        ],
        compiler_params=params(VMEM_MB),
        cost_estimate=cost(19),
        name="attend",
    )(length_used, qc, qp, k, v, rel)


def norm_parts(rows):
    mean = jnp.mean(rows, axis=1, keepdims=True)
    centred = rows - mean
    spread = jnp.mean(centred * centred, axis=1, keepdims=True)
    inverse = lax.rsqrt(spread + EPS_NORM)
    return centred * inverse, inverse


def norm_back(unit, inverse, scaled):
    return (
        scaled
        - jnp.mean(scaled, axis=1, keepdims=True)
        - unit * jnp.mean(scaled * unit, axis=1, keepdims=True)
    ) * inverse


def mlp_kernel(
    blocks, nv_ref, hb_ref, mixed_hbm, x_hbm, cot_hbm, w_hbm,
    out_hbm, unit_hbm, inv_ref, gh2_hbm, gw_hbm, ghid_hbm, sums_ref,
    mixed_ref, x_ref, cot_ref, w_ref, out_ref, unit_ref, gh2_ref, gw_ref,
    low_ref, turned_ref, act_ref, slope_ref, gffn_ref, gturned_ref, ghid_ref, total_ref, hsum_ref,
    in_sem, out_sem,
):
    copy_in = lambda source, target, at: pltpu.make_async_copy(source, target, in_sem.at[at])
    copy_w = lambda at: copy_in(stacked_block(w_hbm, at), w_ref.at[at], at)
    copy_mixed = copy_in(mixed_hbm, mixed_ref, 2 * blocks + 1)
    copy_x = copy_in(x_hbm, x_ref, 2 * blocks + 2)
    copy_cot = copy_in(cot_hbm, cot_ref, 2 * blocks + 3)
    copy_mixed.start()
    copy_w(2 * blocks).start()
    copy_x.start()
    for i in range(blocks):
        copy_w(i).start()
        copy_w(blocks + i).start()
    copy_cot.start()

    copy_out = lambda source, target, at: pltpu.make_async_copy(source, target, out_sem.at[at])
    copy_g = lambda at: copy_out(gw_ref.at[at], one_block(gw_hbm, at), at)
    copy_h = lambda at: copy_out(ghid_ref.at[at], ghid_hbm.at[at], 2 * blocks + at)
    copy_unit = copy_out(unit_ref, unit_hbm, 3 * blocks)
    copy_result = copy_out(out_ref, out_hbm, 3 * blocks + 1)
    copy_gh2 = copy_out(gh2_ref, gh2_hbm, 3 * blocks + 2)

    copy_mixed.wait()
    copy_w(2 * blocks).wait()
    attn = mm(mixed_ref[...], full_matrix(w_ref.at[2 * blocks]), NT)
    copy_x.wait()
    unit, inverse = norm_parts(x_ref[...].astype(F32) + attn + nv_ref[4:5])
    unit_ref[...] = unit
    copy_unit.start()
    inv_ref[...] = jnp.broadcast_to(inverse, inv_ref.shape)
    first = unit * nv_ref[0:1] + nv_ref[1:2]
    low_ref[...] = first.astype(BF)
    total_ref[...] = first + nv_ref[5:6]
    turned_ref[...] = low_ref[...].T

    def forward(i, carry):
        copy_w(i).wait()
        hidden = mm(low_ref[...], full_matrix(w_ref.at[i])) + hb_ref[i]
        bell = 0.5 * (1.0 + lax.erf(hidden * 0.7071067811865476))
        act_ref[i] = (hidden * bell).astype(BF)
        slope_ref[i] = (
            bell + hidden * (jnp.exp(hidden * hidden * -0.5) * 0.3989422804014327)
        ).astype(BF)
        copy_w(blocks + i).wait()
        total_ref[...] += mm(act_ref[i], full_matrix(w_ref.at[blocks + i]), NT)
        return carry

    lax.fori_loop(0, blocks, forward, 0, unroll=UNROLL)
    copy_cot.wait()
    unit, inverse = norm_parts(total_ref[...])
    out_ref[...] = (unit * nv_ref[2:3] + nv_ref[3:4]).astype(BF)
    copy_result.start()
    cot = cot_ref[...].astype(F32)
    gh2 = norm_back(unit, inverse, cot * nv_ref[2:3])
    gh2_ref[...] = gh2
    copy_gh2.start()
    gffn_ref[...] = gh2.astype(BF)
    for i, value in enumerate((cot * unit, cot, gh2)):
        sums_ref[i : i + 1] = jnp.sum(value, axis=0, keepdims=True)
    gturned_ref[...] = gffn_ref[...].T

    def backward(i, carry):
        gact = mm(gffn_ref[...], full_matrix(w_ref.at[blocks + i]))
        store_matrix(gw_ref.at[2 * i + 1], mm(gturned_ref[...], act_ref[i]))
        copy_g(2 * i + 1).start()
        ghid = (gact * slope_ref[i].astype(F32)).astype(BF)
        ghid_ref[i] = ghid
        copy_h(i).start()
        hsum_ref[i] = jnp.sum(ghid.astype(F32), axis=0, keepdims=True)
        store_matrix(gw_ref.at[2 * i], mm(turned_ref[...], ghid_ref[i]))
        copy_g(2 * i).start()
        return carry

    lax.fori_loop(0, blocks, backward, 0, unroll=2)
    for i in range(blocks):
        sums_ref[3 + i : 4 + i] = hsum_ref[i]
    copy_unit.wait()
    copy_result.wait()
    copy_gh2.wait()
    for i in range(blocks):
        copy_h(i).wait()
        copy_g(2 * i).wait()
        copy_g(2 * i + 1).wait()


def stacked_block(ref, at):
    return ref.at[at] if ref.shape[1] == 2 else ref.at[:, at]


def one_matrix(shape):
    return shape[1:] if shape[1] == 2 else shape[:1] + shape[2:]


def mlp(mixed, w_feed, x, nv, hb, cot, lines, rows):
    length, width = x.shape
    blocks = hb.shape[0]
    token = lambda d, *lead: jax.ShapeDtypeStruct((*lead, length, width), d)
    full = grad_shape(2 * blocks, lines, rows, width // 2)
    one_g = full[:2] + full[3:] if len(full) == 5 else full[1:]
    buffer = lambda d, *lead: pltpu.VMEM((*lead, length, width), d)
    anywhere = pl.BlockSpec(memory_space=pl.ANY)
    side = pltpu.VMEM((width, length), BF)
    return pl.pallas_call(
        functools.partial(mlp_kernel, blocks),
        grid=(1,),
        in_specs=[held(nv.shape), held(hb.shape)] + [anywhere] * 4,
        out_specs=[
            anywhere, anywhere, whole((length, 128)), anywhere, anywhere, anywhere,
            whole((3 + blocks, width)),
        ],
        out_shape=[
            token(BF), token(F32), jax.ShapeDtypeStruct((length, 128), F32), token(F32),
            jax.ShapeDtypeStruct(full, BF), token(BF, blocks),
            jax.ShapeDtypeStruct((3 + blocks, width), F32),
        ],
        scratch_shapes=[
            buffer(BF), buffer(BF), buffer(BF),
            pltpu.VMEM((2 * blocks + 1, *one_matrix(w_feed.shape)), BF),
            buffer(BF), buffer(F32), buffer(F32), pltpu.VMEM((2 * blocks, *one_g), BF),
            buffer(BF), side, buffer(BF, blocks), buffer(BF, blocks), buffer(BF), side,
            buffer(BF, blocks), buffer(F32), pltpu.VMEM((blocks, 1, width), F32),
            pltpu.SemaphoreType.DMA((2 * blocks + 4,)), pltpu.SemaphoreType.DMA((3 * blocks + 3,)),
        ],
        compiler_params=params(VMEM_MB),
        cost_estimate=cost(23),
        name="mlp",
    )(nv, hb, mixed, x, cot, w_feed)


def norm_down_kernel(
    blocks, nv_ref, inv_ref, unit_hbm, gh2_hbm, ghid_hbm, w_hbm,
    gh1_ref, gattn_ref, gmixed_ref, sums_ref,
    unit_ref, total_ref, ghid_ref, w_ref, sem,
):
    copy_in = lambda source, target, at: pltpu.make_async_copy(source, target, sem.at[at])
    copy_h = lambda i: copy_in(ghid_hbm.at[i], ghid_ref.at[i], i)
    copy_w = lambda i: copy_in(stacked_block(w_hbm, i), w_ref.at[i], blocks + i)
    copy_gh2 = copy_in(gh2_hbm, total_ref, 2 * blocks)
    copy_unit = copy_in(unit_hbm, unit_ref, 2 * blocks + 1)
    copy_last = copy_in(stacked_block(w_hbm, 2 * blocks), w_ref.at[blocks], 2 * blocks + 2)
    copy_gh2.start()
    for i in range(blocks):
        copy_h(i).start()
        copy_w(i).start()
    copy_unit.start()
    copy_last.start()
    copy_gh2.wait()

    def add(i, carry):
        copy_h(i).wait()
        copy_w(i).wait()
        total_ref[...] += mm(ghid_ref[i], full_matrix(w_ref.at[i]), NT)
        return carry

    lax.fori_loop(0, blocks, add, 0)
    copy_unit.wait()
    gfirst = total_ref[...]
    unit = unit_ref[...]
    gh1 = norm_back(unit, inv_ref[:, 0:1], gfirst * nv_ref[0:1])
    gh1_ref[...] = gh1
    gattn_ref[...] = gh1.astype(BF)
    copy_last.wait()
    gmixed_ref[...] = mm(gattn_ref[...], full_matrix(w_ref.at[blocks])).astype(BF)
    for i, value in enumerate((gfirst * unit, gfirst, gh1)):
        sums_ref[i : i + 1] = jnp.sum(value, axis=0, keepdims=True)


def norm_down(gh2, ghid, unit, inv, nv, w_feed):
    length, width = gh2.shape
    blocks = ghid.shape[0]
    one = whole((length, width))
    token = lambda d: jax.ShapeDtypeStruct((length, width), d)
    buffer = lambda d, *lead: pltpu.VMEM((*lead, length, width), d)
    return pl.pallas_call(
        functools.partial(norm_down_kernel, blocks),
        grid=(1,),
        in_specs=[held(nv.shape), held(inv.shape)] + [pl.BlockSpec(memory_space=pl.ANY)] * 4,
        out_specs=[one, one, one, whole((3, width))],
        out_shape=[token(F32), token(BF), token(BF), jax.ShapeDtypeStruct((3, width), F32)],
        scratch_shapes=[
            buffer(F32), buffer(F32), buffer(BF, blocks),
            pltpu.VMEM((blocks + 1, *one_matrix(w_feed.shape)), BF),
            pltpu.SemaphoreType.DMA((2 * blocks + 3,)),
        ],
        compiler_params=params(VMEM_MB),
        cost_estimate=cost(8),
        name="norm_down",
    )(nv, inv, unit, gh2, ghid, w_feed)


def attend_back_kernel(
    probs_ref, gm_ref, qc_ref, qp_ref, k_ref, v_ref, rel_ref,
    gqkv_ref, grel_ref, sums_ref,
    rel_acc,
):
    length, pair = gm_ref.shape
    block = ROW_BLOCK
    span = length + block
    zero = jnp.zeros((), BF)
    flip = (
        lax.broadcasted_iota(jnp.int32, (block, block), 0)
        + lax.broadcasted_iota(jnp.int32, (block, block), 1)
        == block - 1
    ).astype(F32).astype(BF)
    k = k_ref[...]
    v = v_ref[...]
    tops = range(0, length, block)
    jobs = [(top, head) for top in tops for head in range(2)]
    pick = lambda ref, top, head: jnp.where(
        lane_mask(head, (block, pair)), ref[pl.ds(top, block), :], zero
    )
    band = lambda top: pl.ds(length - block - top, span)
    gprobs = [mm(pick(gm_ref, top, head), v, NT) for top, head in jobs]
    turned_qp = {top: mm(flip, qp_ref[pl.ds(top, block), :]).astype(BF) for top in tops}
    gsums = []
    for (top, head), gprob in zip(jobs, gprobs):
        probs = probs_ref[head, pl.ds(top, block), :].astype(F32)
        product = probs * gprob
        inner = jnp.sum(product, axis=1, keepdims=True)
        gsums.append((product - probs * inner).astype(BF))
    wides = []
    for gsum in gsums:
        wide = jnp.concatenate([mm(flip, gsum), jnp.zeros((block, block), F32)], axis=1)
        wides.append(pltpu.roll(wide, 0, 1, stride=1, stride_axis=0).astype(BF))
    gk = gv = None
    gqc, gqp = {}, {}
    for (top, head), gsum in zip(jobs, gsums):
        tall = lane_mask(head, (length, pair))
        a = mm(gsum, jnp.where(tall, k, zero))
        gqc[top] = a if head == 0 else gqc[top] + a
        b = mm(gsum, pick(qc_ref, top, head), TN)
        c = mm(probs_ref[head, pl.ds(top, block), :], pick(gm_ref, top, head), TN)
        gk = b if gk is None else gk + b
        gv = c if gv is None else gv + c
    rel_acc[...] = jnp.zeros_like(rel_acc)
    for (top, head), wide in zip(jobs, wides):
        rel = jnp.where(lane_mask(head, (span, pair)), rel_ref[band(top), :], zero)
        d = mm(wide, rel)
        gqp[top] = d if head == 0 else gqp[top] + d
        mask = lane_mask(head, (block, pair))
        rel_acc[band(top), :] += mm(wide, jnp.where(mask, turned_qp[top], zero), TN)
    sum_c = sum_p = None
    for top in tops:
        c, p = gqc[top] * SCALE, gqp[top] * SCALE
        high = p.astype(BF)
        rest = (p - high.astype(F32)).astype(BF)
        straight = mm(flip, high) + mm(flip, rest)
        gqkv_ref[0, pl.ds(top, block), :] = (c + straight).astype(BF)
        e = jnp.sum(c, axis=0, keepdims=True)
        f = jnp.sum(p, axis=0, keepdims=True)
        sum_c = e if sum_c is None else sum_c + e
        sum_p = f if sum_p is None else sum_p + f
    gqkv_ref[1] = gk.astype(BF)
    gqkv_ref[2] = gv.astype(BF)
    grel_ref[...] = rel_acc[...].astype(BF)
    sums_ref[0:1] = sum_c
    sums_ref[1:2] = sum_p


def attend_back(probs, gm, qc, qp, k, v, rel):
    length, width = qc.shape
    pair = 2 * HEAD_FEATURES
    heads = width // HEAD_FEATURES
    column = pl.BlockSpec((length, pair), lambda p: (0, p))
    tall = pl.BlockSpec((rel.shape[0], pair), lambda p: (0, p))
    return pl.pallas_call(
        attend_back_kernel,
        grid=(heads // 2,),
        in_specs=[pl.BlockSpec((2, length, length), lambda p: (p, 0, 0))] + [column] * 5 + [tall],
        out_specs=[
            pl.BlockSpec((3, length, pair), lambda p: (0, 0, p)),
            tall,
            pl.BlockSpec((2, pair), lambda p: (0, p)),
        ],
        out_shape=[
            jax.ShapeDtypeStruct((3, length, width), BF),
            jax.ShapeDtypeStruct(rel.shape, BF),
            jax.ShapeDtypeStruct((2, width), F32),
        ],
        scratch_shapes=[pltpu.VMEM((rel.shape[0], pair), F32)],
        compiler_params=params(VMEM_MB),
        cost_estimate=cost(28),
        name="attend_back",
    )(probs, gm, qc, qp, k, v, rel)


def project_back_kernel(
    core_ref, x_ref, gqkv_ref, grel_hbm, sine_hbm, gattn_hbm, mixed_hbm, *refs,
):
    *gw_refs, turned_ref, grel_ref, sine_ref, gattn_ref, mixed_ref, sem = refs
    step = pl.program_id(0)
    late = (grel_hbm, grel_ref), (sine_hbm, sine_ref), (gattn_hbm, gattn_ref), (mixed_hbm, mixed_ref)
    late = [pltpu.make_async_copy(*pair, sem.at[i]) for i, pair in enumerate(late)]

    def store(value):
        if len(gw_refs) == 2:
            store_split(*gw_refs, core_ref[0], value)
        else:
            store_matrix(gw_refs[0], value)

    @pl.when(step == 0)
    def _():
        for copy in late:
            copy.start()
        turned_ref[...] = x_ref[...].T

    @pl.when(step < 3)
    def _():
        store(mm(turned_ref[...], gqkv_ref[...]))

    @pl.when(step == 3)
    def _():
        for copy in late:
            copy.wait()
        store(mm(sine_ref[...], grel_ref[...], TN))

    @pl.when(step == 4)
    def _():
        store(mm(gattn_ref[...], mixed_ref[...], TN))


def project_back(core, x, gqkv, grel, sine, gattn, mixed, lines, rows):
    length, width = x.shape
    if layered(lines, rows):
        shapes = [(len(SQUARE), lines, 5, rows, width // 2)] * 2
    else:
        shapes = [grad_shape(5, lines, rows, width // 2)]
    return pl.pallas_call(
        project_back_kernel,
        grid=(5,),
        in_specs=[
            pl.BlockSpec(memory_space=pltpu.SMEM),
            held((length, width)),
            pl.BlockSpec((None, length, width), lambda b: (jnp.minimum(b, 2), 0, 0)),
        ]
        + [pl.BlockSpec(memory_space=pl.ANY)] * 4,
        out_specs=[grad_spec(shape) for shape in shapes],
        out_shape=[jax.ShapeDtypeStruct(shape, BF) for shape in shapes],
        scratch_shapes=[pltpu.VMEM((width, length), BF)]
        + [pltpu.VMEM(a.shape, BF) for a in (grel, sine, gattn, mixed)]
        + [pltpu.SemaphoreType.DMA((4,))],
        compiler_params=params(VMEM_MB),
        cost_estimate=cost(9),
        name="project_back",
    )(core, x, gqkv, grel, sine, gattn, mixed)


def token_grad_kernel(gqkv_ref, w_ref, gh1_ref, gtok_ref):
    total = gh1_ref[...]
    for i in range(3):
        total += mm(gqkv_ref[i], full_matrix(w_ref.at[i]), NT)
    gtok_ref[...] = total


def token_grad(gqkv, w, gh1):
    one = whole(gh1.shape)
    return pl.pallas_call(
        token_grad_kernel,
        grid=(1,),
        in_specs=[whole(gqkv.shape), whole((3,) + w.shape[1:]), one],
        out_specs=one,
        out_shape=jax.ShapeDtypeStruct(gh1.shape, F32),
        compiler_params=params(VMEM_MB),
        cost_estimate=cost(6),
        name="token_grad",
    )(gqkv, w, gh1)


def swap_x(value):
    return lax.ppermute(value, "mp", [(0, 1), (1, 0)])


def swap_dp(value, bit):
    return lax.ppermute(value, "dp", [(d, d ^ bit) for d in range(lax.axis_size("dp"))])


def shift_line(value, step):
    dp = lax.axis_size("dp")
    return lax.ppermute(value, "dp", [(d, (d + 4 * step) % dp) for d in range(dp)])


def gather_matrices(shard):
    dp = lax.axis_size("dp")
    if shard.shape[1] % 16 == 0:
        order = [mp * dp + index for mp, index in ring_order(dp // 4)]
        return lax.all_gather(
            shard, ("mp", "dp"), axis=0, axis_index_groups=[order], tiled=False
        )
    pieces = lax.all_gather(shard, ("mp", "dp"), axis=0, tiled=False)
    return whole_matrices(pieces.reshape((2, dp) + shard.shape))


def whole_matrices(pieces):
    mp, dp, blocks, rows, columns = pieces.shape
    return pieces.transpose(2, 0, 1, 3, 4).reshape(blocks, mp, dp * rows, columns)


def gather_lines(shard, others):
    lines = lax.axis_size("dp") // 4
    if lines != 4 or shard.shape[1] % 16 != 0:
        return shard, others
    near = [shard] + [shift_line(shard, step) for step in range(1, lines)]
    near, others = lax.optimization_barrier((near, others))
    return jnp.stack(near), others


def gather_stepwise(near, shard):
    dp = lax.axis_size("dp")
    blocks, rows, columns = shard.shape
    lines = dp // 4
    if lines != 4 or rows % 16 != 0:
        pieces = lax.all_gather(shard, ("mp", "dp"), axis=0, tiled=False)
        return (whole_matrices(pieces.reshape((2, dp) + shard.shape)),)
    cut = blocks // 2
    one, two = near[:, :cut], near[:, cut:]
    one_x = swap_x(one)
    two_y = swap_dp(two, 2)
    one_y = swap_dp(one, 2)
    two_x = swap_x(two)
    one_xy = swap_dp(one_x, 2)
    two_xy = swap_x(two_y)
    lane = [one, two, one_x, two_y, one_y, two_x, one_xy, two_xy]
    return tuple(lane + [swap_dp(part, 1) for part in lane])


def own_place():
    index = lax.axis_index("dp")
    place = jnp.stack([lax.axis_index("mp"), index // 4, (index // 2) % 2, index % 2])
    return place.astype(jnp.int32)


def plane_groups(dp):
    return [
        [mp * dp + line * 4 + y * 2 + core for mp, y, core in RING] for line in range(dp // 4)
    ]


def line_groups(dp):
    return [
        [mp * dp + line * 4 + low for line in range(dp // 4)] for mp in range(2) for low in range(4)
    ]


def scatter_plane(grads):
    dp = lax.axis_size("dp")
    if grads.ndim == 4:
        blocks, _, all_rows, columns = grads.shape
        grads = grads.reshape(blocks, 2, dp // 4, 2, 2, all_rows // dp, columns)
        grads = jnp.stack([grads[:, mp, :, y, core] for mp, y, core in RING])
        grads = grads.transpose(0, 2, 1, 3, 4)
    return lax.psum_scatter(
        grads, ("mp", "dp"), scatter_dimension=0, axis_index_groups=plane_groups(dp), tiled=False
    )


def scatter_square(keep, send, before):
    dp = lax.axis_size("dp")
    grads = (keep.astype(F32) + swap_dp(send, 1).astype(F32)).astype(BF)
    grads, before = lax.optimization_barrier((grads, before))
    groups = [
        [mp * dp + line * 4 + y * 2 + core for mp, y in SQUARE]
        for line in range(dp // 4)
        for core in range(2)
    ]
    part = lax.psum_scatter(
        grads, ("mp", "dp"), scatter_dimension=0, axis_index_groups=groups, tiled=False
    )
    return part, before


def line_pieces(part):
    dp = lax.axis_size("dp")
    lines = dp // 4
    if lines != 4:
        return [part]
    line = lax.axis_index("dp") // 4
    return [
        lax.dynamic_index_in_dim(part, (line + step) % lines, 0, keepdims=False)
        for step in range(lines)
    ]


def trade_pieces(pieces):
    dp = lax.axis_size("dp")
    if len(pieces) == 1:
        return [
            lax.psum_scatter(
                pieces[0], ("mp", "dp"), scatter_dimension=0, axis_index_groups=line_groups(dp),
                tiled=False,
            )
        ]
    return [pieces[0]] + [shift_line(pieces[step], step) for step in range(1, len(pieces))]


def sum_plane(value, meanwhile):
    value = value + swap_dp(value, 1)
    value = value + swap_x(value)
    value, *meanwhile = lax.optimization_barrier((value, *meanwhile))
    return value + swap_dp(value, 2), meanwhile


def sum_line(value):
    lines = lax.axis_size("dp") // 4
    if lines != 4:
        return lax.psum(value, ("dp",), axis_index_groups=line_only(lines))
    total = value
    for piece in [shift_line(value, step) for step in range(1, lines)]:
        total = total + piece
    return total


def line_only(lines):
    return [[line * 4 + low for line in range(lines)] for low in range(4)]


def adam_kernel(order, count, *refs):
    pieces = refs[:count]
    p_ref, one_ref, two_ref = refs[count : count + 3]
    outs = refs[-3:]
    for block, at in enumerate(order):
        grad = pieces[0][block].astype(F32)
        for piece in pieces[1:]:
            grad = grad + piece[block].astype(F32)
        results = adam_update(p_ref[at], grad, one_ref[at], two_ref[at], RATE_BIG)
        for out, result in zip(outs, results):
            out[at] = result


def adam_blocks(pieces, order, param, one, two, done):
    blocks, rows, columns = pieces[0].shape
    shape = jax.ShapeDtypeStruct(param.shape, F32)
    part = whole((blocks, rows, columns) if done else param.shape)
    if done:
        param, one, two = param[:blocks], one[:blocks], two[:blocks]
    count = len(pieces)
    return pl.pallas_call(
        functools.partial(adam_kernel, order, count),
        grid=(1,),
        in_specs=[whole(pieces[0].shape)] * count
        + [part] * 3
        + [pl.BlockSpec(memory_space=pl.ANY)] * len(done),
        out_specs=[part] * 3,
        out_shape=[shape] * 3,
        input_output_aliases={count + 3 + i: i for i in range(len(done))},
        compiler_params=params(ADAM_MB),
        cost_estimate=cost(blocks // 2),
        name="adam",
    )(*pieces, param, one, two, *done)


def per_device(
    tokens,
    lengths,
    weights,
    weight_m1,
    weight_m2,
    head_vecs,
    head_m1,
    head_m2,
    norm_vecs,
    norm_m1,
    norm_m2,
    cotangent,
):
    mp_index = lax.axis_index("mp")
    seq_len = cotangent.shape[0]
    weight_rows = weights.shape[0]
    local_width = weights.shape[2]
    model_width = tokens.shape[1]
    lines = lax.axis_size("dp") // 4
    x = lax.dynamic_slice_in_dim(tokens, mp_index * seq_len, seq_len, 0)
    used = lax.dynamic_slice_in_dim(lengths, mp_index, 1, 0)
    sine = relative_embedding(seq_len, model_width).astype(BF)
    shard = weights.transpose(1, 0, 2)
    shard_low, shard_feed = round_shard(shard)
    heads_all = lax.all_gather(head_vecs, "mp", axis=1, tiled=True)
    w_feed = gather_matrices(shard_feed)
    near, (x, sine, heads_all) = gather_lines(shard_low, (x, sine, heads_all))
    parts = gather_stepwise(near, shard_low)

    qc, qp, k, v, rel, w = project_parts(x, parts, heads_all[0:2], sine, own_place())
    probs, mixed = attend(used, qc, qp, k, v, rel)
    hb = heads_all[2:6].reshape(4, 1, model_width)
    out, unit, inv, gh2, gw_feed, ghid, sums2 = mlp(
        mixed, w_feed, x, norm_vecs, hb, cotangent, lines, weight_rows
    )
    part_feed = scatter_plane(gw_feed)
    gh1, gattn, gmixed, sums1 = norm_down(gh2, ghid, unit, inv, norm_vecs, w_feed)
    gqkv, grel, sums_q = attend_back(probs, gmixed, qc, qp, k, v, rel)
    small = sum_line(jnp.concatenate([sums2, sums1, sums_q], axis=0))
    place = own_place()
    gproj = project_back(
        place[3:4], x, gqkv, grel, sine, gattn, mixed, lines, weight_rows
    )
    *gproj, small = lax.optimization_barrier((*gproj, small))
    if len(gproj) == 2:
        part_proj, part_feed = scatter_square(*gproj, part_feed)
    else:
        gproj, part_feed = lax.optimization_barrier((gproj[0], part_feed))
        part_proj = scatter_plane(gproj)

    pieces_feed = line_pieces(part_feed)
    *pieces_feed, gqkv = lax.optimization_barrier((*pieces_feed, gqkv))
    grad_tokens = token_grad(gqkv, w, gh1)
    pieces_feed = trade_pieces(pieces_feed)
    small, grad_tokens = lax.optimization_barrier((small, grad_tokens))
    small, pieces_feed = sum_plane(small, pieces_feed)
    norm_grad = jnp.concatenate([small[7:9], small[0:2], small[9:10], small[2:3]], axis=0)
    head_grad = jnp.concatenate([small[10:12], small[3:7]], axis=0)
    head_grad = lax.dynamic_slice_in_dim(head_grad, mp_index * local_width, local_width, 1)
    state = (shard, weight_m1.transpose(1, 0, 2), weight_m2.transpose(1, 0, 2))
    done = adam_blocks(pieces_feed, (5, 9, 6, 10, 7, 11, 8, 12), *state, ())
    small, norm_grad, done, part_proj = lax.optimization_barrier((small, norm_grad, done, part_proj))
    pieces_proj = trade_pieces(line_pieces(part_proj))
    new_big = adam_blocks(pieces_proj, tuple(range(5)), *state, done)
    new_weights, new_weight_m1, new_weight_m2 = [a.transpose(1, 0, 2) for a in new_big]
    new_head, new_head_m1, new_head_m2 = adam_update(
        head_vecs, head_grad, head_m1, head_m2, RATE_SMALL
    )
    new_norm, new_norm_m1, new_norm_m2 = adam_update(
        norm_vecs, norm_grad, norm_m1, norm_m2, RATE_SMALL
    )
    return (
        out,
        grad_tokens,
        new_weights,
        new_weight_m1,
        new_weight_m2,
        new_head,
        new_head_m1,
        new_head_m2,
        new_norm,
        new_norm_m1,
        new_norm_m2,
    )


def solution(mesh):
    shard = P("dp", None, "mp")
    return jax.shard_map(
        per_device,
        mesh=mesh,
        in_specs=(P("dp", None), P("dp"), shard, shard, shard)
        + (P(None, "mp"),) * 3
        + (P(),) * 3
        + (P(("dp", "mp"), None),),
        out_specs=(P(("dp", "mp"), None),) * 2
        + (shard,) * 3
        + (P(None, "mp"),) * 3
        + (P(),) * 3,
        check_vma=False,
    )
```
